256 devices in a mesh: bucket: 64 (over x, z, y_lo), replica: 4 (over y_hi, core).
Axes of the slice: x: 4, y: 4 (y_hi: 2, y_lo: 2; y = y_hi * 2 + y_lo), z: 8, core: 2. Of those that a mesh axis runs over, the one named last changes fastest.
Arguments:
- left_embed: float32 [4, 32768, 400], P('replica', 'bucket'), may hold values from -2.4 to 2.4
- right_embed: float32 [4, 32768, 400], P('replica', 'bucket'), may hold values from -2.4 to 2.4
- right_state: float32 [4, 32768], P('replica', 'bucket'), may hold values from 0.001 to 0.01
- relation_embed: float32 [2066, 400], replicated, may hold values from -3 to 3
- relation_state: float32 [2066], replicated, may hold values from 0.001 to 0.01
- source_rows: int32 [4, 64, 2, 1000], P('replica', 'bucket'), may hold values from 0 to 511
- target_rows: int32 [4, 64, 2, 1000], P('replica', 'bucket'), may hold values from 0 to 511
- relation_ids: int32 [4, 64, 2, 1000], P('replica', 'bucket'), may hold values from 0 to 2065
- negative_rows: int32 [4, 64, 2, 500], P('replica', 'bucket'), may hold values from 0 to 511
Outputs:
- right_out: float32 [4, 32768, 400], P('replica', 'bucket')
- state_out: float32 [4, 32768], P('replica', 'bucket')
- relation_out: float32 [2066, 400], replicated
- relation_state_out: float32 [2066], replicated
The draws below stay inside these ranges and needn't reach their ends.
All inputs are finite; a program needn't handle non-finite values.
Results may differ from the reference program's by a relative error of at most 0.00045.
The reference program's roundings to bfloat16 on the way (of `prod` and `d_rel`) count: a program that leaves them out, or rounds other values in their place, can miss the bound.
Values may be sent and summed in bfloat16 or wider, within the bound.
No kernel may reach another device: no remote copies, remote signals or barrier semaphores. Data moves between devices by JAX's collectives and lax.ppermute only.
A program may use at most 64 MiB of HBM per device.

```python
import math
import jax
import jax.numpy as jnp
import numpy as np
from jax import lax

D = 400
NREL = 2066
EDGES = 1000
NEG = 500
ROWS = 512
STEPS = 2
ENTITIES = 32768
N_BUCKET = 64
N_REPLICA = 4


def plant(array, rng, smallest, high):
    shape = array.shape
    place = [jax.random.randint(jax.random.fold_in(rng, axis), (), 0, shape[axis]) for axis in range(len(shape))]
    array = array.at[tuple(place)].set(smallest)
    longest = shape.index(max(shape))
    place[longest] = (place[longest] + 1) % shape[longest]
    return array.at[tuple(place)].set(high)


def block_levels(own_key, shape, shards, least, largest):
    def one(dim, shards_of):
        steps = jax.random.uniform(jax.random.fold_in(jax.random.fold_in(own_key, 6), dim), (shards_of,), jnp.float32, least / len(shards), largest / len(shards))
        return jnp.repeat(jnp.exp(steps), shape[dim] // shards_of).reshape((-1,) + (1,) * (len(shape) - dim - 1))

    level = one(*shards[0])
    for cut in shards[1:]:
        level = level * one(*cut)
    return level


def rank_bounds(number_of, slope):
    portions = [(1 << 20) // math.isqrt(grade ** slope) + 1 for grade in range(1, number_of + 1)]
    scale = 1 + sum(portions) // (1 << 30)
    return np.cumsum(np.array([max(1, weight // scale) for weight in portions]))


def skewed_ids(own_key, shape, amount, skew):
    grid = rank_bounds(amount, skew)
    pick = jax.random.randint(jax.random.fold_in(own_key, 1), shape, 0, int(grid[amount - 1]))
    standing = jnp.searchsorted(jnp.asarray(grid, jnp.int32), pick, side="right")
    return jax.random.permutation(jax.random.fold_in(own_key, 2), amount)[standing].astype(jnp.int32)


def normal_values(rng, extent, deviation, bound, pieces=(), kind=jnp.bfloat16):
    array = jax.random.normal(rng, extent, jnp.float32) * deviation
    if len(pieces) > 0:
        array = block_levels(rng, extent, pieces, -0.22, 0.18) * array
    return jnp.clip(array, min=-bound, max=bound).astype(kind)


def setup_inputs(seed: int = 0) -> dict:
    splits = jax.random.split(jax.random.key(seed), 10)
    return {
        "left_embed": normal_values(splits[0], (N_REPLICA, ENTITIES, D), 0.4, 2.4, ((0, 4), (1, 64)), jnp.float32),
        "right_embed": normal_values(splits[1], (N_REPLICA, ENTITIES, D), 0.4, 2.4, ((0, 4), (1, 64)), jnp.float32),
        "right_state": jnp.clip(jnp.exp(math.log(0.01) - 2.30258502 * jax.random.uniform(splits[2], (N_REPLICA, ENTITIES), jnp.float32) ** block_levels(splits[2], (N_REPLICA, ENTITIES), ((0, 4), (1, 64)), -0.2, 0.2)), 0.001, 0.01),
        "relation_embed": normal_values(splits[3], (NREL, D), 0.5, 3.0, (), jnp.float32),
        "relation_state": jnp.clip(jnp.exp(jax.random.uniform(splits[4], (NREL,), jnp.float32, math.log(0.001), math.log(0.01))), 0.001, 0.01),
        "source_rows": plant(jax.random.randint(splits[5], (N_REPLICA, N_BUCKET, STEPS, EDGES), 0, ROWS), jax.random.fold_in(splits[5], 1), 0, ROWS - 1).astype(jnp.int32),
        "target_rows": plant(jax.random.randint(splits[6], (N_REPLICA, N_BUCKET, STEPS, EDGES), 0, ROWS), jax.random.fold_in(splits[6], 1), 0, ROWS - 1).astype(jnp.int32),
        "relation_ids": plant(skewed_ids(splits[7], (N_REPLICA, N_BUCKET, STEPS, EDGES), NREL, 2), jax.random.fold_in(splits[7], 3), 0, NREL - 1).astype(jnp.int32),
        "negative_rows": plant(jax.random.randint(splits[8], (N_REPLICA, N_BUCKET, STEPS, NEG), 0, ROWS), jax.random.fold_in(splits[8], 1), 0, ROWS - 1).astype(jnp.int32),
    }


def edge_terms(left, slab, rel_table, src, dst, rel, neg):
    half = left.shape[1] // 2
    heads = left[src].astype(jnp.bfloat16).astype(jnp.float32)
    pos_rows = slab[dst].astype(jnp.bfloat16).astype(jnp.float32)
    neg_rows = slab[neg].astype(jnp.bfloat16).astype(jnp.float32)
    rel_rows = rel_table[rel].astype(jnp.bfloat16).astype(jnp.float32)
    real_part = heads[:, :half] * rel_rows[:, :half] - heads[:, half:] * rel_rows[:, half:]
    imag_part = heads[:, :half] * rel_rows[:, half:] + heads[:, half:] * rel_rows[:, :half]
    prod = jnp.concatenate([real_part, imag_part], 1).astype(jnp.bfloat16).astype(jnp.float32)
    pos = lax.optimization_barrier(jnp.sum(prod * pos_rows, 1))
    neg_scores = jnp.einsum('ed,nd->en', prod, neg_rows)
    g_pos = -jax.nn.sigmoid(-pos)
    g_neg = (jax.nn.sigmoid(neg_scores) / NEG).astype(jnp.bfloat16).astype(jnp.float32)
    d_pos = (g_pos[:, None] * prod).astype(jnp.bfloat16).astype(jnp.float32)
    d_neg = jnp.einsum('en,ed->nd', g_neg, prod).astype(jnp.bfloat16).astype(jnp.float32)
    d_prod = g_pos[:, None] * pos_rows + jnp.einsum('en,nd->ed', g_neg, neg_rows)
    d_real = d_prod[:, :half] * heads[:, :half] + d_prod[:, half:] * heads[:, half:]
    d_imag = d_prod[:, half:] * heads[:, :half] - d_prod[:, :half] * heads[:, half:]
    d_rel = jnp.concatenate([d_real, d_imag], 1).astype(jnp.bfloat16).astype(jnp.float32)
    grad = jnp.zeros(slab.shape, jnp.float32).at[dst].add(d_pos).at[neg].add(d_neg)
    rel_grad = jnp.zeros(rel_table.shape, jnp.float32).at[rel].add(d_rel)
    return (grad, rel_grad)

def adagrad(table, state, grad, rate):
    new_state = state + lax.optimization_barrier(jnp.mean(grad * grad, axis=-1))
    return (table - rate * grad / jnp.sqrt(new_state)[..., None], new_state)

def reference(left_embed, right_embed, right_state, relation_embed, relation_state, source_rows, target_rows, relation_ids, negative_rows):
    train = jax.vmap(edge_terms, in_axes=(0, 0, None, 0, 0, 0, 0))
    update = jax.vmap(adagrad, in_axes=(0, 0, 0, None))
    rel_total = jnp.zeros(relation_embed.shape, jnp.float32)
    slabs_out = []
    states_out = []
    for group in range(N_REPLICA):
        left = left_embed[group].reshape(N_BUCKET, ROWS, D)
        slab = right_embed[group].reshape(N_BUCKET, ROWS, D)
        state = right_state[group].reshape(N_BUCKET, ROWS)
        grad, rel_grad = train(left, slab, relation_embed, source_rows[group, :, 0], target_rows[group, :, 0], relation_ids[group, :, 0], negative_rows[group, :, 0])
        slab, state = update(slab, state, grad, 0.1)
        rel_total = rel_total + lax.optimization_barrier(jnp.sum(rel_grad, axis=0))
        rolled = jnp.roll(slab, 1, axis=0)
        rolled_state = jnp.roll(state, 1, axis=0)
        grad, rel_grad = train(left, rolled, relation_embed, source_rows[group, :, 1], target_rows[group, :, 1], relation_ids[group, :, 1], negative_rows[group, :, 1])
        rolled, rolled_state = update(rolled, rolled_state, grad, 0.1)
        rel_total = rel_total + lax.optimization_barrier(jnp.sum(rel_grad, axis=0))
        slabs_out.append(jnp.roll(rolled, -1, axis=0).reshape(ENTITIES, D))
        states_out.append(jnp.roll(rolled_state, -1, axis=0).reshape(ENTITIES))
    relation_out, relation_state_out = adagrad(relation_embed, relation_state, rel_total, 0.2)
    return (jnp.stack(slabs_out), jnp.stack(states_out), relation_out, relation_state_out)
```

```python
import jax
import jax.numpy as jnp
from jax import lax
from jax.sharding import PartitionSpec as P


BUCKET = ("x", "z", "y_lo")
REPLICA = ("y_hi", "core")
PLANE = ("x", "y_lo", "y_hi")
HALF = 200
WIDE = 256
PART = 144
LEVELS = 32000.0


def from_next(block):
    count = lax.axis_size(BUCKET)
    return lax.ppermute(block, BUCKET, [((i + 1) % count, i) for i in range(count)])


def swap_core(block):
    return lax.ppermute(block, "core", [(0, 1), (1, 0)])


def encode(block):
    lane = lax.broadcasted_iota(jnp.int32, block.shape, block.ndim - 1)
    top = jnp.max(jnp.abs(block), axis=-1, keepdims=True)
    power = jnp.ceil(jnp.log2(jnp.maximum(top, 1e-30)))
    code = jnp.round(block * (LEVELS * jnp.exp2(-power)))
    return jnp.where(lane < HALF, code, power).astype(jnp.int16)


def decode(code):
    lane = lax.broadcasted_iota(jnp.int32, code.shape, code.ndim - 1)
    wide = code.astype(jnp.float32)
    step = jnp.exp2(wide[..., HALF : HALF + 1]) * (1.0 / LEVELS)
    return jnp.where(lane < HALF, wide * step, 0.0)


def to_all(block, axes):
    count = lax.axis_size(axes)
    copies = jnp.broadcast_to(block[None], (count, *block.shape))
    return lax.all_to_all(copies, axes, 0, 0, tiled=True)


def summed_over_devices(mine, other):
    total = mine + swap_core(other)
    parts = encode(total).reshape(16, PART, WIDE)
    total = jnp.sum(decode(lax.all_to_all(parts, PLANE, 0, 0, tiled=True)), 0)
    total = jnp.sum(decode(to_all(encode(total), "z")), 0)
    ours = to_all(encode(total), PLANE).reshape(16 * PART, WIDE)
    theirs = swap_core(ours)
    first = lax.axis_index("core") == 0
    real, imag = jnp.where(first, ours, theirs), jnp.where(first, theirs, ours)
    return jnp.concatenate([decode(real)[:, :HALF], decode(imag)[:, :HALF]], 1)


def one_hot(index, count):
    return (index[:, None] == jnp.arange(count, dtype=jnp.int32)[None, :]).astype(jnp.bfloat16)


def pick_rows(index, table_low):
    return jnp.dot(
        one_hot(index, table_low.shape[0]), table_low, preferred_element_type=jnp.float32
    ).astype(jnp.bfloat16)


def edge_terms(heads, slab, rel_low, dst, rel, neg):
    rows = slab.shape[0]
    half = slab.shape[1] // 2
    negatives = neg.shape[0]
    slab_low = slab.astype(jnp.bfloat16)
    pos_rows = pick_rows(dst, slab_low)
    neg_rows = pick_rows(neg, slab_low)
    rel_rows = pick_rows(rel, rel_low).astype(jnp.float32)
    head_vals = heads.astype(jnp.float32)
    real_part = head_vals[:, :half] * rel_rows[:, :half] - head_vals[:, half:] * rel_rows[:, half:]
    imag_part = head_vals[:, :half] * rel_rows[:, half:] + head_vals[:, half:] * rel_rows[:, :half]
    prod = jnp.concatenate([real_part, imag_part], 1).astype(jnp.bfloat16)
    pos = jnp.sum(prod.astype(jnp.float32) * pos_rows.astype(jnp.float32), 1)
    neg_scores = jnp.einsum("ed,nd->en", prod, neg_rows, preferred_element_type=jnp.float32)
    g_pos = -jax.nn.sigmoid(-pos)
    g_neg = (jax.nn.sigmoid(neg_scores) / negatives).astype(jnp.bfloat16)
    d_pos = (g_pos[:, None] * prod.astype(jnp.float32)).astype(jnp.bfloat16)
    d_neg = jnp.einsum("en,ed->nd", g_neg, prod, preferred_element_type=jnp.float32).astype(
        jnp.bfloat16
    )
    d_prod = g_pos[:, None] * pos_rows.astype(jnp.float32) + jnp.dot(
        g_neg, neg_rows, preferred_element_type=jnp.float32
    )
    d_real = d_prod[:, :half] * head_vals[:, :half] + d_prod[:, half:] * head_vals[:, half:]
    d_imag = d_prod[:, half:] * head_vals[:, :half] - d_prod[:, :half] * head_vals[:, half:]
    d_rel = jnp.concatenate([d_real, d_imag], 1).astype(jnp.bfloat16)
    grad = jnp.einsum("er,ed->rd", one_hot(dst, rows), d_pos, preferred_element_type=jnp.float32)
    grad = grad + jnp.einsum(
        "nr,nd->rd", one_hot(neg, rows), d_neg, preferred_element_type=jnp.float32
    )
    rel_grad = jnp.einsum(
        "ek,ed->kd", one_hot(rel, rel_low.shape[0]), d_rel, preferred_element_type=jnp.float32
    )
    return (grad, rel_grad)


def adagrad(table, state, grad, rate):
    new_state = state + jnp.mean(grad * grad, axis=-1)
    return (table - rate * grad / jnp.sqrt(new_state)[..., None], new_state)


def padded(half):
    return jnp.pad(half, ((0, 16 * PART - half.shape[0]), (0, WIDE - HALF)))


def per_device(
    left_embed,
    right_embed,
    right_state,
    relation_embed,
    relation_state,
    source_rows,
    target_rows,
    relation_ids,
    negative_rows,
):
    left_low = left_embed[0].astype(jnp.bfloat16)
    blocks = jnp.concatenate(
        [source_rows[0, 0], target_rows[0, 0], relation_ids[0, 0], negative_rows[0, 0]], 1
    )
    left_next = from_next(left_low)
    block_next = from_next(blocks[1])
    slab = right_embed[0]
    state = right_state[0]
    rel_low = relation_embed.astype(jnp.bfloat16)
    edges = source_rows.shape[-1]

    def train(left, slab, state, block):
        src, dst, rel = (block[i * edges : (i + 1) * edges] for i in range(3))
        heads = pick_rows(src, left)
        grad, rel_grad = edge_terms(heads, slab, rel_low, dst, rel, block[3 * edges :])
        slab, state = adagrad(slab, state, grad, 0.1)
        return slab, state, rel_grad

    slab, state, rel_first = train(left_low, slab, state, blocks[0])
    slab, state, rel_second = train(left_next, slab, state, block_next)
    rel_sum = rel_first + rel_second
    real, imag = padded(rel_sum[:, :HALF]), padded(rel_sum[:, HALF:])
    first = lax.axis_index("core") == 0
    mine, other = jnp.where(first, real, imag), jnp.where(first, imag, real)
    rel_total = summed_over_devices(mine, other)[: relation_embed.shape[0]]
    relation_out, relation_state_out = adagrad(relation_embed, relation_state, rel_total, 0.2)
    return (slab[None], state[None], relation_out, relation_state_out)


def solution(mesh):
    split = jax.sharding.Mesh(
        mesh.devices.reshape(4, 8, 2, 2, 2), ("x", "z", "y_lo", "y_hi", "core")
    )
    in_specs = (
        P(REPLICA, BUCKET, None),
        P(REPLICA, BUCKET, None),
        P(REPLICA, BUCKET),
        P(),
        P(),
        P(REPLICA, BUCKET, None, None),
        P(REPLICA, BUCKET, None, None),
        P(REPLICA, BUCKET, None, None),
        P(REPLICA, BUCKET, None, None),
    )
    out_specs = (P(REPLICA, BUCKET, None), P(REPLICA, BUCKET), P(), P())
    return jax.shard_map(
        per_device, mesh=split, in_specs=in_specs, out_specs=out_specs, check_vma=False
    )
```

```python
import jax
import jax.numpy as jnp
from jax import lax
from jax.experimental import pallas as pl
from jax.experimental.pallas import tpu as pltpu
from jax.sharding import PartitionSpec as P

AXES = ("x", "z_hi", "z_lo", "y_lo", "y_hi", "core")
BUCKET = ("x", "z_hi", "z_lo", "y_lo")
REPLICA = ("y_hi", "core")
CUBE = ("x", "z_lo", "y_lo", "y_hi")
OWNERS = 32
D = 400
HALF = 200
WIDE = 256
FULL = 2 * WIDE
EDGES = 1000
EPAD = 1024
NEG = 500
NPAD = 512
ROWS = 512
NREL = 2066
PART = 72
RPAD = OWNERS * PART
LEVELS = 32000.0
F32 = jnp.float32
BF16 = jnp.bfloat16


def struct(shape, dtype):
    return jax.ShapeDtypeStruct(shape, dtype)


def call(kernel, out_shape, *args, scratch=(), name):
    return pl.pallas_call(
        kernel,
        out_shape=out_shape,
        scratch_shapes=scratch,
        compiler_params=pltpu.CompilerParams(vmem_limit_bytes=60 * 1024 * 1024),
        name=name,
    )(*args)


def from_next(block):
    count = lax.axis_size(BUCKET)
    return lax.ppermute(block, BUCKET, [((i + 1) % count, i) for i in range(count)])


def swap_core(block):
    return lax.ppermute(block, "core", [(0, 1), (1, 0)])


def dot(a, b, dims=((1,), (0,))):
    return lax.dot_general(a, b, (dims, ((), ())), preferred_element_type=F32)


def spread(rows):
    gap = jnp.zeros((rows.shape[0], WIDE - HALF), rows.dtype)
    return jnp.concatenate([rows[:, :HALF], gap, rows[:, HALF:], gap], 1)


def as_column(row):
    return jnp.transpose(jnp.broadcast_to(row, (8, row.shape[1])))[:, :1]


def picks(column, count):
    at = lax.broadcasted_iota(jnp.int32, (column.shape[0], count), 1)
    return jnp.where(at == column, 1.0, 0.0).astype(BF16)


def places(row, count, start=0):
    at = lax.broadcasted_iota(jnp.int32, (count, row.shape[1]), 0) + start
    return jnp.where(at == row, 1.0, 0.0).astype(BF16)


def edge_terms(left, slab, table, ids):
    cols = jnp.transpose(ids)
    src, dst, rel, neg = (cols[:, i : i + 1] for i in range(4))
    slab_low = slab.astype(BF16)
    heads = dot(picks(src, ROWS), left)
    rel_rows = dot(picks(rel, RPAD), table)
    h_re, h_im = heads[:, :WIDE], heads[:, WIDE:]
    r_re, r_im = rel_rows[:, :WIDE], rel_rows[:, WIDE:]
    prod = jnp.concatenate([h_re * r_re - h_im * r_im, h_re * r_im + h_im * r_re], 1).astype(BF16)
    prod_wide = prod.astype(F32)
    pos_rows = dot(picks(dst, ROWS), slab_low)
    neg_rows = dot(picks(neg[:NPAD], ROWS), slab_low).astype(BF16)
    pos = jnp.sum(prod_wide * pos_rows, 1, keepdims=True)
    g_pos = -jax.nn.sigmoid(-pos)
    g_neg = (jax.nn.sigmoid(dot(prod, neg_rows, ((1,), (1,)))) * (1.0 / NEG)).astype(BF16)
    d_pos = (g_pos * prod_wide).astype(BF16)
    d_prod = g_pos * pos_rows + dot(g_neg, neg_rows)
    p_re, p_im = d_prod[:, :WIDE], d_prod[:, WIDE:]
    d_rel = jnp.concatenate([p_re * h_re + p_im * h_im, p_im * h_re - p_re * h_im], 1)
    return prod, g_neg, d_pos, d_rel.astype(BF16)


def trained(slab, state, ids, prod, g_neg, d_pos):
    d_neg = dot(g_neg, prod, ((0,), (0,))).astype(BF16)
    grad = dot(places(ids[1:2], ROWS), d_pos) + dot(places(ids[3:4, :NPAD], ROWS), d_neg)
    state = state + jnp.sum(grad * grad, 1, keepdims=True) * (1.0 / D)
    return slab - grad * (0.1 * lax.rsqrt(state)), state


def prepare_kernel(left, src, dst, rel, neg, left_low, ids):
    left_low[...] = spread(left[...]).astype(BF16)
    ids[...] = jnp.full(ids.shape, -1, jnp.int32)
    for step in range(2):
        for place, source in enumerate((src, dst, rel, neg)):
            ids[step, place : place + 1, : source.shape[1]] = source[step : step + 1, :]


def first_kernel(left, slab, state, relation, ids, slab_out, state_out, d_rel_out, table_out):
    table_out[:NREL, :] = spread(relation[...]).astype(BF16)
    table_out[NREL:, :] = jnp.zeros((RPAD - NREL, FULL), BF16)
    slab_wide = spread(slab[...])
    prod, g_neg, d_pos, d_rel = edge_terms(left[...], slab_wide, table_out[...], ids[0])
    d_rel_out[...] = d_rel
    slab_out[...], state_out[...] = trained(
        slab_wide, as_column(state[...]), ids[0], prod, g_neg, d_pos
    )


def rel_half(core, ids, ids_next, d_rel, d_rel_next):
    at = pl.multiple_of(core * WIDE, WIDE)
    return dot(places(ids[0, 2:3], RPAD), d_rel[:, pl.ds(at, WIDE)]) + dot(
        places(ids_next[2:3], RPAD), d_rel_next[:, pl.ds(at, WIDE)]
    )


def second_kernel(core, left, slab, table, ids, ids_next, d_rel, prod, g_neg, d_pos, d_rel_next, other):
    prod[...], g_neg[...], d_pos[...], d_rel_next[...] = edge_terms(
        left[...], slab[...], table[...], ids_next[...]
    )
    other[...] = rel_half(1 - core[0], ids, ids_next, d_rel, d_rel_next)


def finish_kernel(core, slab, state, ids, ids_next, d_rel, prod, g_neg, d_pos, d_rel_next, mine, slab_out, state_out):
    mine[...] = rel_half(core[0], ids, ids_next, d_rel, d_rel_next)
    new_slab, new_state = trained(
        slab[...], state[...], ids_next[...], prod[...], g_neg[...], d_pos[...]
    )
    slab_out[:, :HALF] = new_slab[:, :HALF]
    slab_out[:, HALF:] = new_slab[:, WIDE : WIDE + HALF]
    state_out[...] = jnp.transpose(jnp.broadcast_to(new_state, (ROWS, 128)))[:1]


def encode(total):
    top = jnp.max(jnp.abs(total), axis=1, keepdims=True)
    power = jnp.ceil(jnp.log2(jnp.maximum(top, 1e-30)))
    codes = jnp.round(total * (LEVELS * jnp.exp2(-power)))
    lane = lax.broadcasted_iota(jnp.int32, total.shape, 1)
    codes = jnp.where(lane < HALF, codes, power)
    return jnp.concatenate([codes[:, :128], codes[:, 128:]], 0).astype(jnp.int32).astype(jnp.int16)


def decode(codes):
    wide = codes.astype(jnp.int32).astype(F32)
    low, high = wide[:PART], wide[PART:]
    step = jnp.exp2(high[:, 127:128]) * (1.0 / LEVELS)
    lane = lax.broadcasted_iota(jnp.int32, high.shape, 1)
    return low * step, jnp.where(lane < HALF - 128, high * step, 0.0)


def send_kernel(mine, theirs, codes):
    def one(i, _):
        at = pl.ds(pl.multiple_of(i * PART, 8), PART)
        codes[i] = encode(mine[at, :] + theirs[at, :])
        return 0

    lax.fori_loop(0, OWNERS, one, 0)


def gather_kernel(parts, codes):
    low, high = decode(parts[0])
    for i in range(1, OWNERS):
        more = decode(parts[i])
        low, high = low + more[0], high + more[1]
    codes[...] = encode(jnp.concatenate([low, high], 1))


def spread_kernel(a, b, c, d, copies):
    a, b, c, d = (decode(part[...]) for part in (a, b, c, d))
    low, high = ((a[i] + c[i]) + (b[i] + d[i]) for i in range(2))
    code = encode(jnp.concatenate([low, high], 1))
    for i in range(OWNERS):
        copies[i] = code


def update_kernel(core, ours, theirs, relation, state, relation_out, state_out):
    first = core[0] == 0
    ours, theirs = decode(ours[0]), decode(theirs[0])
    total = jnp.sum(sum(part * part for part in (*ours, *theirs)), 1, keepdims=True)
    new_state = state[0] + total * (1.0 / D)
    rate = 0.2 * lax.rsqrt(new_state)
    ours, theirs = (jnp.concatenate(pair, 1) * rate for pair in (ours, theirs))
    real, imag = jnp.where(first, ours, theirs), jnp.where(first, theirs, ours)
    relation_out[:, :HALF] = relation[:, :HALF] - real[:, :HALF]
    relation_out[:, HALF:] = relation[:, HALF:] - imag[:, :HALF]
    state_out[0] = new_state


def per_device(
    left_embed,
    right_embed,
    right_state,
    relation_embed,
    relation_state,
    source_rows,
    target_rows,
    relation_ids,
    negative_rows,
):
    core = lax.axis_index("core").astype(jnp.int32)[None]
    smem = pl.BlockSpec(memory_space=pltpu.SMEM)
    vmem = pl.BlockSpec(memory_space=pltpu.VMEM)

    def with_core(kernel, out_shape, *args, name):
        return pl.pallas_call(
            kernel,
            out_shape=out_shape,
            in_specs=[smem] + [vmem] * len(args),
            compiler_params=pltpu.CompilerParams(vmem_limit_bytes=60 * 1024 * 1024),
            name=name,
        )(core, *args)

    left_low, ids = call(
        prepare_kernel,
        (struct((ROWS, FULL), BF16), struct((2, 8, EPAD), jnp.int32)),
        left_embed[0],
        source_rows[0, 0],
        target_rows[0, 0],
        relation_ids[0, 0],
        negative_rows[0, 0],
        name="prepare",
    )
    left_next = from_next(left_low)
    ids_next = from_next(ids[1])
    edge_array = struct((EPAD, FULL), BF16)
    half_array = struct((RPAD, WIDE), F32)
    slab, state, d_rel, table = call(
        first_kernel,
        (struct((ROWS, FULL), F32), struct((ROWS, 1), F32), edge_array, struct((RPAD, FULL), BF16)),
        left_low,
        right_embed[0],
        right_state,
        relation_embed,
        ids,
        name="first",
    )
    prod, g_neg, d_pos, d_rel_next, other = with_core(
        second_kernel,
        (edge_array, struct((EPAD, NPAD), BF16), edge_array, edge_array, half_array),
        left_next,
        slab,
        table,
        ids,
        ids_next,
        d_rel,
        name="second",
    )
    theirs = swap_core(other)
    mine, slab_out, state_out = with_core(
        finish_kernel,
        (half_array, struct((ROWS, D), F32), struct((1, ROWS), F32)),
        slab,
        state,
        ids,
        ids_next,
        d_rel,
        prod,
        g_neg,
        d_pos,
        d_rel_next,
        name="finish",
    )
    part = struct((2 * PART, 128), jnp.int16)
    parts = struct((OWNERS, 2 * PART, 128), jnp.int16)
    sent = call(send_kernel, parts, mine, theirs, name="send")
    got = lax.all_to_all(sent, CUBE, 0, 0, tiled=True)
    code = call(gather_kernel, part, got, name="gather")
    count = lax.axis_size("z_hi")
    ring = [
        lax.ppermute(code, "z_hi", [((i + k) % count, i) for i in range(count)])
        for k in range(1, count)
    ]
    copies = call(spread_kernel, parts, code, *ring, name="spread")
    ours = lax.all_to_all(copies, CUBE, 0, 0, tiled=True)
    theirs = swap_core(ours)
    block = pl.BlockSpec((1, 2 * PART, 128), lambda i: (i, 0, 0))
    rows = pl.BlockSpec((PART, D), lambda i: (i, 0))
    column = pl.BlockSpec((1, PART, 1), lambda i: (i, 0, 0))
    state_in = jnp.pad(relation_state, (0, RPAD - NREL), constant_values=1.0)
    relation_out, relation_state_out = pl.pallas_call(
        update_kernel,
        grid=(pl.cdiv(NREL, PART),),
        in_specs=[smem, block, block, rows, column],
        out_specs=(rows, column),
        out_shape=(struct((NREL, D), F32), struct((OWNERS, PART, 1), F32)),
        compiler_params=pltpu.CompilerParams(vmem_limit_bytes=60 * 1024 * 1024),
        name="update",
    )(core, ours, theirs, relation_embed, state_in.reshape(OWNERS, PART, 1))
    relation_state_out = relation_state_out.reshape(RPAD)[:NREL]
    return (slab_out[None], state_out, relation_out, relation_state_out)


def solution(mesh):
    split = jax.sharding.Mesh(mesh.devices.reshape(4, 4, 2, 2, 2, 2), AXES)
    in_specs = (
        P(REPLICA, BUCKET, None),
        P(REPLICA, BUCKET, None),
        P(REPLICA, BUCKET),
        P(),
        P(),
        P(REPLICA, BUCKET, None, None),
        P(REPLICA, BUCKET, None, None),
        P(REPLICA, BUCKET, None, None),
        P(REPLICA, BUCKET, None, None),
    )
    out_specs = (P(REPLICA, BUCKET, None), P(REPLICA, BUCKET), P(), P())
    return jax.shard_map(
        per_device, mesh=split, in_specs=in_specs, out_specs=out_specs, check_vma=False
    )
```

```python
import jax
import jax.numpy as jnp
from jax import lax
from jax.experimental import pallas as pl
from jax.experimental.pallas import tpu as pltpu
from jax.sharding import PartitionSpec as P

AXES = ("x", "z_hi", "z_lo", "y_lo", "y_hi", "core")
BUCKET = ("x", "z_hi", "z_lo", "y_lo")
REPLICA = ("y_hi", "core")
CUBE = ("x", "z_lo", "y_lo", "y_hi")
OWNERS = 32
D = 400
HALF = 200
EPAD = 1024
NEG = 500
NPAD = 512
ROWS = 512
NREL = 2066
RMAIN = 2048
RPAD = 2176
CUT = 104
PART = 112
LEVELS = 32000.0
F32 = jnp.float32
BF16 = jnp.bfloat16


def struct(shape, dtype):
    return jax.ShapeDtypeStruct(shape, dtype)


def call(kernel, out_shape, *args, scratch=(), name):
    return pl.pallas_call(
        kernel,
        out_shape=out_shape,
        scratch_shapes=scratch,
        compiler_params=pltpu.CompilerParams(vmem_limit_bytes=60 * 1024 * 1024),
        name=name,
    )(*args)


def from_next(block):
    count = lax.axis_size(BUCKET)
    return lax.ppermute(block, BUCKET, [((i + 1) % count, i) for i in range(count)])


def swap_core(block):
    return lax.ppermute(block, "core", [(0, 1), (1, 0)])


def dot(a, b, dims=((1,), (0,))):
    return lax.dot_general(a, b, (dims, ((), ())), preferred_element_type=F32)


def places(row, count):
    at = lax.broadcasted_iota(jnp.int32, (count, row.shape[1]), 0)
    return jnp.where(at == row, 1.0, 0.0).astype(BF16)


def edge_terms(left, slab, table, ids):
    slab_low = slab.astype(BF16)
    heads = dot(left, places(ids[0:1], ROWS))
    rel_rows = dot(table, places(ids[2:3], RPAD))
    h_re, h_im = heads[:HALF], heads[HALF:]
    r_re, r_im = rel_rows[:HALF], rel_rows[HALF:]
    prod = jnp.concatenate([h_re * r_re - h_im * r_im, h_re * r_im + h_im * r_re], 0).astype(BF16)
    prod_wide = prod.astype(F32)
    pos_rows = dot(slab_low, places(ids[1:2], ROWS))
    neg_rows = dot(slab_low, places(ids[3:4, :NPAD], ROWS)).astype(BF16)
    pos = jnp.sum(prod_wide * pos_rows, 0, keepdims=True)
    g_pos = -jax.nn.sigmoid(-pos)
    g_neg = (jax.nn.sigmoid(dot(neg_rows, prod, ((0,), (0,)))) * (1.0 / NEG)).astype(BF16)
    d_pos = (g_pos * prod_wide).astype(BF16)
    d_prod = g_pos * pos_rows + dot(neg_rows, g_neg)
    p_re, p_im = d_prod[:HALF], d_prod[HALF:]
    d_rel = (p_re * h_re + p_im * h_im, p_im * h_re - p_re * h_im)
    return prod, g_neg, d_pos, [part.astype(BF16) for part in d_rel]


def trained(slab, state, ids, prod, g_neg, d_pos):
    along = ((1,), (1,))
    d_neg = dot(prod, g_neg, along).astype(BF16)
    grad = dot(d_pos, places(ids[1:2], ROWS), along)
    grad = grad + dot(d_neg, places(ids[3:4, :NPAD], ROWS), along)
    state = state + jnp.sum(grad * grad, 0, keepdims=True) * (1.0 / D)
    return slab - grad * (0.1 * lax.rsqrt(state)), state


def prepare_kernel(left, src, dst, rel, neg, left_low, ids):
    left_low[...] = left[...].astype(BF16)
    ids[...] = jnp.full(ids.shape, -1, jnp.int32)
    for step in range(2):
        for place, source in enumerate((src, dst, rel, neg)):
            ids[step, place : place + 1, : source.shape[1]] = source[step : step + 1, :]


def first_kernel(left, slab, state, relation, ids, slab_out, state_out, d_rel_out, table_out):
    table_out[:, :RMAIN] = relation[:, :RMAIN].astype(BF16)
    table_out[:, RMAIN:] = jnp.zeros((D, RPAD - RMAIN), BF16)
    table_out[:, RMAIN:NREL] = relation[:, RMAIN:].astype(BF16)
    prod, g_neg, d_pos, d_rel = edge_terms(left[...], slab[...], table_out[...], ids[0])
    for half in range(2):
        d_rel_out[half] = d_rel[half]
    slab_out[...], state_out[...] = trained(slab[...], state[...], ids[0], prod, g_neg, d_pos)


def rel_half(half, ids, ids_next, d_rel, d_rel_next):
    along = ((1,), (1,))
    return dot(d_rel[half], places(ids[0, 2:3], RPAD), along) + dot(
        d_rel_next[half], places(ids_next[2:3], RPAD), along
    )


def second_kernel(core, left, slab, table, ids, ids_next, d_rel, prod, g_neg, d_pos, d_rel_next, other):
    prod[...], g_neg[...], d_pos[...], parts = edge_terms(
        left[...], slab[...], table[...], ids_next[...]
    )
    for half in range(2):
        d_rel_next[half] = parts[half]
    other[...] = rel_half(1 - core[0], ids, ids_next, d_rel, d_rel_next)


def finish_kernel(core, slab, state, ids, ids_next, d_rel, prod, g_neg, d_pos, d_rel_next, mine, slab_out, state_out):
    mine[...] = rel_half(core[0], ids, ids_next, d_rel, d_rel_next)
    slab_out[...], state_out[...] = trained(
        slab[...], state[...], ids_next[...], prod[...], g_neg[...], d_pos[...]
    )


def power_of(block):
    top = jnp.max(jnp.abs(block), axis=0, keepdims=True)
    return jnp.ceil(jnp.log2(jnp.maximum(top, 1e-30)))


def encode(main, last):
    lane = lax.broadcasted_iota(jnp.int32, last.shape, 1)
    row = lax.broadcasted_iota(jnp.int32, last.shape, 0)
    last = jnp.where(row < 7, last, 0.0)
    main_power, last_power = power_of(main), power_of(last)
    main = jnp.round(main * (LEVELS * jnp.exp2(-main_power)))
    last = jnp.round(last * (LEVELS * jnp.exp2(-last_power)))
    last_power = pltpu.roll(jnp.broadcast_to(last_power, last.shape), 64, 1)
    last = jnp.where(lane < 64, last, last_power)
    last = jnp.where(row == 7, jnp.broadcast_to(main_power, last.shape), last)
    fill = [jnp.zeros((CUT - main.shape[0], 128), F32)] if main.shape[0] < CUT else []
    return jnp.concatenate([main, *fill, last], 0).astype(jnp.int32).astype(jnp.int16)


def decode(codes):
    wide = codes.astype(jnp.int32).astype(F32)
    main, last = wide[:CUT], wide[CUT:]
    lane = lax.broadcasted_iota(jnp.int32, last.shape, 1)
    row = lax.broadcasted_iota(jnp.int32, last.shape, 0)
    main = main * (jnp.exp2(last[7:8]) * (1.0 / LEVELS))
    last_step = jnp.exp2(pltpu.roll(last, 64, 1)) * (1.0 / LEVELS)
    valid = jnp.logical_and(lane < NREL - RMAIN, row < 7)
    return main, jnp.where(valid, last * last_step, 0.0)


def place_of(part):
    tile, low = divmod(part, 2)
    rows = slice(CUT, HALF) if low else slice(0, CUT)
    return rows, slice(128 * tile, 128 * tile + 128)


def send_kernel(mine, theirs, codes, last):
    last[HALF:] = jnp.zeros((last.shape[0] - HALF, 128), F32)
    last[:HALF] = mine[:, RMAIN:] + theirs[:, RMAIN:]
    for part in range(OWNERS):
        at = place_of(part)
        codes[part] = encode(mine[at] + theirs[at], last[7 * part : 7 * part + 8])


def gather_kernel(parts, codes):
    main, last = decode(parts[0])
    for part in range(1, OWNERS):
        more = decode(parts[part])
        main, last = main + more[0], last + more[1]
    codes[...] = encode(main, last)


def spread_kernel(a, b, c, d, copies):
    a, b, c, d = (decode(part[...]) for part in (a, b, c, d))
    code = encode(*((a[i] + c[i]) + (b[i] + d[i]) for i in range(2)))
    for part in range(OWNERS):
        copies[part] = code


def update_kernel(core, ours, theirs, relation, state, relation_out, state_out, grads, last):
    for half, codes in enumerate((ours, theirs)):
        for part in range(OWNERS):
            rows, lanes = place_of(part)
            main, tail = decode(codes[part])
            grads[half, rows, lanes] = main[: rows.stop - rows.start]
            last[7 * part : 7 * part + 8] = tail
        grads[half, :, RMAIN:] = last[:HALF]
    both = grads[0], grads[1]
    total = sum(jnp.sum(part * part, 0, keepdims=True) for part in both)[:, :NREL]
    new_state = state[...] + total * (1.0 / D)
    rate = 0.2 * lax.rsqrt(new_state)
    real, imag = grads[core[0]], grads[1 - core[0]]
    relation_out[:HALF] = relation[:HALF] - real[:, :NREL] * rate
    relation_out[HALF:] = relation[HALF:] - imag[:, :NREL] * rate
    state_out[...] = new_state


def per_device(
    left_embed,
    right_embed,
    right_state,
    relation_embed,
    relation_state,
    source_rows,
    target_rows,
    relation_ids,
    negative_rows,
):
    core = lax.axis_index("core").astype(jnp.int32)[None]
    smem = pl.BlockSpec(memory_space=pltpu.SMEM)
    vmem = pl.BlockSpec(memory_space=pltpu.VMEM)

    def with_core(kernel, out_shape, *args, scratch=(), name):
        return pl.pallas_call(
            kernel,
            out_shape=out_shape,
            scratch_shapes=scratch,
            in_specs=[smem] + [vmem] * len(args),
            compiler_params=pltpu.CompilerParams(vmem_limit_bytes=60 * 1024 * 1024),
            name=name,
        )(core, *args)

    left_low, ids = call(
        prepare_kernel,
        (struct((D, ROWS), BF16), struct((2, 8, EPAD), jnp.int32)),
        left_embed[0].T,
        source_rows[0, 0],
        target_rows[0, 0],
        relation_ids[0, 0],
        negative_rows[0, 0],
        name="prepare",
    )
    left_next = from_next(left_low)
    ids_next = from_next(ids[1])
    relation = relation_embed.T
    slab_array, state_array = struct((D, ROWS), F32), struct((1, ROWS), F32)
    edge_array = struct((D, EPAD), BF16)
    pair_array = struct((2, HALF, EPAD), BF16)
    half_array = struct((HALF, RPAD), F32)
    slab, state, d_rel, table = call(
        first_kernel,
        (slab_array, state_array, pair_array, struct((D, RPAD), BF16)),
        left_low,
        right_embed[0].T,
        right_state,
        relation,
        ids,
        name="first",
    )
    prod, g_neg, d_pos, d_rel_next, other = with_core(
        second_kernel,
        (edge_array, struct((NPAD, EPAD), BF16), edge_array, pair_array, half_array),
        left_next,
        slab,
        table,
        ids,
        ids_next,
        d_rel,
        name="second",
    )
    theirs = swap_core(other)
    mine, slab_out, state_out = with_core(
        finish_kernel,
        (half_array, slab_array, state_array),
        slab,
        state,
        ids,
        ids_next,
        d_rel,
        prod,
        g_neg,
        d_pos,
        d_rel_next,
        name="finish",
    )
    part = struct((PART, 128), jnp.int16)
    parts = struct((OWNERS, PART, 128), jnp.int16)
    last = pltpu.VMEM((232, 128), F32)
    sent = call(send_kernel, parts, mine, theirs, scratch=[last], name="send")
    got = lax.all_to_all(sent, CUBE, 0, 0, tiled=True)
    code = call(gather_kernel, part, got, name="gather")
    count = lax.axis_size("z_hi")
    ring = [
        lax.ppermute(code, "z_hi", [((i + k) % count, i) for i in range(count)])
        for k in range(1, count)
    ]
    copies = call(spread_kernel, parts, code, *ring, name="spread")
    ours = lax.all_to_all(copies, CUBE, 0, 0, tiled=True)
    theirs = swap_core(ours)
    relation_out, relation_state_out = with_core(
        update_kernel,
        (struct((D, NREL), F32), struct((1, NREL), F32)),
        ours,
        theirs,
        relation,
        relation_state[None],
        scratch=[pltpu.VMEM((2, HALF, RPAD), F32), last],
        name="update",
    )
    return (slab_out.T[None], state_out, relation_out.T, relation_state_out[0])


def solution(mesh):
    split = jax.sharding.Mesh(mesh.devices.reshape(4, 4, 2, 2, 2, 2), AXES)
    in_specs = (
        P(REPLICA, BUCKET, None),
        P(REPLICA, BUCKET, None),
        P(REPLICA, BUCKET),
        P(),
        P(),
        P(REPLICA, BUCKET, None, None),
        P(REPLICA, BUCKET, None, None),
        P(REPLICA, BUCKET, None, None),
        P(REPLICA, BUCKET, None, None),
    )
    out_specs = (P(REPLICA, BUCKET, None), P(REPLICA, BUCKET), P(), P())
    return jax.shard_map(
        per_device, mesh=split, in_specs=in_specs, out_specs=out_specs, check_vma=False
    )
```

```python
import jax
import jax.numpy as jnp
from jax import lax
from jax.experimental import pallas as pl
from jax.experimental.pallas import tpu as pltpu
from jax.sharding import PartitionSpec as P

AXES = ("x", "z_hi", "z_lo", "y_lo", "y_hi", "core")
BUCKET = ("x", "z_hi", "z_lo", "y_lo")
REPLICA = ("y_hi", "core")
CUBE = ("x", "z_lo", "y_lo", "y_hi")
OWNERS = 32
D = 400
HALF = 200
EPAD = 1024
NEG = 500
NPAD = 512
ROWS = 512
NREL = 2066
RMAIN = 2048
RPAD = 2176
CUT = 104
PART = 112
LEVELS = 32000.0
F32 = jnp.float32
BF16 = jnp.bfloat16


def struct(shape, dtype):
    return jax.ShapeDtypeStruct(shape, dtype)


def kept(shape, dtype):
    return pltpu.VMEM(shape, dtype)


def near(array):
    return pltpu.with_memory_space_constraint(array, pltpu.VMEM)


def call(kernel, out_shape, *args, core=None, scratch=(), far_out=(), name, limit=32):
    vmem = pl.BlockSpec(memory_space=pltpu.VMEM)
    far = pl.BlockSpec(memory_space=pl.ANY)
    several = isinstance(out_shape, tuple)
    outs = out_shape if several else (out_shape,)
    specs = tuple(far if i in far_out else vmem for i in range(len(outs)))
    in_specs = [vmem] * len(args)
    args = [near(arg) for arg in args]
    if core is not None:
        in_specs, args = [pl.BlockSpec(memory_space=pltpu.SMEM)] + in_specs, [core] + args
    return pl.pallas_call(
        kernel,
        out_shape=out_shape,
        in_specs=in_specs,
        out_specs=specs if several else specs[0],
        scratch_shapes=scratch,
        compiler_params=pltpu.CompilerParams(vmem_limit_bytes=limit * 1024 * 1024),
        name=name,
    )(*args)


def from_next(block):
    count = lax.axis_size(BUCKET)
    return lax.ppermute(block, BUCKET, [((i + 1) % count, i) for i in range(count)])


def swap_core(block):
    return lax.ppermute(block, "core", [(0, 1), (1, 0)])


def dot(a, b, dims=((1,), (0,))):
    return lax.dot_general(a, b, (dims, ((), ())), preferred_element_type=F32)


def places(row, count):
    at = lax.broadcasted_iota(jnp.int32, (count, row.shape[1]), 0).astype(jnp.int16)
    return jnp.where(at == row.astype(jnp.int16), BF16(1), BF16(0))


def edge_terms(left, slab, table, ids):
    slab_low = slab.astype(BF16)
    heads = dot(left, places(ids[0:1], ROWS))
    rel_rows = dot(table, places(ids[2:3], RPAD))
    h_re, h_im = heads[:HALF], heads[HALF:]
    r_re, r_im = rel_rows[:HALF], rel_rows[HALF:]
    prod = jnp.concatenate([h_re * r_re - h_im * r_im, h_re * r_im + h_im * r_re], 0).astype(BF16)
    prod_wide = prod.astype(F32)
    pos_rows = dot(slab_low, places(ids[1:2], ROWS))
    neg_rows = dot(slab_low, places(ids[3:4, :NPAD], ROWS)).astype(BF16)
    pos = jnp.sum(prod_wide * pos_rows, 0, keepdims=True)
    g_pos = -jax.nn.sigmoid(-pos)
    g_neg = (jax.nn.sigmoid(dot(neg_rows, prod, ((0,), (0,)))) * (1.0 / NEG)).astype(BF16)
    d_pos = (g_pos * prod_wide).astype(BF16)
    d_prod = g_pos * pos_rows + dot(neg_rows, g_neg)
    p_re, p_im = d_prod[:HALF], d_prod[HALF:]
    d_rel = (p_re * h_re + p_im * h_im, p_im * h_re - p_re * h_im)
    return prod, g_neg, d_pos, [part.astype(BF16) for part in d_rel]


def trained(slab, state, ids, prod, g_neg, d_pos):
    along = ((1,), (1,))
    d_neg = dot(prod, g_neg, along).astype(BF16)
    grad = dot(d_pos, places(ids[1:2], ROWS), along)
    grad = grad + dot(d_neg, places(ids[3:4, :NPAD], ROWS), along)
    state = state + jnp.sum(grad * grad, 0, keepdims=True) * (1.0 / D)
    return slab - grad * (0.1 * lax.rsqrt(state)), state


def prepare_kernel(left, src, dst, rel, neg, ids, message, next_ids):
    message[:D] = left[...].astype(BF16)
    ids[...] = jnp.full(ids.shape, -1, jnp.int32)
    next_ids[...] = jnp.full(next_ids.shape, -1, jnp.int32)
    for place, source in enumerate((src, dst, rel, neg)):
        ids[place : place + 1, : source.shape[1]] = source[0:1, :]
        next_ids[place : place + 1, : source.shape[1]] = source[1:2, :]
    high, low = (next_ids[...] >> 6).astype(F32), (next_ids[...] & 63).astype(F32)
    halves = slice(0, ROWS), slice(ROWS, EPAD)
    packed = [part[:4, half] for part in (high, low) for half in halves]
    message[D:] = jnp.concatenate(packed, 0).astype(BF16)


def unpacked_ids(message):
    coded = message[D:].astype(F32)
    halves = (coded[4 * i : 4 * i + 4] * 64.0 + coded[8 + 4 * i : 12 + 4 * i] for i in range(2))
    rows = jnp.concatenate(list(halves), 1).astype(jnp.int32)
    return jnp.concatenate([rows, rows], 0)


def first_kernel(left, slab, state, relation, ids, slab_out, state_out, d_rel_out, table_out):
    table_out[:, :RMAIN] = relation[:, :RMAIN].astype(BF16)
    table_out[:, RMAIN:] = jnp.zeros((D, RPAD - RMAIN), BF16)
    table_out[:, RMAIN:NREL] = relation[:, RMAIN:].astype(BF16)
    prod, g_neg, d_pos, d_rel = edge_terms(left[:D], slab[...], table_out[...], ids[...])
    for half in range(2):
        d_rel_out[half] = d_rel[half]
    slab_out[...], state_out[...] = trained(slab[...], state[...], ids[...], prod, g_neg, d_pos)


def rel_half(half, ids, ids_next, d_rel, d_rel_next):
    along = ((1,), (1,))
    return dot(d_rel[half], places(ids[2:3], RPAD), along) + dot(
        d_rel_next[half], places(ids_next[2:3], RPAD), along
    )


def second_kernel(
    core, left, slab, table, ids, d_rel, ids_next, prod, g_neg, d_pos, d_rel_next, other
):
    ids_next[...] = unpacked_ids(left[...])
    prod[...], g_neg[...], d_pos[...], parts = edge_terms(
        left[:D], slab[...], table[...], ids_next[...]
    )
    for half in range(2):
        d_rel_next[half] = parts[half]
    other[...] = rel_half(1 - core[0], ids, ids_next, d_rel, d_rel_next)


def finish_kernel(
    core, slab, state, ids, ids_next, d_rel, prod, g_neg, d_pos, d_rel_next, mine, slab_out, state_out
):
    mine[...] = rel_half(core[0], ids, ids_next, d_rel, d_rel_next)
    slab_out[...], state_out[...] = trained(
        slab[...], state[...], ids_next[...], prod[...], g_neg[...], d_pos[...]
    )


def power_of(block):
    top = jnp.max(jnp.abs(block), axis=0, keepdims=True)
    return jnp.ceil(jnp.log2(jnp.maximum(top, 1e-30)))


def encode(main, last):
    lane = lax.broadcasted_iota(jnp.int32, last.shape, 1)
    row = lax.broadcasted_iota(jnp.int32, last.shape, 0)
    last = jnp.where(row < 7, last, 0.0)
    main_power, last_power = power_of(main), power_of(last)
    main = jnp.round(main * (LEVELS * jnp.exp2(-main_power)))
    last = jnp.round(last * (LEVELS * jnp.exp2(-last_power)))
    last_power = pltpu.roll(jnp.broadcast_to(last_power, last.shape), 64, 1)
    last = jnp.where(lane < 64, last, last_power)
    last = jnp.where(row == 7, jnp.broadcast_to(main_power, last.shape), last)
    fill = [jnp.zeros((CUT - main.shape[0], 128), F32)] if main.shape[0] < CUT else []
    return jnp.concatenate([main, *fill, last], 0).astype(jnp.int32).astype(jnp.int16)


def decode(codes):
    wide = codes.astype(jnp.int32).astype(F32)
    main, last = wide[:CUT], wide[CUT:]
    lane = lax.broadcasted_iota(jnp.int32, last.shape, 1)
    row = lax.broadcasted_iota(jnp.int32, last.shape, 0)
    main = main * (jnp.exp2(last[7:8]) * (1.0 / LEVELS))
    last_step = jnp.exp2(pltpu.roll(last, 64, 1)) * (1.0 / LEVELS)
    valid = jnp.logical_and(lane < NREL - RMAIN, row < 7)
    return main, jnp.where(valid, last * last_step, 0.0)


def place_of(part):
    tile, low = divmod(part, 2)
    rows = slice(CUT, HALF) if low else slice(0, CUT)
    return rows, slice(128 * tile, 128 * tile + 128)


def send_kernel(mine, theirs, codes, last):
    last[HALF:] = jnp.zeros((last.shape[0] - HALF, 128), F32)
    last[:HALF] = mine[:, RMAIN:] + theirs[:, RMAIN:]
    for part in range(OWNERS):
        at = place_of(part)
        codes[part] = encode(mine[at] + theirs[at], last[7 * part : 7 * part + 8])


def gather_kernel(parts, codes):
    main, last = decode(parts[0])
    for part in range(1, OWNERS):
        more = decode(parts[part])
        main, last = main + more[0], last + more[1]
    code = encode(main, last)
    for copy in range(codes.shape[0]):
        codes[copy] = code


def spread_kernel(parts, copies):
    main, last = decode(parts[0])
    for part in range(1, parts.shape[0]):
        more = decode(parts[part])
        main, last = main + more[0], last + more[1]
    code = encode(main, last)
    for copy in range(OWNERS):
        copies[copy] = code


def update_kernel(core, ours, theirs, relation, state, relation_out, state_out, grads, last, wide, sems):
    for half, codes in enumerate((ours, theirs)):
        for part in range(OWNERS):
            rows, lanes = place_of(part)
            main, tail = decode(codes[part])
            grads[half, rows, lanes] = main[: rows.stop - rows.start]
            last[7 * part : 7 * part + 8] = tail
        grads[half, :, RMAIN:] = last[:HALF]
    both = grads[0], grads[1]
    total = sum(jnp.sum(part * part, 0, keepdims=True) for part in both)[:, :NREL]
    new_state = state[...] + total * (1.0 / D)
    rate = 0.2 * lax.rsqrt(new_state)
    state_out[...] = new_state
    copies = []
    for half in range(2):
        rows = slice(half * HALF, half * HALF + HALF)
        grad = grads[core[0] if half == 0 else 1 - core[0]]
        wide[half] = relation[rows] - grad[:, :NREL] * rate
        copies.append(pltpu.make_async_copy(wide.at[half], relation_out.at[rows], sems.at[half]))
        copies[half].start()
    for copy in copies:
        copy.wait()


def per_device(
    left_embed,
    right_embed,
    right_state,
    relation_embed,
    relation_state,
    source_rows,
    target_rows,
    relation_ids,
    negative_rows,
):
    core = lax.axis_index("core").astype(jnp.int32)[None]
    ids, message = call(
        prepare_kernel,
        (kept((8, EPAD), jnp.int32), kept((D + 16, ROWS), BF16)),
        left_embed[0].T,
        source_rows[0, 0],
        target_rows[0, 0],
        relation_ids[0, 0],
        negative_rows[0, 0],
        scratch=[pltpu.VMEM((8, EPAD), jnp.int32)],
        name="prepare",
    )
    message_next = from_next(message)
    relation = relation_embed.T
    slab_array, state_array = (D, ROWS), (1, ROWS)
    edge_array = kept((D, EPAD), BF16)
    pair_array = kept((2, HALF, EPAD), BF16)
    half_array = kept((HALF, RPAD), F32)
    slab, state, d_rel, table = call(
        first_kernel,
        (kept(slab_array, F32), kept(state_array, F32), pair_array, kept((D, RPAD), BF16)),
        message,
        right_embed[0].T,
        right_state,
        relation,
        ids,
        name="first",
    )
    ids_next, prod, g_neg, d_pos, d_rel_next, other = call(
        second_kernel,
        (
            kept((8, EPAD), jnp.int32),
            edge_array,
            kept((NPAD, EPAD), BF16),
            edge_array,
            pair_array,
            half_array,
        ),
        message_next,
        slab,
        table,
        ids,
        d_rel,
        core=core,
        name="second",
    )
    theirs = swap_core(other)
    mine, slab_out, state_out = call(
        finish_kernel,
        (half_array, struct(slab_array, F32), struct(state_array, F32)),
        slab,
        state,
        ids,
        ids_next,
        d_rel,
        prod,
        g_neg,
        d_pos,
        d_rel_next,
        core=core,
        name="finish",
    )
    part = (PART, 128)
    last = pltpu.VMEM((232, 128), F32)
    parts = kept((OWNERS, *part), jnp.int16)
    sent = call(send_kernel, parts, mine, theirs, scratch=[last], name="send")
    got = lax.all_to_all(sent, CUBE, 0, 0, tiled=True)
    count = lax.axis_size("z_hi")
    codes = call(gather_kernel, kept((count, *part), jnp.int16), got, name="gather")
    codes = lax.all_to_all(codes, "z_hi", 0, 0, tiled=True)
    copies = call(spread_kernel, parts, codes, name="spread")
    ours = lax.all_to_all(copies, CUBE, 0, 0, tiled=True)
    theirs = swap_core(ours)
    relation_out, relation_state_out = call(
        update_kernel,
        (struct((D, NREL), F32), struct((1, NREL), F32)),
        ours,
        theirs,
        relation,
        relation_state[None],
        core=core,
        far_out=(0,),
        scratch=[
            pltpu.VMEM((2, HALF, RPAD), F32),
            last,
            pltpu.VMEM((2, HALF, NREL), F32),
            pltpu.SemaphoreType.DMA((2,)),
        ],
        name="update",
    )
    return (slab_out.T[None], state_out, relation_out.T, relation_state_out[0])


def solution(mesh):
    split = jax.sharding.Mesh(mesh.devices.reshape(4, 4, 2, 2, 2, 2), AXES)
    in_specs = (
        P(REPLICA, BUCKET, None),
        P(REPLICA, BUCKET, None),
        P(REPLICA, BUCKET),
        P(),
        P(),
        P(REPLICA, BUCKET, None, None),
        P(REPLICA, BUCKET, None, None),
        P(REPLICA, BUCKET, None, None),
        P(REPLICA, BUCKET, None, None),
    )
    out_specs = (P(REPLICA, BUCKET, None), P(REPLICA, BUCKET), P(), P())
    return jax.shard_map(
        per_device, mesh=split, in_specs=in_specs, out_specs=out_specs, check_vma=False
    )
```

```python
import jax
import jax.numpy as jnp
from jax import lax
from jax.experimental import pallas as pl
from jax.experimental.pallas import tpu as pltpu
from jax.sharding import PartitionSpec as P

AXES = ("x", "z_hi", "z_lo", "y_lo", "y_hi", "core")
BUCKET = ("x", "z_hi", "z_lo", "y_lo")
REPLICA = ("y_hi", "core")
CUBE = ("x", "z_lo", "y_lo", "y_hi")
OWNERS = 32
D = 400
HALF = 200
EPAD = 1024
NEG = 500
NPAD = 512
ROWS = 512
NREL = 2066
RMAIN = 2048
RPAD = 2176
CUT = 104
PART = 112
LEVELS = 32000.0
F32 = jnp.float32
BF16 = jnp.bfloat16


def struct(shape, dtype):
    return jax.ShapeDtypeStruct(shape, dtype)


def kept(shape, dtype):
    return pltpu.VMEM(shape, dtype)


def near(array):
    return pltpu.with_memory_space_constraint(array, pltpu.VMEM)


def away(array):
    return pltpu.with_memory_space_constraint(array, pltpu.HBM)


def call(kernel, out_shape, *args, core=None, scratch=(), far_in=(), far_out=(), name, limit=32):
    vmem = pl.BlockSpec(memory_space=pltpu.VMEM)
    far = pl.BlockSpec(memory_space=pltpu.HBM)
    several = isinstance(out_shape, tuple)
    outs = out_shape if several else (out_shape,)
    specs = tuple(far if i in far_out else vmem for i in range(len(outs)))
    in_specs = [far if i in far_in else vmem for i in range(len(args))]
    args = [away(arg) if i in far_in else near(arg) for i, arg in enumerate(args)]
    if core is not None:
        in_specs, args = [pl.BlockSpec(memory_space=pltpu.SMEM)] + in_specs, [core] + args
    return pl.pallas_call(
        kernel,
        out_shape=out_shape,
        in_specs=in_specs,
        out_specs=specs if several else specs[0],
        scratch_shapes=scratch,
        compiler_params=pltpu.CompilerParams(vmem_limit_bytes=limit * 1024 * 1024),
        name=name,
    )(*args)


def from_next(block):
    count = lax.axis_size(BUCKET)
    return lax.ppermute(block, BUCKET, [((i + 1) % count, i) for i in range(count)])


def swap_core(block):
    return lax.ppermute(block, "core", [(0, 1), (1, 0)])


def dot(a, b, dims=((1,), (0,))):
    return lax.dot_general(a, b, (dims, ((), ())), preferred_element_type=F32)


def places(row, count):
    at = lax.broadcasted_iota(jnp.int32, (count, row.shape[1]), 0).astype(jnp.int16)
    return jnp.where(at == row.astype(jnp.int16), BF16(1), BF16(0))


def target_rows_of(slab_low, ids):
    pos_rows = dot(slab_low, places(ids[1:2], ROWS))
    return pos_rows, dot(slab_low, places(ids[3:4, :NPAD], ROWS)).astype(BF16)


def relation_rows_of(table, ids):
    return dot(table, places(ids[2:3], RPAD))


def edge_terms(heads, pos_rows, neg_rows, rel_rows):
    h_re, h_im = heads[:HALF], heads[HALF:]
    r_re, r_im = rel_rows[:HALF], rel_rows[HALF:]
    prod = jnp.concatenate([h_re * r_re - h_im * r_im, h_re * r_im + h_im * r_re], 0).astype(BF16)
    prod_wide = prod.astype(F32)
    pos = jnp.sum(prod_wide * pos_rows, 0, keepdims=True)
    g_pos = -jax.nn.sigmoid(-pos)
    g_neg = (jax.nn.sigmoid(dot(neg_rows, prod, ((0,), (0,)))) * (1.0 / NEG)).astype(BF16)
    d_pos = (g_pos * prod_wide).astype(BF16)
    d_prod = g_pos * pos_rows + dot(neg_rows, g_neg)
    p_re, p_im = d_prod[:HALF], d_prod[HALF:]
    d_rel = (p_re * h_re + p_im * h_im, p_im * h_re - p_re * h_im)
    return prod, g_neg, d_pos, [part.astype(BF16) for part in d_rel]


def trained(slab, state, ids, prod, g_neg, d_pos):
    along = ((1,), (1,))
    d_neg = dot(prod, g_neg, along).astype(BF16)
    grad = dot(d_pos, places(ids[1:2], ROWS), along)
    grad = grad + dot(d_neg, places(ids[3:4, :NPAD], ROWS), along)
    state = state + jnp.sum(grad * grad, 0, keepdims=True) * (1.0 / D)
    return slab - grad * (0.1 * lax.rsqrt(state)), state


def prepare_kernel(left, src, dst, rel, neg, ids, next_ids, left_low, wide, places_in, sems):
    sources = (src, dst, rel, neg)
    copies = [pltpu.make_async_copy(left, wide, sems.at[4])]
    copies += [pltpu.make_async_copy(r, places_in[i], sems.at[i]) for i, r in enumerate(sources)]
    for copy in copies:
        copy.start()
    for step_ids in (ids, next_ids):
        step_ids[...] = jnp.full(step_ids.shape, -1, jnp.int32)
    for copy in copies[1:]:
        copy.wait()
    for place, source in enumerate(places_in):
        for step, step_ids in enumerate((ids, next_ids)):
            step_ids[place : place + 1, : source.shape[1]] = source[step : step + 1, :]
    copies[0].wait()
    left_low[...] = wide[...].astype(BF16)


CHUNKS = ((0, 104), (104, 200), (200, 304), (304, 400))


def first_kernel(
    left, ids, slab_far, state_far, relation_far, slab_out, state_out, d_rel_out, table, slab, state, relation, sems
):
    copies = [
        pltpu.make_async_copy(slab_far, slab, sems.at[0]),
        pltpu.make_async_copy(state_far, state, sems.at[1]),
    ]
    for i, (start, stop) in enumerate(CHUNKS):
        rows = slice(start, stop)
        copies.append(pltpu.make_async_copy(relation_far.at[rows], relation.at[rows], sems.at[2 + i]))
    for copy in copies:
        copy.start()
    heads = dot(left[...], places(ids[0:1], ROWS))
    for copy in copies[:2]:
        copy.wait()
    pos_rows, neg_rows = target_rows_of(slab[...].astype(BF16), ids)
    for copy in copies[2:]:
        copy.wait()
    table[:, :RMAIN] = relation[:, :RMAIN].astype(BF16)
    table[:, RMAIN:] = jnp.zeros((D, RPAD - RMAIN), BF16)
    table[:, RMAIN:NREL] = relation[:, RMAIN:].astype(BF16)
    rel_rows = relation_rows_of(table[...], ids)
    prod, g_neg, d_pos, d_rel = edge_terms(heads, pos_rows, neg_rows, rel_rows)
    d_rel_out[:HALF], d_rel_out[HALF:] = d_rel
    slab_out[...], state_out[...] = trained(slab[...], state[...], ids[...], prod, g_neg, d_pos)


def between_kernel(slab, table, ids, ids_next, d_rel, pos_rows, neg_rows, rel_rows, rel_grad):
    pos_rows[...], neg_rows[...] = target_rows_of(slab[...].astype(BF16), ids_next)
    rel_rows[...] = relation_rows_of(table[...], ids_next)
    whole = dot(d_rel[...], places(ids[2:3], RPAD), ((1,), (1,)))
    for half in range(2):
        rel_grad[half] = whole[half * HALF : half * HALF + HALF]


def rel_half(half, ids, d_rel, rel_grad):
    return rel_grad[half] + dot(d_rel[half], places(ids[2:3], RPAD), ((1,), (1,)))


def second_kernel(
    core, left, ids, pos_rows, neg_rows, rel_rows, rel_grad, prod, g_neg, d_pos, d_rel, other
):
    heads = dot(left[...], places(ids[0:1], ROWS))
    prod[...], g_neg[...], d_pos[...], parts = edge_terms(
        heads, pos_rows[...], neg_rows[...], rel_rows[...]
    )
    for half in range(2):
        d_rel[half] = parts[half]
    other[...] = rel_half(1 - core[0], ids, d_rel, rel_grad)


def finish_kernel(
    core, slab, state, ids, rel_grad, prod, g_neg, d_pos, d_rel, mine, slab_out, state_out
):
    mine[...] = rel_half(core[0], ids, d_rel, rel_grad)
    slab_out[...], state_out[...] = trained(
        slab[...], state[...], ids[...], prod[...], g_neg[...], d_pos[...]
    )


def power_of(block):
    top = jnp.max(jnp.abs(block), axis=0, keepdims=True)
    return jnp.ceil(jnp.log2(jnp.maximum(top, 1e-30)))


def encode(main, last):
    lane = lax.broadcasted_iota(jnp.int32, last.shape, 1)
    row = lax.broadcasted_iota(jnp.int32, last.shape, 0)
    last = jnp.where(row < 7, last, 0.0)
    main_power, last_power = power_of(main), power_of(last)
    main = jnp.round(main * (LEVELS * jnp.exp2(-main_power)))
    last = jnp.round(last * (LEVELS * jnp.exp2(-last_power)))
    last_power = pltpu.roll(jnp.broadcast_to(last_power, last.shape), 64, 1)
    last = jnp.where(lane < 64, last, last_power)
    last = jnp.where(row == 7, jnp.broadcast_to(main_power, last.shape), last)
    fill = [jnp.zeros((CUT - main.shape[0], 128), F32)] if main.shape[0] < CUT else []
    return jnp.concatenate([main, *fill, last], 0).astype(jnp.int32).astype(jnp.int16)


def decode(codes):
    wide = codes.astype(jnp.int32).astype(F32)
    main, last = wide[:CUT], wide[CUT:]
    lane = lax.broadcasted_iota(jnp.int32, last.shape, 1)
    row = lax.broadcasted_iota(jnp.int32, last.shape, 0)
    main = main * (jnp.exp2(last[7:8]) * (1.0 / LEVELS))
    last_step = jnp.exp2(pltpu.roll(last, 64, 1)) * (1.0 / LEVELS)
    valid = jnp.logical_and(lane < NREL - RMAIN, row < 7)
    return main, jnp.where(valid, last * last_step, 0.0)


def place_of(part):
    tile, low = divmod(part, 2)
    rows = slice(CUT, HALF) if low else slice(0, CUT)
    return rows, slice(128 * tile, 128 * tile + 128)


def send_kernel(mine, theirs, codes, last):
    last[HALF:] = jnp.zeros((last.shape[0] - HALF, 128), F32)
    last[:HALF] = mine[:, RMAIN:] + theirs[:, RMAIN:]
    for part in range(OWNERS):
        at = place_of(part)
        codes[part] = encode(mine[at] + theirs[at], last[7 * part : 7 * part + 8])


def gather_kernel(parts, codes):
    main, last = decode(parts[0])
    for part in range(1, OWNERS):
        more = decode(parts[part])
        main, last = main + more[0], last + more[1]
    code = encode(main, last)
    for copy in range(codes.shape[0]):
        codes[copy] = code


def spread_kernel(parts, copies):
    main, last = decode(parts[0])
    for part in range(1, parts.shape[0]):
        more = decode(parts[part])
        main, last = main + more[0], last + more[1]
    code = encode(main, last)
    for copy in range(OWNERS):
        copies[copy] = code


def decoded_into(codes, grads, last):
    for part in range(OWNERS):
        rows, lanes = place_of(part)
        main, tail = decode(codes[part])
        grads[rows, lanes] = main[: rows.stop - rows.start]
        last[7 * part : 7 * part + 8] = tail
    grads[:, RMAIN:] = last[:HALF]
    return jnp.sum(grads[...] * grads[...], 0, keepdims=True)


def ours_kernel(codes, grads, squares, last):
    squares[...] = decoded_into(codes, grads, last)


def update_kernel(
    core, ours, squares, codes, relation, state, relation_out, state_out, theirs, last, wide, sems
):
    total = squares[...] + decoded_into(codes, theirs, last)
    new_state = state[...].reshape(1, NREL) + total[:, :NREL] * (1.0 / D)
    rate = 0.2 * lax.rsqrt(new_state)
    state_out[...] = new_state.reshape(NREL)
    starts = core[0] * HALF, (1 - core[0]) * HALF
    copies = []
    for place, (grad, start) in enumerate(zip((ours, theirs), starts)):
        rows = pl.ds(pl.multiple_of(start, 8), HALF)
        wide[rows] = relation[rows] - grad[:, :NREL] * rate
        copies.append(pltpu.make_async_copy(wide.at[rows], relation_out.at[rows], sems.at[place]))
        copies[place].start()
    for copy in copies:
        copy.wait()


def per_device(
    left_embed,
    right_embed,
    right_state,
    relation_embed,
    relation_state,
    source_rows,
    target_rows,
    relation_ids,
    negative_rows,
):
    core = lax.axis_index("core").astype(jnp.int32)[None]
    id_array = kept((8, EPAD), jnp.int32)
    index_arrays = [
        array[0, 0] for array in (source_rows, target_rows, relation_ids, negative_rows)
    ]
    dma = pltpu.SemaphoreType.DMA
    ids, ids_next, left_low = call(
        prepare_kernel,
        (id_array, id_array, kept((D, ROWS), BF16)),
        left_embed[0].T,
        *index_arrays,
        far_in=range(5),
        scratch=[
            pltpu.VMEM((D, ROWS), F32),
            [pltpu.VMEM(array.shape, jnp.int32) for array in index_arrays],
            dma((5,)),
        ],
        name="prepare",
    )
    ids_next = from_next(ids_next)
    left_next = from_next(left_low)
    relation = relation_embed.T
    slab_array, state_array = (D, ROWS), (1, ROWS)
    edge_array = kept((D, EPAD), BF16)
    half_array = kept((HALF, RPAD), F32)
    slab, state, d_rel, table = call(
        first_kernel,
        (kept(slab_array, F32), kept(state_array, F32), edge_array, kept((D, RPAD), BF16)),
        left_low,
        ids,
        right_embed[0].T,
        right_state,
        relation,
        far_in=(2, 3, 4),
        scratch=[
            pltpu.VMEM(slab_array, F32),
            pltpu.VMEM(state_array, F32),
            pltpu.VMEM((D, NREL), F32),
            dma((6,)),
        ],
        name="first",
    )
    wide_array = kept((D, EPAD), F32)
    pos_rows, neg_rows, rel_rows, rel_grad = call(
        between_kernel,
        (wide_array, kept((D, NPAD), BF16), wide_array, kept((2, HALF, RPAD), F32)),
        slab,
        table,
        ids,
        ids_next,
        d_rel,
        name="between",
    )
    prod, g_neg, d_pos, d_rel, other = call(
        second_kernel,
        (
            edge_array,
            kept((NPAD, EPAD), BF16),
            edge_array,
            kept((2, HALF, EPAD), BF16),
            half_array,
        ),
        left_next,
        ids_next,
        pos_rows,
        neg_rows,
        rel_rows,
        rel_grad,
        core=core,
        name="second",
    )
    theirs = swap_core(other)
    mine, slab_out, state_out = call(
        finish_kernel,
        (half_array, struct(slab_array, F32), struct(state_array, F32)),
        slab,
        state,
        ids_next,
        rel_grad,
        prod,
        g_neg,
        d_pos,
        d_rel,
        core=core,
        name="finish",
    )
    part = (PART, 128)
    last = pltpu.VMEM((232, 128), F32)
    parts = kept((OWNERS, *part), jnp.int16)
    sent = call(send_kernel, parts, mine, theirs, scratch=[last], name="send")
    got = lax.all_to_all(sent, CUBE, 0, 0, tiled=True)
    count = lax.axis_size("z_hi")
    codes = call(gather_kernel, kept((count, *part), jnp.int16), got, name="gather")
    codes = lax.all_to_all(codes, "z_hi", 0, 0, tiled=True)
    copies = call(spread_kernel, parts, codes, name="spread")
    ours = lax.all_to_all(copies, CUBE, 0, 0, tiled=True)
    theirs = swap_core(ours)
    grads, squares = call(
        ours_kernel, (half_array, kept((1, RPAD), F32)), ours, scratch=[last], name="ours"
    )
    relation_out, relation_state_out = call(
        update_kernel,
        (struct((D, NREL), F32), struct((NREL,), F32)),
        grads,
        squares,
        theirs,
        relation,
        relation_state,
        core=core,
        far_out=(0,),
        scratch=[
            pltpu.VMEM((HALF, RPAD), F32),
            last,
            pltpu.VMEM((D, NREL), F32),
            dma((2,)),
        ],
        name="update",
    )
    return (slab_out.T[None], state_out, relation_out.T, relation_state_out)


def solution(mesh):
    split = jax.sharding.Mesh(mesh.devices.reshape(4, 4, 2, 2, 2, 2), AXES)
    in_specs = (
        P(REPLICA, BUCKET, None),
        P(REPLICA, BUCKET, None),
        P(REPLICA, BUCKET),
        P(),
        P(),
        P(REPLICA, BUCKET, None, None),
        P(REPLICA, BUCKET, None, None),
        P(REPLICA, BUCKET, None, None),
        P(REPLICA, BUCKET, None, None),
    )
    out_specs = (P(REPLICA, BUCKET, None), P(REPLICA, BUCKET), P(), P())
    return jax.shard_map(
        per_device, mesh=split, in_specs=in_specs, out_specs=out_specs, check_vma=False
    )
```

```python
import jax
import jax.numpy as jnp
from jax import lax
from jax.experimental import pallas as pl
from jax.experimental.pallas import tpu as pltpu
from jax.sharding import PartitionSpec as P

AXES = ("x", "z", "y_lo", "y_hi", "core")
BUCKET = ("x", "z", "y_lo")
REPLICA = ("y_hi", "core")
PLANE = ("x", "y_lo", "y_hi")
OWNERS = 16
D = 400
HALF = 200
EPAD = 1024
NEG = 500
NPAD = 512
ROWS = 512
NREL = 2066
RMAIN = 2048
RPAD = 2176
SHARE = 13
TAIL = 24
PART = HALF + TAIL
LEVELS = 32000.0
F32 = jnp.float32
BF16 = jnp.bfloat16


def struct(shape, dtype):
    return jax.ShapeDtypeStruct(shape, dtype)


def kept(shape, dtype):
    return pltpu.VMEM(shape, dtype)


def near(array):
    return pltpu.with_memory_space_constraint(array, pltpu.VMEM)


def away(array):
    return pltpu.with_memory_space_constraint(array, pltpu.HBM)


def call(kernel, out_shape, *args, core=None, scratch=(), far_in=(), far_out=(), name, limit=32):
    vmem = pl.BlockSpec(memory_space=pltpu.VMEM)
    far = pl.BlockSpec(memory_space=pltpu.HBM)
    several = isinstance(out_shape, tuple)
    outs = out_shape if several else (out_shape,)
    specs = tuple(far if i in far_out else vmem for i in range(len(outs)))
    in_specs = [far if i in far_in else vmem for i in range(len(args))]
    args = [away(arg) if i in far_in else near(arg) for i, arg in enumerate(args)]
    if core is not None:
        in_specs, args = [pl.BlockSpec(memory_space=pltpu.SMEM)] + in_specs, [core] + args
    return pl.pallas_call(
        kernel,
        out_shape=out_shape,
        in_specs=in_specs,
        out_specs=specs if several else specs[0],
        scratch_shapes=scratch,
        compiler_params=pltpu.CompilerParams(vmem_limit_bytes=limit * 1024 * 1024),
        name=name,
    )(*args)


def from_next(block):
    count = lax.axis_size(BUCKET)
    return lax.ppermute(block, BUCKET, [((i + 1) % count, i) for i in range(count)])


def swap_core(block):
    return lax.ppermute(block, "core", [(0, 1), (1, 0)])


def dot(a, b, dims=((1,), (0,))):
    return lax.dot_general(a, b, (dims, ((), ())), preferred_element_type=F32)


def places(row, count):
    at = lax.broadcasted_iota(jnp.int32, (count, row.shape[1]), 0).astype(jnp.int16)
    return jnp.where(at == row.astype(jnp.int16), BF16(1), BF16(0))


def target_rows_of(slab_low, ids):
    pos_rows = dot(slab_low, places(ids[1:2], ROWS))
    return pos_rows, dot(slab_low, places(ids[3:4, :NPAD], ROWS)).astype(BF16)


def relation_rows_of(table, ids):
    return dot(table, places(ids[2:3], RPAD))


def edge_terms(heads, pos_rows, neg_rows, rel_rows):
    h_re, h_im = heads[:HALF], heads[HALF:]
    r_re, r_im = rel_rows[:HALF], rel_rows[HALF:]
    prod = jnp.concatenate([h_re * r_re - h_im * r_im, h_re * r_im + h_im * r_re], 0).astype(BF16)
    prod_wide = prod.astype(F32)
    pos = jnp.sum(prod_wide * pos_rows, 0, keepdims=True)
    g_pos = -jax.nn.sigmoid(-pos)
    g_neg = (jax.nn.sigmoid(dot(neg_rows, prod, ((0,), (0,)))) * (1.0 / NEG)).astype(BF16)
    d_pos = (g_pos * prod_wide).astype(BF16)
    d_prod = g_pos * pos_rows + dot(neg_rows, g_neg)
    p_re, p_im = d_prod[:HALF], d_prod[HALF:]
    d_rel = (p_re * h_re + p_im * h_im, p_im * h_re - p_re * h_im)
    return prod, g_neg, d_pos, d_rel


def trained(slab, state, ids, prod, g_neg, d_pos):
    along = ((1,), (1,))
    d_neg = dot(prod, g_neg, along).astype(BF16)
    grad = dot(d_pos, places(ids[1:2], ROWS), along)
    grad = grad + dot(d_neg, places(ids[3:4, :NPAD], ROWS), along)
    state = state + jnp.sum(grad * grad, 0, keepdims=True) * (1.0 / D)
    return slab - grad * (0.1 * lax.rsqrt(state)), state


def prepare_kernel(left, src, dst, rel, neg, ids, message, wide, next_ids, places_in, sems):
    sources = (src, dst, rel, neg)
    copies = [pltpu.make_async_copy(left, wide, sems.at[4])]
    copies += [pltpu.make_async_copy(r, places_in[i], sems.at[i]) for i, r in enumerate(sources)]
    for copy in copies:
        copy.start()
    for step_ids in (ids, next_ids):
        step_ids[...] = jnp.full(step_ids.shape, -1, jnp.int32)
    for copy in copies[1:]:
        copy.wait()
    for place, source in enumerate(places_in):
        for step, step_ids in enumerate((ids, next_ids)):
            step_ids[place : place + 1, : source.shape[1]] = source[step : step + 1, :]
    high, low = (next_ids[...] >> 6).astype(F32), (next_ids[...] & 63).astype(F32)
    halves = slice(0, ROWS), slice(ROWS, EPAD)
    packed = [part[:4, half] for part in (high, low) for half in halves]
    message[D:] = jnp.concatenate(packed, 0).astype(BF16)
    copies[0].wait()
    message[:D] = wide[...].astype(BF16)


def unpacked_ids(message):
    coded = message[D:].astype(F32)
    halves = (coded[4 * i : 4 * i + 4] * 64.0 + coded[8 + 4 * i : 12 + 4 * i] for i in range(2))
    rows = jnp.concatenate(list(halves), 1).astype(jnp.int32)
    return jnp.concatenate([rows, rows], 0)


CHUNKS = ((0, 104), (104, 200), (200, 304), (304, 400))


def first_kernel(
    left, ids, slab_far, state_far, relation_far, slab_out, state_out, rel_grad, table, slab, state, relation, sems
):
    copies = [
        pltpu.make_async_copy(slab_far, slab, sems.at[0]),
        pltpu.make_async_copy(state_far, state, sems.at[1]),
    ]
    for i, (start, stop) in enumerate(CHUNKS):
        rows = slice(start, stop)
        copies.append(pltpu.make_async_copy(relation_far.at[rows], relation.at[rows], sems.at[2 + i]))
    for copy in copies:
        copy.start()
    heads = dot(left[:D], places(ids[0:1], ROWS))
    for copy in copies[:2]:
        copy.wait()
    pos_rows, neg_rows = target_rows_of(slab[...].astype(BF16), ids)
    for copy in copies[2:]:
        copy.wait()
    table[:, :RMAIN] = relation[:, :RMAIN].astype(BF16)
    table[:, RMAIN:] = jnp.zeros((D, RPAD - RMAIN), BF16)
    table[:, RMAIN:NREL] = relation[:, RMAIN:].astype(BF16)
    rel_rows = relation_rows_of(table[...], ids)
    prod, g_neg, d_pos, d_rel = edge_terms(heads, pos_rows, neg_rows, rel_rows)
    slab_out[...], state_out[...] = trained(slab[...], state[...], ids[...], prod, g_neg, d_pos)
    whole = dot(jnp.concatenate(d_rel, 0).astype(BF16), places(ids[2:3], RPAD), ((1,), (1,)))
    for half in range(2):
        rel_grad[half] = whole[half * HALF : half * HALF + HALF]


def rel_half(half, ids, d_rel, rel_grad):
    return rel_grad[half] + dot(d_rel[half], places(ids[2:3], RPAD), ((1,), (1,)))


def second_kernel(
    core, message, slab, table, rel_grad, ids, prod, g_neg, d_pos, d_rel, other
):
    ids[...] = unpacked_ids(message[...])
    heads = dot(message[:D], places(ids[0:1], ROWS))
    rel_rows = relation_rows_of(table[...], ids)
    pos_rows, neg_rows = target_rows_of(slab[...].astype(BF16), ids)
    prod[...], g_neg[...], d_pos[...], parts = edge_terms(heads, pos_rows, neg_rows, rel_rows)
    for half in range(2):
        d_rel[half] = parts[half].astype(BF16)
    other[...] = rel_half(1 - core[0], ids, d_rel, rel_grad)


def finish_kernel(
    core, slab, state, ids, rel_grad, prod, g_neg, d_pos, d_rel, mine, slab_out, state_out
):
    mine[...] = rel_half(core[0], ids, d_rel, rel_grad)
    slab_out[...], state_out[...] = trained(
        slab[...], state[...], ids[...], prod[...], g_neg[...], d_pos[...]
    )


def power_of(block):
    top = jnp.max(jnp.abs(block), axis=0, keepdims=True)
    return jnp.ceil(jnp.log2(jnp.maximum(top, 1e-30)))


def encode(main, last):
    lane = lax.broadcasted_iota(jnp.int32, last.shape, 1)
    row = lax.broadcasted_iota(jnp.int32, last.shape, 0)
    last = jnp.where(row < SHARE, last, 0.0)
    main_power, last_power = power_of(main), power_of(last)
    main = jnp.round(main * (LEVELS * jnp.exp2(-main_power)))
    last = jnp.round(last * (LEVELS * jnp.exp2(-last_power)))
    last_power = pltpu.roll(jnp.broadcast_to(last_power, last.shape), 64, 1)
    last = jnp.where(lane < 64, last, last_power)
    last = jnp.where(row == TAIL - 1, jnp.broadcast_to(main_power, last.shape), last)
    return jnp.concatenate([main, last], 0).astype(jnp.int32).astype(jnp.int16)


def decode(codes):
    wide = codes.astype(jnp.int32).astype(F32)
    main, last = wide[:HALF], wide[HALF:]
    lane = lax.broadcasted_iota(jnp.int32, last.shape, 1)
    row = lax.broadcasted_iota(jnp.int32, last.shape, 0)
    main = main * (jnp.exp2(last[TAIL - 1 :]) * (1.0 / LEVELS))
    last_step = jnp.exp2(pltpu.roll(last, 64, 1)) * (1.0 / LEVELS)
    valid = jnp.logical_and(lane < NREL - RMAIN, row < SHARE)
    return main, jnp.where(valid, last * last_step, 0.0)


def send_kernel(mine, theirs, codes, last):
    last[HALF:] = jnp.zeros((last.shape[0] - HALF, 128), F32)
    last[:HALF] = mine[:, RMAIN:] + theirs[:, RMAIN:]
    for part in range(OWNERS):
        at = slice(None), slice(128 * part, 128 * part + 128)
        codes[part] = encode(mine[at] + theirs[at], last[SHARE * part : SHARE * part + TAIL])


def gather_kernel(parts, codes):
    main, last = decode(parts[0])
    for part in range(1, OWNERS):
        more = decode(parts[part])
        main, last = main + more[0], last + more[1]
    code = encode(main, last)
    for copy in range(codes.shape[0]):
        codes[copy] = code


def spread_kernel(parts, copies):
    main, last = decode(parts[0])
    for part in range(1, parts.shape[0]):
        more = decode(parts[part])
        main, last = main + more[0], last + more[1]
    code = encode(main, last)
    for copy in range(OWNERS):
        copies[copy] = code


def decoded_into(codes, grads, last):
    for part in range(OWNERS):
        main, tail = decode(codes[part])
        grads[:, 128 * part : 128 * part + 128] = main
        last[SHARE * part : SHARE * part + TAIL] = tail
    grads[:, RMAIN:] = last[:HALF]
    return jnp.sum(grads[...] * grads[...], 0, keepdims=True)


def ours_kernel(codes, grads, squares, last):
    squares[...] = decoded_into(codes, grads, last)


def update_kernel(
    core, ours, squares, codes, relation, state, relation_out, state_out, theirs, last, wide, sems
):
    total = squares[...] + decoded_into(codes, theirs, last)
    new_state = state[...].reshape(1, NREL) + total[:, :NREL] * (1.0 / D)
    rate = 0.2 * lax.rsqrt(new_state)
    state_out[...] = new_state.reshape(NREL)
    starts = core[0] * HALF, (1 - core[0]) * HALF
    copies = []
    for place, (grad, start) in enumerate(zip((ours, theirs), starts)):
        rows = pl.ds(pl.multiple_of(start, 8), HALF)
        wide[rows] = relation[rows] - grad[:, :NREL] * rate
        copies.append(pltpu.make_async_copy(wide.at[rows], relation_out.at[rows], sems.at[place]))
        copies[place].start()
    for copy in copies:
        copy.wait()


def per_device(
    left_embed,
    right_embed,
    right_state,
    relation_embed,
    relation_state,
    source_rows,
    target_rows,
    relation_ids,
    negative_rows,
):
    core = lax.axis_index("core").astype(jnp.int32)[None]
    id_array = kept((8, EPAD), jnp.int32)
    index_arrays = [
        array[0, 0] for array in (source_rows, target_rows, relation_ids, negative_rows)
    ]
    dma = pltpu.SemaphoreType.DMA
    ids, message = call(
        prepare_kernel,
        (id_array, kept((D + 16, ROWS), BF16)),
        left_embed[0].T,
        *index_arrays,
        far_in=range(5),
        scratch=[
            pltpu.VMEM((D, ROWS), F32),
            id_array,
            [pltpu.VMEM(array.shape, jnp.int32) for array in index_arrays],
            dma((5,)),
        ],
        name="prepare",
    )
    message_next = from_next(message)
    relation = relation_embed.T
    slab_array, state_array = (D, ROWS), (1, ROWS)
    edge_array = kept((D, EPAD), BF16)
    half_array = kept((HALF, RPAD), F32)
    slab, state, rel_grad, table = call(
        first_kernel,
        (
            kept(slab_array, F32),
            kept(state_array, F32),
            kept((2, HALF, RPAD), F32),
            kept((D, RPAD), BF16),
        ),
        message,
        ids,
        right_embed[0].T,
        right_state,
        relation,
        far_in=(2, 3, 4),
        scratch=[
            pltpu.VMEM(slab_array, F32),
            pltpu.VMEM(state_array, F32),
            pltpu.VMEM((D, NREL), F32),
            dma((6,)),
        ],
        name="first",
    )
    ids_next, prod, g_neg, d_pos, d_rel, other = call(
        second_kernel,
        (
            id_array,
            edge_array,
            kept((NPAD, EPAD), BF16),
            edge_array,
            kept((2, HALF, EPAD), BF16),
            half_array,
        ),
        message_next,
        slab,
        table,
        rel_grad,
        core=core,
        name="second",
    )
    theirs = swap_core(other)
    mine, slab_out, state_out = call(
        finish_kernel,
        (half_array, struct(slab_array, F32), struct(state_array, F32)),
        slab,
        state,
        ids_next,
        rel_grad,
        prod,
        g_neg,
        d_pos,
        d_rel,
        core=core,
        name="finish",
    )
    part = (PART, 128)
    last = pltpu.VMEM((232, 128), F32)
    parts = kept((OWNERS, *part), jnp.int16)
    sent = call(send_kernel, parts, mine, theirs, scratch=[last], name="send")
    got = lax.all_to_all(sent, PLANE, 0, 0, tiled=True)
    count = lax.axis_size("z")
    codes = call(gather_kernel, kept((count, *part), jnp.int16), got, name="gather")
    codes = lax.all_to_all(codes, "z", 0, 0, tiled=True)
    copies = call(spread_kernel, parts, codes, name="spread")
    ours = lax.all_to_all(copies, PLANE, 0, 0, tiled=True)
    theirs = swap_core(ours)
    grads, squares = call(
        ours_kernel, (half_array, kept((1, RPAD), F32)), ours, scratch=[last], name="ours"
    )
    relation_out, relation_state_out = call(
        update_kernel,
        (struct((D, NREL), F32), struct((NREL,), F32)),
        grads,
        squares,
        theirs,
        relation,
        relation_state,
        core=core,
        far_out=(0,),
        scratch=[
            pltpu.VMEM((HALF, RPAD), F32),
            last,
            pltpu.VMEM((D, NREL), F32),
            dma((2,)),
        ],
        name="update",
    )
    return (slab_out.T[None], state_out, relation_out.T, relation_state_out)


def solution(mesh):
    split = jax.sharding.Mesh(mesh.devices.reshape(4, 8, 2, 2, 2), AXES)
    in_specs = (
        P(REPLICA, BUCKET, None),
        P(REPLICA, BUCKET, None),
        P(REPLICA, BUCKET),
        P(),
        P(),
        P(REPLICA, BUCKET, None, None),
        P(REPLICA, BUCKET, None, None),
        P(REPLICA, BUCKET, None, None),
        P(REPLICA, BUCKET, None, None),
    )
    out_specs = (P(REPLICA, BUCKET, None), P(REPLICA, BUCKET), P(), P())
    return jax.shard_map(
        per_device, mesh=split, in_specs=in_specs, out_specs=out_specs, check_vma=False
    )
```

```python
import jax
import jax.numpy as jnp
from jax import lax
from jax.experimental import pallas as pl
from jax.experimental.pallas import tpu as pltpu
from jax.sharding import PartitionSpec as P

AXES = ("x", "z_hi", "z_lo", "y_lo", "y_hi", "core")
BUCKET = ("x", "z_hi", "z_lo", "y_lo")
REPLICA = ("y_hi", "core")
CUBE = ("x", "z_lo", "y_lo", "y_hi")
OWNERS = 32
D = 400
HALF = 200
EPAD = 1024
NEG = 500
NPAD = 512
ROWS = 512
NREL = 2066
RMAIN = 2048
RPAD = 2176
CUT = 104
PART = 112
LEVELS = 32000.0
F32 = jnp.float32
BF16 = jnp.bfloat16


def struct(shape, dtype):
    return jax.ShapeDtypeStruct(shape, dtype)


def kept(shape, dtype):
    return pltpu.VMEM(shape, dtype)


def near(array):
    return pltpu.with_memory_space_constraint(array, pltpu.VMEM)


def away(array):
    return pltpu.with_memory_space_constraint(array, pltpu.HBM)


def call(kernel, out_shape, *args, core=None, scratch=(), far_in=(), far_out=(), name, flops=None):
    vmem = pl.BlockSpec(memory_space=pltpu.VMEM)
    far = pl.BlockSpec(memory_space=pltpu.HBM)
    several = isinstance(out_shape, tuple)
    outs = out_shape if several else (out_shape,)
    specs = tuple(far if i in far_out else vmem for i in range(len(outs)))
    in_specs = [far if i in far_in else vmem for i in range(len(args))]
    args = [away(arg) if i in far_in else near(arg) for i, arg in enumerate(args)]
    if core is not None:
        in_specs, args = [pl.BlockSpec(memory_space=pltpu.SMEM)] + in_specs, [core] + args
    return pl.pallas_call(
        kernel,
        out_shape=out_shape,
        in_specs=in_specs,
        out_specs=specs if several else specs[0],
        scratch_shapes=scratch,
        compiler_params=pltpu.CompilerParams(vmem_limit_bytes=32 * 1024 * 1024),
        cost_estimate=flops and pl.CostEstimate(flops=flops, bytes_accessed=0, transcendentals=0),
        name=name,
    )(*args)


def from_next(block):
    count = lax.axis_size(BUCKET)
    return lax.ppermute(block, BUCKET, [((i + 1) % count, i) for i in range(count)])


def swap_core(block):
    return lax.ppermute(block, "core", [(0, 1), (1, 0)])


def dot(a, b, dims=((1,), (0,))):
    return lax.dot_general(a, b, (dims, ((), ())), preferred_element_type=F32)


def places(row, count):
    at = lax.broadcasted_iota(jnp.int32, (count, row.shape[1]), 0).astype(jnp.int16)
    return jnp.where(at == row.astype(jnp.int16), BF16(1), BF16(0))


def target_rows_of(slab_low, ids):
    pos_rows = dot(slab_low, places(ids[1:2], ROWS))
    return pos_rows, dot(slab_low, places(ids[3:4, :NPAD], ROWS)).astype(BF16)


def relation_rows_of(table, ids):
    return dot(table, places(ids[2:3], RPAD))


def edge_terms(heads, pos_rows, neg_rows, rel_rows):
    h_re, h_im = heads[:HALF], heads[HALF:]
    r_re, r_im = rel_rows[:HALF], rel_rows[HALF:]
    prod = jnp.concatenate([h_re * r_re - h_im * r_im, h_re * r_im + h_im * r_re], 0).astype(BF16)
    prod_wide = prod.astype(F32)
    pos = jnp.sum(prod_wide * pos_rows, 0, keepdims=True)
    g_pos = -jax.nn.sigmoid(-pos)
    g_neg = (jax.nn.sigmoid(dot(neg_rows, prod, ((0,), (0,)))) * (1.0 / NEG)).astype(BF16)
    d_pos = (g_pos * prod_wide).astype(BF16)
    d_prod = g_pos * pos_rows + dot(neg_rows, g_neg)
    p_re, p_im = d_prod[:HALF], d_prod[HALF:]
    d_rel = (p_re * h_re + p_im * h_im, p_im * h_re - p_re * h_im)
    return prod, g_neg, d_pos, [part.astype(BF16) for part in d_rel]


def trained(slab, state, ids, prod, g_neg, d_pos):
    along = ((1,), (1,))
    d_neg = dot(prod, g_neg, along).astype(BF16)
    grad = dot(d_pos, places(ids[1:2], ROWS), along)
    grad = grad + dot(d_neg, places(ids[3:4, :NPAD], ROWS), along)
    state = state + jnp.sum(grad * grad, 0, keepdims=True) * (1.0 / D)
    return slab - grad * (0.1 * lax.rsqrt(state)), state


def prepare_kernel(left, src, dst, rel, neg, ids, next_ids, left_low, wide, places_in, sems):
    sources = (src, dst, rel, neg)
    copies = [pltpu.make_async_copy(left, wide, sems.at[4])]
    copies += [pltpu.make_async_copy(r, places_in[i], sems.at[i]) for i, r in enumerate(sources)]
    for copy in copies:
        copy.start()
    for step_ids in (ids, next_ids):
        step_ids[...] = jnp.full(step_ids.shape, -1, jnp.int32)
    for copy in copies[1:]:
        copy.wait()
    for place, source in enumerate(places_in):
        for step, step_ids in enumerate((ids, next_ids)):
            step_ids[place : place + 1, : source.shape[1]] = source[step : step + 1, :]
    copies[0].wait()
    left_low[...] = wide[...].astype(BF16)


CHUNKS = ((0, 104), (104, 200), (200, 304), (304, 400))


def first_kernel(
    left, ids, slab_far, state_far, relation_far, slab_out, state_out, d_rel_out, table, slab, state, relation, sems
):
    copies = [
        pltpu.make_async_copy(slab_far, slab, sems.at[0]),
        pltpu.make_async_copy(state_far, state, sems.at[1]),
    ]
    for i, (start, stop) in enumerate(CHUNKS):
        rows = slice(start, stop)
        copies.append(pltpu.make_async_copy(relation_far.at[rows], relation.at[rows], sems.at[2 + i]))
    for copy in copies:
        copy.start()
    heads = dot(left[...], places(ids[0:1], ROWS))
    for copy in copies[:2]:
        copy.wait()
    pos_rows, neg_rows = target_rows_of(slab[...].astype(BF16), ids)
    for copy in copies[2:]:
        copy.wait()
    table[:, :RMAIN] = relation[:, :RMAIN].astype(BF16)
    table[:, RMAIN:] = jnp.zeros((D, RPAD - RMAIN), BF16)
    table[:, RMAIN:NREL] = relation[:, RMAIN:].astype(BF16)
    rel_rows = relation_rows_of(table[...], ids)
    prod, g_neg, d_pos, d_rel = edge_terms(heads, pos_rows, neg_rows, rel_rows)
    d_rel_out[:HALF], d_rel_out[HALF:] = d_rel
    slab_out[...], state_out[...] = trained(slab[...], state[...], ids[...], prod, g_neg, d_pos)


def between_kernel(slab, table, ids, ids_next, d_rel, pos_rows, neg_rows, rel_rows, rel_grad):
    pos_rows[...], neg_rows[...] = target_rows_of(slab[...].astype(BF16), ids_next)
    rel_rows[...] = relation_rows_of(table[...], ids_next)
    whole = dot(d_rel[...], places(ids[2:3], RPAD), ((1,), (1,)))
    for half in range(2):
        rel_grad[half] = whole[half * HALF : half * HALF + HALF]


def rel_half(half, ids, d_rel, rel_grad):
    return rel_grad[half] + dot(d_rel[half], places(ids[2:3], RPAD), ((1,), (1,)))


def second_kernel(
    core, left, ids, pos_rows, neg_rows, rel_rows, rel_grad, prod, g_neg, d_pos, d_rel, other
):
    heads = dot(left[...], places(ids[0:1], ROWS))
    prod[...], g_neg[...], d_pos[...], parts = edge_terms(
        heads, pos_rows[...], neg_rows[...], rel_rows[...]
    )
    for half in range(2):
        d_rel[half] = parts[half]
    other[...] = rel_half(1 - core[0], ids, d_rel, rel_grad)


def finish_kernel(
    core, slab, state, ids, rel_grad, prod, g_neg, d_pos, d_rel, mine, slab_out, state_out
):
    mine[...] = rel_half(core[0], ids, d_rel, rel_grad)
    slab_out[...], state_out[...] = trained(
        slab[...], state[...], ids[...], prod[...], g_neg[...], d_pos[...]
    )


def power_of(block):
    top = jnp.max(jnp.abs(block), axis=0, keepdims=True)
    return jnp.ceil(jnp.log2(jnp.maximum(top, 1e-30)))


def encode(main, last):
    lane = lax.broadcasted_iota(jnp.int32, last.shape, 1)
    row = lax.broadcasted_iota(jnp.int32, last.shape, 0)
    last = jnp.where(row < 7, last, 0.0)
    main_power, last_power = power_of(main), power_of(last)
    main = jnp.round(main * (LEVELS * jnp.exp2(-main_power)))
    last = jnp.round(last * (LEVELS * jnp.exp2(-last_power)))
    last_power = pltpu.roll(jnp.broadcast_to(last_power, last.shape), 64, 1)
    last = jnp.where(lane < 64, last, last_power)
    last = jnp.where(row == 7, jnp.broadcast_to(main_power, last.shape), last)
    fill = [jnp.zeros((CUT - main.shape[0], 128), F32)] if main.shape[0] < CUT else []
    return jnp.concatenate([main, *fill, last], 0).astype(jnp.int32).astype(jnp.int16)


def decode(codes):
    wide = codes.astype(jnp.int32).astype(F32)
    main, last = wide[:CUT], wide[CUT:]
    lane = lax.broadcasted_iota(jnp.int32, last.shape, 1)
    row = lax.broadcasted_iota(jnp.int32, last.shape, 0)
    main = main * (jnp.exp2(last[7:8]) * (1.0 / LEVELS))
    last_step = jnp.exp2(pltpu.roll(last, 64, 1)) * (1.0 / LEVELS)
    valid = jnp.logical_and(lane < NREL - RMAIN, row < 7)
    return main, jnp.where(valid, last * last_step, 0.0)


def place_of(part):
    tile, low = divmod(part, 2)
    rows = slice(CUT, HALF) if low else slice(0, CUT)
    return rows, slice(128 * tile, 128 * tile + 128)


def send_kernel(mine, theirs, codes, last):
    last[HALF:] = jnp.zeros((last.shape[0] - HALF, 128), F32)
    last[:HALF] = mine[:, RMAIN:] + theirs[:, RMAIN:]
    for part in range(OWNERS):
        at = place_of(part)
        codes[part] = encode(mine[at] + theirs[at], last[7 * part : 7 * part + 8])


def gather_kernel(parts, codes):
    main, last = decode(parts[0])
    for part in range(1, OWNERS):
        more = decode(parts[part])
        main, last = main + more[0], last + more[1]
    code = encode(main, last)
    for copy in range(codes.shape[0]):
        codes[copy] = code


def spread_kernel(parts, copies):
    main, last = decode(parts[0])
    for part in range(1, parts.shape[0]):
        more = decode(parts[part])
        main, last = main + more[0], last + more[1]
    code = encode(main, last)
    for copy in range(OWNERS):
        copies[copy] = code


def decoded_into(codes, grads, last):
    for part in range(OWNERS):
        rows, lanes = place_of(part)
        main, tail = decode(codes[part])
        grads[rows, lanes] = main[: rows.stop - rows.start]
        last[7 * part : 7 * part + 8] = tail
    grads[:, RMAIN:] = last[:HALF]
    return jnp.sum(grads[...] * grads[...], 0, keepdims=True)


def ours_kernel(codes, grads, squares, last):
    squares[...] = decoded_into(codes, grads, last)


def update_kernel(
    core, ours, squares, codes, relation, state, relation_out, state_out, theirs, last, wide, sems
):
    total = squares[...] + decoded_into(codes, theirs, last)
    new_state = state[...].reshape(1, NREL) + total[:, :NREL] * (1.0 / D)
    rate = 0.2 * lax.rsqrt(new_state)
    state_out[...] = new_state.reshape(NREL)
    copies = []
    for grad, half in ((ours, core[0]), (theirs, 1 - core[0])):
        for start, stop in ((0, 56), (56, 104), (104, 152), (152, 200)):
            rows = pl.ds(pl.multiple_of(half * HALF + start, 8), stop - start)
            wide[rows] = relation[rows] - grad[start:stop, :NREL] * rate
            copies.append(
                pltpu.make_async_copy(wide.at[rows], relation_out.at[rows], sems.at[len(copies)])
            )
            copies[-1].start()
    for copy in copies:
        copy.wait()


def per_device(
    left_embed,
    right_embed,
    right_state,
    relation_embed,
    relation_state,
    source_rows,
    target_rows,
    relation_ids,
    negative_rows,
):
    core = lax.axis_index("core").astype(jnp.int32)[None]
    id_array = kept((8, EPAD), jnp.int32)
    index_arrays = [
        array[0, 0] for array in (source_rows, target_rows, relation_ids, negative_rows)
    ]
    dma = pltpu.SemaphoreType.DMA
    ids, ids_next, left_low = call(
        prepare_kernel,
        (id_array, id_array, kept((D, ROWS), BF16)),
        left_embed[0].T,
        *index_arrays,
        far_in=range(5),
        scratch=[
            pltpu.VMEM((D, ROWS), F32),
            [pltpu.VMEM(array.shape, jnp.int32) for array in index_arrays],
            dma((5,)),
        ],
        name="prepare",
    )
    ids_next = from_next(ids_next)
    left_next = from_next(left_low)
    relation = relation_embed.T
    slab_array, state_array = (D, ROWS), (1, ROWS)
    edge_array = kept((D, EPAD), BF16)
    half_array = kept((HALF, RPAD), F32)
    slab, state, d_rel, table = call(
        first_kernel,
        (kept(slab_array, F32), kept(state_array, F32), edge_array, kept((D, RPAD), BF16)),
        left_low,
        ids,
        right_embed[0].T,
        right_state,
        relation,
        far_in=(2, 3, 4),
        scratch=[
            pltpu.VMEM(slab_array, F32),
            pltpu.VMEM(state_array, F32),
            pltpu.VMEM((D, NREL), F32),
            dma((6,)),
        ],
        flops=1000,
        name="first",
    )
    wide_array = kept((D, EPAD), F32)
    pos_rows, neg_rows, rel_rows, rel_grad = call(
        between_kernel,
        (wide_array, kept((D, NPAD), BF16), wide_array, kept((2, HALF, RPAD), F32)),
        slab,
        table,
        ids,
        ids_next,
        d_rel,
        flops=2 * 10**10,
        name="between",
    )
    prod, g_neg, d_pos, d_rel, other = call(
        second_kernel,
        (
            edge_array,
            kept((NPAD, EPAD), BF16),
            edge_array,
            kept((2, HALF, EPAD), BF16),
            half_array,
        ),
        left_next,
        ids_next,
        pos_rows,
        neg_rows,
        rel_rows,
        rel_grad,
        core=core,
        name="second",
    )
    theirs = swap_core(other)
    mine, slab_out, state_out = call(
        finish_kernel,
        (half_array, struct(slab_array, F32), struct(state_array, F32)),
        slab,
        state,
        ids_next,
        rel_grad,
        prod,
        g_neg,
        d_pos,
        d_rel,
        core=core,
        name="finish",
    )
    part = (PART, 128)
    last = pltpu.VMEM((232, 128), F32)
    parts = kept((OWNERS, *part), jnp.int16)
    sent = call(send_kernel, parts, mine, theirs, scratch=[last], name="send")
    got = lax.all_to_all(sent, CUBE, 0, 0, tiled=True)
    count = lax.axis_size("z_hi")
    codes = call(gather_kernel, kept((count, *part), jnp.int16), got, name="gather")
    codes = lax.all_to_all(codes, "z_hi", 0, 0, tiled=True)
    copies = call(spread_kernel, parts, codes, name="spread")
    ours = lax.all_to_all(copies, CUBE, 0, 0, tiled=True)
    theirs = swap_core(ours)
    grads, squares = call(
        ours_kernel, (half_array, kept((1, RPAD), F32)), ours, scratch=[last], name="ours"
    )
    relation_out, relation_state_out = call(
        update_kernel,
        (struct((D, NREL), F32), struct((NREL,), F32)),
        grads,
        squares,
        theirs,
        relation,
        relation_state,
        core=core,
        far_out=(0,),
        scratch=[
            pltpu.VMEM((HALF, RPAD), F32),
            last,
            pltpu.VMEM((D, NREL), F32),
            dma((8,)),
        ],
        name="update",
    )
    return (slab_out.T[None], state_out, relation_out.T, relation_state_out)


def solution(mesh):
    split = jax.sharding.Mesh(mesh.devices.reshape(4, 4, 2, 2, 2, 2), AXES)
    in_specs = (
        P(REPLICA, BUCKET, None),
        P(REPLICA, BUCKET, None),
        P(REPLICA, BUCKET),
        P(),
        P(),
        P(REPLICA, BUCKET, None, None),
        P(REPLICA, BUCKET, None, None),
        P(REPLICA, BUCKET, None, None),
        P(REPLICA, BUCKET, None, None),
    )
    out_specs = (P(REPLICA, BUCKET, None), P(REPLICA, BUCKET), P(), P())
    return jax.shard_map(
        per_device, mesh=split, in_specs=in_specs, out_specs=out_specs, check_vma=False
    )
```

```python
import jax
import jax.numpy as jnp
from jax import lax
from jax.experimental import pallas as pl
from jax.experimental.pallas import tpu as pltpu
from jax.sharding import PartitionSpec as P

AXES = ("x", "z_hi", "z_lo", "y_lo", "y_hi", "core")
BUCKET = ("x", "z_hi", "z_lo", "y_lo")
REPLICA = ("y_hi", "core")
CUBE = ("x", "z_lo", "y_lo", "y_hi")
OWNERS = 32
D = 400
HALF = 200
EPAD = 1024
NEG = 500
NPAD = 512
ROWS = 512
NREL = 2066
RMAIN = 2048
RPAD = 2176
CUT = 104
PART = 112
LEVELS = 32000.0
F32 = jnp.float32
BF16 = jnp.bfloat16


def struct(shape, dtype):
    return jax.ShapeDtypeStruct(shape, dtype)


def kept(shape, dtype):
    return pltpu.VMEM(shape, dtype)


def near(array):
    return pltpu.with_memory_space_constraint(array, pltpu.VMEM)


def away(array):
    return pltpu.with_memory_space_constraint(array, pltpu.HBM)


def call(kernel, out_shape, *args, core=None, scratch=(), far_in=(), far_out=(), name, flops=None):
    vmem = pl.BlockSpec(memory_space=pltpu.VMEM)
    far = pl.BlockSpec(memory_space=pltpu.HBM)
    several = isinstance(out_shape, tuple)
    outs = out_shape if several else (out_shape,)
    specs = tuple(far if i in far_out else vmem for i in range(len(outs)))
    in_specs = [far if i in far_in else vmem for i in range(len(args))]
    args = [away(arg) if i in far_in else near(arg) for i, arg in enumerate(args)]
    if core is not None:
        in_specs, args = [pl.BlockSpec(memory_space=pltpu.SMEM)] + in_specs, [core] + args
    return pl.pallas_call(
        kernel,
        out_shape=out_shape,
        in_specs=in_specs,
        out_specs=specs if several else specs[0],
        scratch_shapes=scratch,
        compiler_params=pltpu.CompilerParams(vmem_limit_bytes=32 * 1024 * 1024),
        cost_estimate=flops and pl.CostEstimate(flops=flops, bytes_accessed=0, transcendentals=0),
        name=name,
    )(*args)


def from_next(block):
    count = lax.axis_size(BUCKET)
    return lax.ppermute(block, BUCKET, [((i + 1) % count, i) for i in range(count)])


def swap_core(block):
    return lax.ppermute(block, "core", [(0, 1), (1, 0)])


def dot(a, b, dims=((1,), (0,))):
    return lax.dot_general(a, b, (dims, ((), ())), preferred_element_type=F32)


def places(row, count):
    at = lax.broadcasted_iota(jnp.int32, (count, row.shape[1]), 0).astype(jnp.int16)
    return jnp.where(at == row.astype(jnp.int16), BF16(1), BF16(0))


def target_rows_of(slab_low, ids):
    pos_rows = dot(slab_low, places(ids[1:2], ROWS))
    return pos_rows, dot(slab_low, places(ids[3:4, :NPAD], ROWS)).astype(BF16)


def relation_rows_of(table, ids):
    return dot(table, places(ids[2:3], RPAD))


def edge_terms(heads, pos_rows, neg_rows, rel_rows):
    h_re, h_im = heads[:HALF], heads[HALF:]
    r_re, r_im = rel_rows[:HALF], rel_rows[HALF:]
    prod = jnp.concatenate([h_re * r_re - h_im * r_im, h_re * r_im + h_im * r_re], 0).astype(BF16)
    prod_wide = prod.astype(F32)
    pos = jnp.sum(prod_wide * pos_rows, 0, keepdims=True)
    g_pos = -jax.nn.sigmoid(-pos)
    g_neg = (jax.nn.sigmoid(dot(neg_rows, prod, ((0,), (0,)))) * (1.0 / NEG)).astype(BF16)
    d_pos = (g_pos * prod_wide).astype(BF16)
    d_prod = g_pos * pos_rows + dot(neg_rows, g_neg)
    p_re, p_im = d_prod[:HALF], d_prod[HALF:]
    d_rel = (p_re * h_re + p_im * h_im, p_im * h_re - p_re * h_im)
    return prod, g_neg, d_pos, d_rel


def trained(slab, state, ids, prod, g_neg, d_pos):
    along = ((1,), (1,))
    d_neg = dot(prod, g_neg, along).astype(BF16)
    grad = dot(d_pos, places(ids[1:2], ROWS), along)
    grad = grad + dot(d_neg, places(ids[3:4, :NPAD], ROWS), along)
    state = state + jnp.sum(grad * grad, 0, keepdims=True) * (1.0 / D)
    return slab - grad * (0.1 * lax.rsqrt(state)), state


def prepare_kernel(left, src, dst, rel, neg, ids, next_ids, left_low, wide, places_in, sems):
    sources = (src, dst, rel, neg)
    copies = [pltpu.make_async_copy(left, wide, sems.at[4])]
    copies += [pltpu.make_async_copy(r, places_in[i], sems.at[i]) for i, r in enumerate(sources)]
    for copy in copies:
        copy.start()
    for step_ids in (ids, next_ids):
        step_ids[...] = jnp.full(step_ids.shape, -1, jnp.int32)
    for copy in copies[1:]:
        copy.wait()
    for place, source in enumerate(places_in):
        for step, step_ids in enumerate((ids, next_ids)):
            step_ids[place : place + 1, : source.shape[1]] = source[step : step + 1, :]
    copies[0].wait()
    left_low[...] = wide[...].astype(BF16)


CHUNKS = ((0, 104), (104, 200), (200, 304), (304, 400))


def first_kernel(
    left, ids, slab_far, state_far, relation_far, slab_out, state_out, rel_grad, table, slab, state, relation, sems
):
    copies = [
        pltpu.make_async_copy(slab_far, slab, sems.at[0]),
        pltpu.make_async_copy(state_far, state, sems.at[1]),
    ]
    for i, (start, stop) in enumerate(CHUNKS):
        rows = slice(start, stop)
        copies.append(pltpu.make_async_copy(relation_far.at[rows], relation.at[rows], sems.at[2 + i]))
    for copy in copies:
        copy.start()
    heads = dot(left[...], places(ids[0:1], ROWS))
    for copy in copies[:2]:
        copy.wait()
    pos_rows, neg_rows = target_rows_of(slab[...].astype(BF16), ids)
    for copy in copies[2:]:
        copy.wait()
    table[:, :RMAIN] = relation[:, :RMAIN].astype(BF16)
    table[:, RMAIN:] = jnp.zeros((D, RPAD - RMAIN), BF16)
    table[:, RMAIN:NREL] = relation[:, RMAIN:].astype(BF16)
    rel_rows = relation_rows_of(table[...], ids)
    prod, g_neg, d_pos, d_rel = edge_terms(heads, pos_rows, neg_rows, rel_rows)
    slab_out[...], state_out[...] = trained(slab[...], state[...], ids[...], prod, g_neg, d_pos)
    whole = dot(jnp.concatenate(d_rel, 0).astype(BF16), places(ids[2:3], RPAD), ((1,), (1,)))
    for half in range(2):
        rel_grad[half] = whole[half * HALF : half * HALF + HALF]


def between_kernel(slab, table, ids, pos_rows, neg_rows, rel_rows):
    pos_rows[...], neg_rows[...] = target_rows_of(slab[...].astype(BF16), ids)
    rel_rows[...] = relation_rows_of(table[...], ids)


def rel_half(half, ids, d_rel, rel_grad):
    return rel_grad[half] + dot(d_rel[half], places(ids[2:3], RPAD), ((1,), (1,)))


def second_kernel(
    core, left, ids, pos_rows, neg_rows, rel_rows, rel_grad, prod, g_neg, d_pos, d_rel, other
):
    heads = dot(left[...], places(ids[0:1], ROWS))
    prod[...], g_neg[...], d_pos[...], parts = edge_terms(
        heads, pos_rows[...], neg_rows[...], rel_rows[...]
    )
    for half in range(2):
        d_rel[half] = parts[half].astype(BF16)
    other[...] = rel_half(1 - core[0], ids, d_rel, rel_grad)


def finish_kernel(
    core, slab, state, ids, rel_grad, prod, g_neg, d_pos, d_rel, mine, slab_out, state_out
):
    mine[...] = rel_half(core[0], ids, d_rel, rel_grad)
    slab_out[...], state_out[...] = trained(
        slab[...], state[...], ids[...], prod[...], g_neg[...], d_pos[...]
    )


def power_of(block):
    top = jnp.max(jnp.abs(block), axis=0, keepdims=True)
    return jnp.ceil(jnp.log2(jnp.maximum(top, 1e-30)))


def encode(main, last):
    lane = lax.broadcasted_iota(jnp.int32, last.shape, 1)
    row = lax.broadcasted_iota(jnp.int32, last.shape, 0)
    last = jnp.where(row < 7, last, 0.0)
    main_power, last_power = power_of(main), power_of(last)
    main = jnp.round(main * (LEVELS * jnp.exp2(-main_power)))
    last = jnp.round(last * (LEVELS * jnp.exp2(-last_power)))
    last_power = pltpu.roll(jnp.broadcast_to(last_power, last.shape), 64, 1)
    last = jnp.where(lane < 64, last, last_power)
    last = jnp.where(row == 7, jnp.broadcast_to(main_power, last.shape), last)
    fill = [jnp.zeros((CUT - main.shape[0], 128), F32)] if main.shape[0] < CUT else []
    return jnp.concatenate([main, *fill, last], 0).astype(jnp.int32).astype(jnp.int16)


def decode(codes):
    wide = codes.astype(jnp.int32).astype(F32)
    main, last = wide[:CUT], wide[CUT:]
    lane = lax.broadcasted_iota(jnp.int32, last.shape, 1)
    row = lax.broadcasted_iota(jnp.int32, last.shape, 0)
    main = main * (jnp.exp2(last[7:8]) * (1.0 / LEVELS))
    last_step = jnp.exp2(pltpu.roll(last, 64, 1)) * (1.0 / LEVELS)
    valid = jnp.logical_and(lane < NREL - RMAIN, row < 7)
    return main, jnp.where(valid, last * last_step, 0.0)


def place_of(part):
    tile, low = divmod(part, 2)
    rows = slice(CUT, HALF) if low else slice(0, CUT)
    return rows, slice(128 * tile, 128 * tile + 128)


def send_kernel(mine, theirs, codes, last):
    last[HALF:] = jnp.zeros((last.shape[0] - HALF, 128), F32)
    last[:HALF] = mine[:, RMAIN:] + theirs[:, RMAIN:]
    for part in range(OWNERS):
        at = place_of(part)
        codes[part] = encode(mine[at] + theirs[at], last[7 * part : 7 * part + 8])


def gather_kernel(parts, codes):
    main, last = decode(parts[0])
    for part in range(1, OWNERS):
        more = decode(parts[part])
        main, last = main + more[0], last + more[1]
    code = encode(main, last)
    for copy in range(codes.shape[0]):
        codes[copy] = code


def spread_kernel(parts, copies):
    main, last = decode(parts[0])
    for part in range(1, parts.shape[0]):
        more = decode(parts[part])
        main, last = main + more[0], last + more[1]
    code = encode(main, last)
    for copy in range(OWNERS):
        copies[copy] = code


def decoded_into(codes, grads, last):
    for part in range(OWNERS):
        rows, lanes = place_of(part)
        main, tail = decode(codes[part])
        grads[rows, lanes] = main[: rows.stop - rows.start]
        last[7 * part : 7 * part + 8] = tail
    grads[:, RMAIN:] = last[:HALF]
    return jnp.sum(grads[...] * grads[...], 0, keepdims=True)


def ours_kernel(codes, grads, squares, last):
    squares[...] = decoded_into(codes, grads, last)


def update_kernel(
    core, ours, squares, codes, relation, state, relation_out, state_out, theirs, last, wide, sems
):
    total = squares[...] + decoded_into(codes, theirs, last)
    new_state = state[...].reshape(1, NREL) + total[:, :NREL] * (1.0 / D)
    rate = 0.2 * lax.rsqrt(new_state)
    state_out[...] = new_state.reshape(NREL)
    copies = []
    for grad, half in ((ours, core[0]), (theirs, 1 - core[0])):
        for start, stop in ((0, 56), (56, 104), (104, 152), (152, 200)):
            rows = pl.ds(pl.multiple_of(half * HALF + start, 8), stop - start)
            wide[rows] = relation[rows] - grad[start:stop, :NREL] * rate
            copies.append(
                pltpu.make_async_copy(wide.at[rows], relation_out.at[rows], sems.at[len(copies)])
            )
            copies[-1].start()
    for copy in copies:
        copy.wait()


def per_device(
    left_embed,
    right_embed,
    right_state,
    relation_embed,
    relation_state,
    source_rows,
    target_rows,
    relation_ids,
    negative_rows,
):
    core = lax.axis_index("core").astype(jnp.int32)[None]
    id_array = kept((8, EPAD), jnp.int32)
    index_arrays = [
        array[0, 0] for array in (source_rows, target_rows, relation_ids, negative_rows)
    ]
    dma = pltpu.SemaphoreType.DMA
    ids, ids_next, left_low = call(
        prepare_kernel,
        (id_array, id_array, kept((D, ROWS), BF16)),
        left_embed[0].T,
        *index_arrays,
        far_in=range(5),
        scratch=[
            pltpu.VMEM((D, ROWS), F32),
            [pltpu.VMEM(array.shape, jnp.int32) for array in index_arrays],
            dma((5,)),
        ],
        name="prepare",
    )
    ids_next = from_next(ids_next)
    left_next = from_next(left_low)
    relation = relation_embed.T
    slab_array, state_array = (D, ROWS), (1, ROWS)
    edge_array = kept((D, EPAD), BF16)
    half_array = kept((HALF, RPAD), F32)
    slab, state, rel_grad, table = call(
        first_kernel,
        (
            kept(slab_array, F32),
            kept(state_array, F32),
            kept((2, HALF, RPAD), F32),
            kept((D, RPAD), BF16),
        ),
        left_low,
        ids,
        right_embed[0].T,
        right_state,
        relation,
        far_in=(2, 3, 4),
        scratch=[
            pltpu.VMEM(slab_array, F32),
            pltpu.VMEM(state_array, F32),
            pltpu.VMEM((D, NREL), F32),
            dma((6,)),
        ],

        name="first",
    )
    wide_array = kept((D, EPAD), F32)
    pos_rows, neg_rows, rel_rows = call(
        between_kernel,
        (wide_array, kept((D, NPAD), BF16), wide_array),
        slab,
        table,
        ids_next,
        flops=2 * 10**10,
        name="between",
    )
    prod, g_neg, d_pos, d_rel, other = call(
        second_kernel,
        (
            edge_array,
            kept((NPAD, EPAD), BF16),
            edge_array,
            kept((2, HALF, EPAD), BF16),
            half_array,
        ),
        left_next,
        ids_next,
        pos_rows,
        neg_rows,
        rel_rows,
        rel_grad,
        core=core,
        name="second",
    )
    theirs = swap_core(other)
    mine, slab_out, state_out = call(
        finish_kernel,
        (half_array, struct(slab_array, F32), struct(state_array, F32)),
        slab,
        state,
        ids_next,
        rel_grad,
        prod,
        g_neg,
        d_pos,
        d_rel,
        core=core,
        name="finish",
    )
    part = (PART, 128)
    last = pltpu.VMEM((232, 128), F32)
    parts = kept((OWNERS, *part), jnp.int16)
    sent = call(send_kernel, parts, mine, theirs, scratch=[last], name="send")
    got = lax.all_to_all(sent, CUBE, 0, 0, tiled=True)
    count = lax.axis_size("z_hi")
    codes = call(gather_kernel, kept((count, *part), jnp.int16), got, name="gather")
    codes = lax.all_to_all(codes, "z_hi", 0, 0, tiled=True)
    copies = call(spread_kernel, parts, codes, name="spread")
    ours = lax.all_to_all(copies, CUBE, 0, 0, tiled=True)
    theirs = swap_core(ours)
    grads, squares = call(
        ours_kernel, (half_array, kept((1, RPAD), F32)), ours, scratch=[last], name="ours"
    )
    relation_out, relation_state_out = call(
        update_kernel,
        (struct((D, NREL), F32), struct((NREL,), F32)),
        grads,
        squares,
        theirs,
        relation,
        relation_state,
        core=core,
        far_out=(0,),
        scratch=[
            pltpu.VMEM((HALF, RPAD), F32),
            last,
            pltpu.VMEM((D, NREL), F32),
            dma((8,)),
        ],
        name="update",
    )
    return (slab_out.T[None], state_out, relation_out.T, relation_state_out)


def solution(mesh):
    split = jax.sharding.Mesh(mesh.devices.reshape(4, 4, 2, 2, 2, 2), AXES)
    in_specs = (
        P(REPLICA, BUCKET, None),
        P(REPLICA, BUCKET, None),
        P(REPLICA, BUCKET),
        P(),
        P(),
        P(REPLICA, BUCKET, None, None),
        P(REPLICA, BUCKET, None, None),
        P(REPLICA, BUCKET, None, None),
        P(REPLICA, BUCKET, None, None),
    )
    out_specs = (P(REPLICA, BUCKET, None), P(REPLICA, BUCKET), P(), P())
    return jax.shard_map(
        per_device, mesh=split, in_specs=in_specs, out_specs=out_specs, check_vma=False
    )
```

```python
import jax
import jax.numpy as jnp
from jax import lax
from jax.experimental import pallas as pl
from jax.experimental.pallas import tpu as pltpu
from jax.sharding import PartitionSpec as P

AXES = ("x", "z_hi", "z_lo", "y_lo", "y_hi", "core")
BUCKET = ("x", "z_hi", "z_lo", "y_lo")
REPLICA = ("y_hi", "core")
CUBE = ("x", "z_lo", "y_lo", "y_hi")
OWNERS = 32
D = 400
HALF = 200
EPAD = 1024
NEG = 500
NPAD = 512
ROWS = 512
NREL = 2066
RMAIN = 2048
RPAD = 2176
CUT = 104
PART = 112
LEVELS = 32000.0
F32 = jnp.float32
BF16 = jnp.bfloat16


def struct(shape, dtype):
    return jax.ShapeDtypeStruct(shape, dtype)


def kept(shape, dtype):
    return pltpu.VMEM(shape, dtype)


def near(array):
    return pltpu.with_memory_space_constraint(array, pltpu.VMEM)


def away(array):
    return pltpu.with_memory_space_constraint(array, pltpu.HBM)


def call(kernel, out_shape, *args, core=None, scratch=(), far_in=(), far_out=(), name, flops=None):
    vmem = pl.BlockSpec(memory_space=pltpu.VMEM)
    far = pl.BlockSpec(memory_space=pltpu.HBM)
    several = isinstance(out_shape, tuple)
    outs = out_shape if several else (out_shape,)
    specs = tuple(far if i in far_out else vmem for i in range(len(outs)))
    in_specs = [far if i in far_in else vmem for i in range(len(args))]
    args = [away(arg) if i in far_in else near(arg) for i, arg in enumerate(args)]
    if core is not None:
        in_specs, args = [pl.BlockSpec(memory_space=pltpu.SMEM)] + in_specs, [core] + args
    return pl.pallas_call(
        kernel,
        out_shape=out_shape,
        in_specs=in_specs,
        out_specs=specs if several else specs[0],
        scratch_shapes=scratch,
        compiler_params=pltpu.CompilerParams(vmem_limit_bytes=32 * 1024 * 1024),
        cost_estimate=flops and pl.CostEstimate(flops=flops, bytes_accessed=0, transcendentals=0),
        name=name,
    )(*args)


def from_next(block):
    count = lax.axis_size(BUCKET)
    return lax.ppermute(block, BUCKET, [((i + 1) % count, i) for i in range(count)])


def swap_core(block):
    return lax.ppermute(block, "core", [(0, 1), (1, 0)])


def dot(a, b, dims=((1,), (0,))):
    return lax.dot_general(a, b, (dims, ((), ())), preferred_element_type=F32)


def places(row, count):
    at = lax.broadcasted_iota(jnp.int32, (count, row.shape[1]), 0).astype(jnp.int16)
    return jnp.where(at == row.astype(jnp.int16), BF16(1), BF16(0))


def target_rows_of(slab_low, ids):
    pos_rows = dot(slab_low, places(ids[1:2], ROWS))
    return pos_rows, dot(slab_low, places(ids[3:4, :NPAD], ROWS)).astype(BF16)


def relation_rows_of(table, ids):
    return dot(table, places(ids[2:3], RPAD))


def edge_terms(heads, pos_rows, neg_rows, rel_rows):
    h_re, h_im = heads[:HALF], heads[HALF:]
    r_re, r_im = rel_rows[:HALF], rel_rows[HALF:]
    prod = jnp.concatenate([h_re * r_re - h_im * r_im, h_re * r_im + h_im * r_re], 0).astype(BF16)
    prod_wide = prod.astype(F32)
    pos = jnp.sum(prod_wide * pos_rows, 0, keepdims=True)
    g_pos = -jax.nn.sigmoid(-pos)
    g_neg = (jax.nn.sigmoid(dot(neg_rows, prod, ((0,), (0,)))) * (1.0 / NEG)).astype(BF16)
    d_pos = (g_pos * prod_wide).astype(BF16)
    d_prod = g_pos * pos_rows + dot(neg_rows, g_neg)
    p_re, p_im = d_prod[:HALF], d_prod[HALF:]
    d_rel = (p_re * h_re + p_im * h_im, p_im * h_re - p_re * h_im)
    return prod, g_neg, d_pos, d_rel


def trained(slab, state, ids, prod, g_neg, d_pos):
    along = ((1,), (1,))
    d_neg = dot(prod, g_neg, along).astype(BF16)
    grad = dot(d_pos, places(ids[1:2], ROWS), along)
    grad = grad + dot(d_neg, places(ids[3:4, :NPAD], ROWS), along)
    state = state + jnp.sum(grad * grad, 0, keepdims=True) * (1.0 / D)
    return slab - grad * (0.1 * lax.rsqrt(state)), state


def prepare_kernel(left, src, dst, rel, neg, ids, next_ids, left_low, wide, places_in, sems):
    sources = (src, dst, rel, neg)
    copies = [pltpu.make_async_copy(left, wide, sems.at[4])]
    copies += [pltpu.make_async_copy(r, places_in[i], sems.at[i]) for i, r in enumerate(sources)]
    for copy in copies:
        copy.start()
    for step_ids in (ids, next_ids):
        step_ids[...] = jnp.full(step_ids.shape, -1, jnp.int32)
    for copy in copies[1:]:
        copy.wait()
    for place, source in enumerate(places_in):
        for step, step_ids in enumerate((ids, next_ids)):
            step_ids[place : place + 1, : source.shape[1]] = source[step : step + 1, :]
    copies[0].wait()
    left_low[...] = wide[...].astype(BF16)


CHUNKS = ((0, 104), (104, 200), (200, 304), (304, 400))


def first_kernel(
    left, ids, slab_far, state_far, relation_far, slab_out, state_out, rel_grad, table, slab, state, relation, sems
):
    copies = [
        pltpu.make_async_copy(slab_far, slab, sems.at[0]),
        pltpu.make_async_copy(state_far, state, sems.at[1]),
    ]
    for i, (start, stop) in enumerate(CHUNKS):
        rows = slice(start, stop)
        copies.append(pltpu.make_async_copy(relation_far.at[rows], relation.at[rows], sems.at[2 + i]))
    for copy in copies:
        copy.start()
    heads = dot(left[...], places(ids[0:1], ROWS))
    for copy in copies[:2]:
        copy.wait()
    pos_rows, neg_rows = target_rows_of(slab[...].astype(BF16), ids)
    for copy in copies[2:]:
        copy.wait()
    table[:, :RMAIN] = relation[:, :RMAIN].astype(BF16)
    table[:, RMAIN:] = jnp.zeros((D, RPAD - RMAIN), BF16)
    table[:, RMAIN:NREL] = relation[:, RMAIN:].astype(BF16)
    rel_rows = relation_rows_of(table[...], ids)
    prod, g_neg, d_pos, d_rel = edge_terms(heads, pos_rows, neg_rows, rel_rows)
    slab_out[...], state_out[...] = trained(slab[...], state[...], ids[...], prod, g_neg, d_pos)
    whole = dot(jnp.concatenate(d_rel, 0).astype(BF16), places(ids[2:3], RPAD), ((1,), (1,)))
    for half in range(2):
        rel_grad[half] = whole[half * HALF : half * HALF + HALF]


def between_kernel(slab, table, ids, pos_rows, neg_rows, rel_rows):
    pos_rows[...], neg_rows[...] = target_rows_of(slab[...].astype(BF16), ids)
    rel_rows[...] = relation_rows_of(table[...], ids)


def rel_half(half, ids, d_rel, rel_grad):
    return rel_grad[half] + dot(d_rel[half], places(ids[2:3], RPAD), ((1,), (1,)))


def second_kernel(
    core, left, ids, pos_rows, neg_rows, rel_rows, rel_grad, prod, g_neg, d_pos, d_rel, other, grads, last
):
    heads = dot(left[...], places(ids[0:1], ROWS))
    prod[...], g_neg[...], d_pos[...], parts = edge_terms(
        heads, pos_rows[...], neg_rows[...], rel_rows[...]
    )
    for half in range(2):
        d_rel[half] = parts[half].astype(BF16)
    grads[...] = rel_half(1 - core[0], ids, d_rel, rel_grad)
    last[HALF:] = jnp.zeros((last.shape[0] - HALF, 128), F32)
    last[:HALF] = grads[:, RMAIN:]
    for part in range(OWNERS):
        other[part] = encode(grads[place_of(part)], last[7 * part : 7 * part + 8])


def own_half_kernel(core, ids, rel_grad, d_rel, mine):
    mine[...] = rel_half(core[0], ids, d_rel, rel_grad)


def target_kernel(after, slab, state, ids, prod, g_neg, d_pos, slab_out, state_out, done):
    slab_out[...], state_out[...] = trained(
        slab[...], state[...], ids[...], prod[...], g_neg[...], d_pos[...]
    )
    done[...] = after[:, :128]


def power_of(block):
    top = jnp.max(jnp.abs(block), axis=0, keepdims=True)
    return jnp.ceil(jnp.log2(jnp.maximum(top, 1e-30)))


def encode(main, last):
    lane = lax.broadcasted_iota(jnp.int32, last.shape, 1)
    row = lax.broadcasted_iota(jnp.int32, last.shape, 0)
    last = jnp.where(row < 7, last, 0.0)
    main_power, last_power = power_of(main), power_of(last)
    main = jnp.round(main * (LEVELS * jnp.exp2(-main_power)))
    last = jnp.round(last * (LEVELS * jnp.exp2(-last_power)))
    last_power = pltpu.roll(jnp.broadcast_to(last_power, last.shape), 64, 1)
    last = jnp.where(lane < 64, last, last_power)
    last = jnp.where(row == 7, jnp.broadcast_to(main_power, last.shape), last)
    fill = [jnp.zeros((CUT - main.shape[0], 128), F32)] if main.shape[0] < CUT else []
    return jnp.concatenate([main, *fill, last], 0).astype(jnp.int32).astype(jnp.int16)


def decode(codes):
    wide = codes.astype(jnp.int32).astype(F32)
    main, last = wide[:CUT], wide[CUT:]
    lane = lax.broadcasted_iota(jnp.int32, last.shape, 1)
    row = lax.broadcasted_iota(jnp.int32, last.shape, 0)
    main = main * (jnp.exp2(last[7:8]) * (1.0 / LEVELS))
    last_step = jnp.exp2(pltpu.roll(last, 64, 1)) * (1.0 / LEVELS)
    valid = jnp.logical_and(lane < NREL - RMAIN, row < 7)
    return main, jnp.where(valid, last * last_step, 0.0)


def place_of(part):
    tile, low = divmod(part, 2)
    rows = slice(CUT, HALF) if low else slice(0, CUT)
    return rows, slice(128 * tile, 128 * tile + 128)


def send_kernel(mine, theirs, codes, last):
    last[HALF:] = jnp.zeros((last.shape[0] - HALF, 128), F32)
    last[:HALF] = mine[:, RMAIN:]
    for part in range(OWNERS):
        rows, lanes = place_of(part)
        main, tail = decode(theirs[part])
        main = mine[rows, lanes] + main[: rows.stop - rows.start]
        codes[part] = encode(main, last[7 * part : 7 * part + 8] + tail)


def gather_kernel(parts, codes):
    main, last = decode(parts[0])
    for part in range(1, OWNERS):
        more = decode(parts[part])
        main, last = main + more[0], last + more[1]
    code = encode(main, last)
    for copy in range(codes.shape[0]):
        codes[copy] = code


def spread_kernel(parts, copies):
    main, last = decode(parts[0])
    for part in range(1, parts.shape[0]):
        more = decode(parts[part])
        main, last = main + more[0], last + more[1]
    code = encode(main, last)
    for copy in range(OWNERS):
        copies[copy] = code


def decoded_into(codes, grads, last):
    for part in range(OWNERS):
        rows, lanes = place_of(part)
        main, tail = decode(codes[part])
        grads[rows, lanes] = main[: rows.stop - rows.start]
        last[7 * part : 7 * part + 8] = tail
    grads[:, RMAIN:] = last[:HALF]
    return jnp.sum(grads[...] * grads[...], 0, keepdims=True)


def ours_kernel(codes, grads, squares, last):
    squares[...] = decoded_into(codes, grads, last)


def update_kernel(
    core, ours, squares, codes, relation, state, done, relation_out, state_out, theirs, last, wide, sems
):
    total = squares[...] + decoded_into(codes, theirs, last)
    new_state = state[...].reshape(1, NREL) + total[:, :NREL] * (1.0 / D)
    rate = 0.2 * lax.rsqrt(new_state)
    state_out[...] = new_state.reshape(NREL)
    copies = []
    for grad, half in ((ours, core[0]), (theirs, 1 - core[0])):
        for start, stop in ((0, 56), (56, 104), (104, 152), (152, 200)):
            rows = pl.ds(pl.multiple_of(half * HALF + start, 8), stop - start)
            wide[rows] = relation[rows] - grad[start:stop, :NREL] * rate
            copies.append(
                pltpu.make_async_copy(wide.at[rows], relation_out.at[rows], sems.at[len(copies)])
            )
            copies[-1].start()
    for copy in copies:
        copy.wait()


def per_device(
    left_embed,
    right_embed,
    right_state,
    relation_embed,
    relation_state,
    source_rows,
    target_rows,
    relation_ids,
    negative_rows,
):
    core = lax.axis_index("core").astype(jnp.int32)[None]
    id_array = kept((8, EPAD), jnp.int32)
    index_arrays = [
        array[0, 0] for array in (source_rows, target_rows, relation_ids, negative_rows)
    ]
    dma = pltpu.SemaphoreType.DMA
    ids, ids_next, left_low = call(
        prepare_kernel,
        (id_array, id_array, kept((D, ROWS), BF16)),
        left_embed[0].T,
        *index_arrays,
        far_in=range(5),
        scratch=[
            pltpu.VMEM((D, ROWS), F32),
            [pltpu.VMEM(array.shape, jnp.int32) for array in index_arrays],
            dma((5,)),
        ],
        name="prepare",
    )
    ids_next = from_next(ids_next)
    left_next = from_next(left_low)
    relation = relation_embed.T
    slab_array, state_array = (D, ROWS), (1, ROWS)
    edge_array = kept((D, EPAD), BF16)
    half_array = kept((HALF, RPAD), F32)
    slab, state, rel_grad, table = call(
        first_kernel,
        (
            kept(slab_array, F32),
            kept(state_array, F32),
            kept((2, HALF, RPAD), F32),
            kept((D, RPAD), BF16),
        ),
        left_low,
        ids,
        right_embed[0].T,
        right_state,
        relation,
        far_in=(2, 3, 4),
        scratch=[
            pltpu.VMEM(slab_array, F32),
            pltpu.VMEM(state_array, F32),
            pltpu.VMEM((D, NREL), F32),
            dma((6,)),
        ],

        name="first",
    )
    wide_array = kept((D, EPAD), F32)
    part = (PART, 128)
    last = pltpu.VMEM((232, 128), F32)
    parts = kept((OWNERS, *part), jnp.int16)
    pos_rows, neg_rows, rel_rows = call(
        between_kernel,
        (wide_array, kept((D, NPAD), BF16), wide_array),
        slab,
        table,
        ids_next,
        flops=2 * 10**10,
        name="between",
    )
    prod, g_neg, d_pos, d_rel, other = call(
        second_kernel,
        (
            edge_array,
            kept((NPAD, EPAD), BF16),
            edge_array,
            kept((2, HALF, EPAD), BF16),
            parts,
        ),
        left_next,
        ids_next,
        pos_rows,
        neg_rows,
        rel_rows,
        rel_grad,
        core=core,
        scratch=[pltpu.VMEM((HALF, RPAD), F32), last],
        name="second",
    )
    theirs = swap_core(other)
    mine = call(
        own_half_kernel, half_array, ids_next, rel_grad, d_rel, core=core, name="own_half"
    )
    sent = call(send_kernel, parts, mine, theirs, scratch=[last], name="send")
    got = lax.all_to_all(sent, CUBE, 0, 0, tiled=True)
    count = lax.axis_size("z_hi")
    codes = call(gather_kernel, kept((count, *part), jnp.int16), got, name="gather")
    codes = lax.all_to_all(codes, "z_hi", 0, 0, tiled=True)
    copies = call(spread_kernel, parts, codes, name="spread")
    ours = lax.all_to_all(copies, CUBE, 0, 0, tiled=True)
    theirs = swap_core(ours)
    grads, squares = call(
        ours_kernel, (half_array, kept((1, RPAD), F32)), ours, scratch=[last], name="ours"
    )
    slab_out, state_out, done = call(
        target_kernel,
        (struct(slab_array, F32), struct(state_array, F32), kept((1, 128), F32)),
        squares,
        slab,
        state,
        ids_next,
        prod,
        g_neg,
        d_pos,
        name="target",
    )
    relation_out, relation_state_out = call(
        update_kernel,
        (struct((D, NREL), F32), struct((NREL,), F32)),
        grads,
        squares,
        theirs,
        relation,
        relation_state,
        done,
        core=core,
        far_out=(0,),
        scratch=[
            pltpu.VMEM((HALF, RPAD), F32),
            last,
            pltpu.VMEM((D, NREL), F32),
            dma((8,)),
        ],
        name="update",
    )
    return (slab_out.T[None], state_out, relation_out.T, relation_state_out)


def solution(mesh):
    split = jax.sharding.Mesh(mesh.devices.reshape(4, 4, 2, 2, 2, 2), AXES)
    in_specs = (
        P(REPLICA, BUCKET, None),
        P(REPLICA, BUCKET, None),
        P(REPLICA, BUCKET),
        P(),
        P(),
        P(REPLICA, BUCKET, None, None),
        P(REPLICA, BUCKET, None, None),
        P(REPLICA, BUCKET, None, None),
        P(REPLICA, BUCKET, None, None),
    )
    out_specs = (P(REPLICA, BUCKET, None), P(REPLICA, BUCKET), P(), P())
    return jax.shard_map(
        per_device, mesh=split, in_specs=in_specs, out_specs=out_specs, check_vma=False
    )
```

```python
import jax
import jax.numpy as jnp
from jax import lax
from jax.experimental import pallas as pl
from jax.experimental.pallas import tpu as pltpu
from jax.sharding import PartitionSpec as P

AXES = ("x", "z_hi", "z_lo", "y_lo", "y_hi", "core")
BUCKET = ("x", "z_hi", "z_lo", "y_lo")
REPLICA = ("y_hi", "core")
CUBE = ("x", "z_lo", "y_lo", "y_hi")
OWNERS = 32
D = 400
HALF = 200
EPAD = 1024
NEG = 500
NPAD = 512
ROWS = 512
NREL = 2066
RMAIN = 2048
RPAD = 2176
CUT = 100
PART = 104
EXTRA = NREL - RMAIN
LEVELS = 32000.0
F32 = jnp.float32
BF16 = jnp.bfloat16


def struct(shape, dtype):
    return jax.ShapeDtypeStruct(shape, dtype)


def kept(shape, dtype):
    return pltpu.VMEM(shape, dtype)


def near(array):
    return pltpu.with_memory_space_constraint(array, pltpu.VMEM)


def away(array):
    return pltpu.with_memory_space_constraint(array, pltpu.HBM)


def call(kernel, out_shape, *args, core=None, scratch=(), far_in=(), far_out=(), name, flops=None):
    vmem = pl.BlockSpec(memory_space=pltpu.VMEM)
    far = pl.BlockSpec(memory_space=pltpu.HBM)
    several = isinstance(out_shape, tuple)
    outs = out_shape if several else (out_shape,)
    specs = tuple(far if i in far_out else vmem for i in range(len(outs)))
    in_specs = [far if i in far_in else vmem for i in range(len(args))]
    args = [away(arg) if i in far_in else near(arg) for i, arg in enumerate(args)]
    if core is not None:
        in_specs, args = [pl.BlockSpec(memory_space=pltpu.SMEM)] + in_specs, [core] + args
    return pl.pallas_call(
        kernel,
        out_shape=out_shape,
        in_specs=in_specs,
        out_specs=specs if several else specs[0],
        scratch_shapes=scratch,
        compiler_params=pltpu.CompilerParams(vmem_limit_bytes=32 * 1024 * 1024),
        cost_estimate=flops and pl.CostEstimate(flops=flops, bytes_accessed=0, transcendentals=0),
        name=name,
    )(*args)


def from_next(block):
    count = lax.axis_size(BUCKET)
    return lax.ppermute(block, BUCKET, [((i + 1) % count, i) for i in range(count)])


def swap_core(block):
    return lax.ppermute(block, "core", [(0, 1), (1, 0)])


def dot(a, b, dims=((1,), (0,))):
    return lax.dot_general(a, b, (dims, ((), ())), preferred_element_type=F32)


def places(row, count):
    at = lax.broadcasted_iota(jnp.int32, (count, row.shape[1]), 0).astype(jnp.int16)
    return jnp.where(at == row.astype(jnp.int16), BF16(1), BF16(0))


def target_rows_of(slab_low, ids):
    pos_rows = dot(slab_low, places(ids[1:2], ROWS))
    return pos_rows, dot(slab_low, places(ids[3:4, :NPAD], ROWS)).astype(BF16)


def relation_rows_of(table, ids):
    return dot(table, places(ids[2:3], RPAD))


def edge_terms(heads, pos_rows, neg_rows, rel_rows):
    h_re, h_im = heads[:HALF], heads[HALF:]
    r_re, r_im = rel_rows[:HALF], rel_rows[HALF:]
    prod = jnp.concatenate([h_re * r_re - h_im * r_im, h_re * r_im + h_im * r_re], 0).astype(BF16)
    prod_wide = prod.astype(F32)
    pos = jnp.sum(prod_wide * pos_rows, 0, keepdims=True)
    g_pos = -jax.nn.sigmoid(-pos)
    g_neg = (jax.nn.sigmoid(dot(neg_rows, prod, ((0,), (0,)))) * (1.0 / NEG)).astype(BF16)
    d_pos = (g_pos * prod_wide).astype(BF16)
    d_prod = g_pos * pos_rows + dot(neg_rows, g_neg)
    p_re, p_im = d_prod[:HALF], d_prod[HALF:]
    d_rel = (p_re * h_re + p_im * h_im, p_im * h_re - p_re * h_im)
    return prod, g_neg, d_pos, d_rel


def trained(slab, state, ids, prod, g_neg, d_pos):
    along = ((1,), (1,))
    d_neg = dot(prod, g_neg, along).astype(BF16)
    grad = dot(d_pos, places(ids[1:2], ROWS), along)
    grad = grad + dot(d_neg, places(ids[3:4, :NPAD], ROWS), along)
    state = state + jnp.sum(grad * grad, 0, keepdims=True) * (1.0 / D)
    return slab - grad * (0.1 * lax.rsqrt(state)), state


def prepare_kernel(left, src, dst, rel, neg, ids, next_ids, left_low, wide, places_in, sems):
    sources = (src, dst, rel, neg)
    copies = [pltpu.make_async_copy(left, wide, sems.at[4])]
    copies += [pltpu.make_async_copy(r, places_in[i], sems.at[i]) for i, r in enumerate(sources)]
    for copy in copies:
        copy.start()
    for step_ids in (ids, next_ids):
        step_ids[...] = jnp.full(step_ids.shape, -1, jnp.int32)
    for copy in copies[1:]:
        copy.wait()
    for place, source in enumerate(places_in):
        for step, step_ids in enumerate((ids, next_ids)):
            step_ids[place : place + 1, : source.shape[1]] = source[step : step + 1, :]
    copies[0].wait()
    left_low[...] = wide[...].astype(BF16)


CHUNKS = ((0, 104), (104, 200), (200, 304), (304, 400))


def first_kernel(
    left, ids, slab_far, state_far, relation_far, slab_out, state_out, rel_grad, table, slab, state, relation, sems
):
    copies = [
        pltpu.make_async_copy(slab_far, slab, sems.at[0]),
        pltpu.make_async_copy(state_far, state, sems.at[1]),
    ]
    for i, (start, stop) in enumerate(CHUNKS):
        rows = slice(start, stop)
        copies.append(pltpu.make_async_copy(relation_far.at[rows], relation.at[rows], sems.at[2 + i]))
    for copy in copies:
        copy.start()
    heads = dot(left[...], places(ids[0:1], ROWS))
    for copy in copies[:2]:
        copy.wait()
    pos_rows, neg_rows = target_rows_of(slab[...].astype(BF16), ids)
    for copy in copies[2:]:
        copy.wait()
    table[:, :RMAIN] = relation[:, :RMAIN].astype(BF16)
    table[:, RMAIN:] = jnp.zeros((D, RPAD - RMAIN), BF16)
    table[:, RMAIN:NREL] = relation[:, RMAIN:].astype(BF16)
    rel_rows = relation_rows_of(table[...], ids)
    prod, g_neg, d_pos, d_rel = edge_terms(heads, pos_rows, neg_rows, rel_rows)
    slab_out[...], state_out[...] = trained(slab[...], state[...], ids[...], prod, g_neg, d_pos)
    whole = dot(jnp.concatenate(d_rel, 0).astype(BF16), places(ids[2:3], RPAD), ((1,), (1,)))
    for half in range(2):
        rel_grad[half] = whole[half * HALF : half * HALF + HALF]


def between_kernel(slab, table, ids, pos_rows, neg_rows, rel_rows):
    pos_rows[...], neg_rows[...] = target_rows_of(slab[...].astype(BF16), ids)
    rel_rows[...] = relation_rows_of(table[...], ids)


def rel_half(half, ids, d_rel, rel_grad):
    return rel_grad[half] + dot(d_rel[half], places(ids[2:3], RPAD), ((1,), (1,)))


def second_kernel(
    core, left, ids, pos_rows, neg_rows, rel_rows, rel_grad, prod, g_neg, d_pos, d_rel, other, grads
):
    heads = dot(left[...], places(ids[0:1], ROWS))
    prod[...], g_neg[...], d_pos[...], parts = edge_terms(
        heads, pos_rows[...], neg_rows[...], rel_rows[...]
    )
    for half in range(2):
        d_rel[half] = parts[half].astype(BF16)
    grads[...] = rel_half(1 - core[0], ids, d_rel, rel_grad)
    firsts, seconds = last_relations(grads)
    for part in range(OWNERS):
        other[part] = encode(block_of(grads, part), *picked(firsts, seconds, part))


def own_half_kernel(core, ids, rel_grad, d_rel, mine):
    mine[...] = rel_half(core[0], ids, d_rel, rel_grad)


def target_kernel(after, slab, state, ids, prod, g_neg, d_pos, slab_out, state_out, done):
    slab_out[...], state_out[...] = trained(
        slab[...], state[...], ids[...], prod[...], g_neg[...], d_pos[...]
    )
    done[...] = after[:, :128]


def power_of(top):
    return jnp.ceil(jnp.log2(jnp.maximum(top, 1e-30)))


def iota(shape, axis):
    return lax.broadcasted_iota(jnp.int32, shape, axis)


def encode(main, first, second):
    row = iota(main.shape, 0)
    main = jnp.where(row < CUT, main, 0.0)
    power = power_of(jnp.max(jnp.abs(main), axis=0, keepdims=True))
    top = jnp.maximum(jnp.abs(first), jnp.abs(second))
    last_power = power_of(jnp.max(top, axis=1, keepdims=True))
    scale = LEVELS * jnp.exp2(-last_power)
    second = jnp.where(iota(second.shape, 1) == 127, last_power, jnp.round(second * scale))
    codes = jnp.round(main * (LEVELS * jnp.exp2(-power)))
    codes = jnp.where(row == CUT, jnp.round(first * scale), codes)
    codes = jnp.where(row == CUT + 1, second, codes)
    codes = jnp.where(row == CUT + 2, power, codes)
    return codes.astype(jnp.int32).astype(jnp.int16)


def decode(codes):
    wide = codes.astype(jnp.int32).astype(F32)
    first, second, power = (wide[CUT + i : CUT + i + 1] for i in range(3))
    step = jnp.exp2(second[:, 127:]) * (1.0 / LEVELS)
    second = jnp.where(iota(second.shape, 1) < HALF - 128, second * step, 0.0)
    main = jnp.where(iota(wide.shape, 0) < CUT, wide, 0.0)
    return main * (jnp.exp2(power) * (1.0 / LEVELS)), first * step, second


def block_of(grads, part):
    tile, low = divmod(part, 2)
    lanes = slice(128 * tile, 128 * tile + 128)
    return pltpu.roll(grads[HALF - PART :, lanes], CUT, 0) if low else grads[:PART, lanes]


def last_relations(grads):
    gap = jnp.zeros((256 - HALF, 128), F32)
    rows = jnp.transpose(jnp.concatenate([grads[:, RMAIN:], gap], 0))
    return rows[:, :128], rows[:, 128:]


def picked(firsts, seconds, part):
    if part >= EXTRA:
        return jnp.zeros((1, 128), F32), jnp.zeros((1, 128), F32)
    return firsts[part : part + 1], seconds[part : part + 1]


def send_kernel(mine, theirs, codes):
    firsts, seconds = last_relations(mine)
    for part in range(OWNERS):
        main, first, second = decode(theirs[part])
        own_first, own_second = picked(firsts, seconds, part)
        codes[part] = encode(block_of(mine, part) + main, own_first + first, own_second + second)


def summed(parts):
    total = decode(parts[0])
    for part in range(1, parts.shape[0]):
        total = tuple(old + new for old, new in zip(total, decode(parts[part])))
    return total


def gather_kernel(parts, codes):
    code = encode(*summed(parts))
    for copy in range(codes.shape[0]):
        codes[copy] = code


def decoded_into(codes, grads, last):
    last[...] = jnp.zeros(last.shape, F32)
    for tile in range(OWNERS // 2):
        lanes = slice(128 * tile, 128 * tile + 128)
        blocks = []
        for part in (2 * tile, 2 * tile + 1):
            block, first, second = decode(codes[part])
            blocks.append(block)
            if part < EXTRA:
                last[part : part + 1, :128] = first
                last[part : part + 1, 128:] = second
        upper, lower = blocks[0], pltpu.roll(blocks[1], PART - CUT, 0)
        grads[: HALF - PART, lanes] = upper[: HALF - PART]
        grads[HALF - PART : PART, lanes] = upper[HALF - PART :] + lower[: 2 * PART - HALF]
        grads[PART:, lanes] = lower[2 * PART - HALF :]
    grads[:, RMAIN:] = jnp.transpose(last[...])[:HALF]
    return jnp.sum(grads[...] * grads[...], 0, keepdims=True)


def ours_kernel(codes, grads, squares, last):
    squares[...] = decoded_into(codes, grads, last)


def update_kernel(
    core, ours, squares, codes, relation, state, done, relation_out, state_out, theirs, last, wide, sems
):
    total = squares[...] + decoded_into(codes, theirs, last)
    new_state = state[...].reshape(1, NREL) + total[:, :NREL] * (1.0 / D)
    rate = 0.2 * lax.rsqrt(new_state)
    state_out[...] = new_state.reshape(NREL)
    copies = []
    for grad, half in ((ours, core[0]), (theirs, 1 - core[0])):
        for start, stop in ((0, 56), (56, 104), (104, 152), (152, 200)):
            rows = pl.ds(pl.multiple_of(half * HALF + start, 8), stop - start)
            wide[rows] = relation[rows] - grad[start:stop, :NREL] * rate
            copies.append(
                pltpu.make_async_copy(wide.at[rows], relation_out.at[rows], sems.at[len(copies)])
            )
            copies[-1].start()
    for copy in copies:
        copy.wait()


def per_device(
    left_embed,
    right_embed,
    right_state,
    relation_embed,
    relation_state,
    source_rows,
    target_rows,
    relation_ids,
    negative_rows,
):
    core = lax.axis_index("core").astype(jnp.int32)[None]
    id_array = kept((8, EPAD), jnp.int32)
    index_arrays = [
        array[0, 0] for array in (source_rows, target_rows, relation_ids, negative_rows)
    ]
    dma = pltpu.SemaphoreType.DMA
    ids, ids_next, left_low = call(
        prepare_kernel,
        (id_array, id_array, kept((D, ROWS), BF16)),
        left_embed[0].T,
        *index_arrays,
        far_in=range(5),
        scratch=[
            pltpu.VMEM((D, ROWS), F32),
            [pltpu.VMEM(array.shape, jnp.int32) for array in index_arrays],
            dma((5,)),
        ],
        name="prepare",
    )
    ids_next = from_next(ids_next)
    left_next = from_next(left_low)
    relation = relation_embed.T
    slab_array, state_array = (D, ROWS), (1, ROWS)
    edge_array = kept((D, EPAD), BF16)
    half_array = kept((HALF, RPAD), F32)
    slab, state, rel_grad, table = call(
        first_kernel,
        (
            kept(slab_array, F32),
            kept(state_array, F32),
            kept((2, HALF, RPAD), F32),
            kept((D, RPAD), BF16),
        ),
        left_low,
        ids,
        right_embed[0].T,
        right_state,
        relation,
        far_in=(2, 3, 4),
        scratch=[
            pltpu.VMEM(slab_array, F32),
            pltpu.VMEM(state_array, F32),
            pltpu.VMEM((D, NREL), F32),
            dma((6,)),
        ],

        name="first",
    )
    wide_array = kept((D, EPAD), F32)
    part = (PART, 128)
    last = pltpu.VMEM((128, 256), F32)
    parts = kept((OWNERS, *part), jnp.int16)
    pos_rows, neg_rows, rel_rows = call(
        between_kernel,
        (wide_array, kept((D, NPAD), BF16), wide_array),
        slab,
        table,
        ids_next,
        flops=2 * 10**10,
        name="between",
    )
    prod, g_neg, d_pos, d_rel, other = call(
        second_kernel,
        (
            edge_array,
            kept((NPAD, EPAD), BF16),
            edge_array,
            kept((2, HALF, EPAD), BF16),
            parts,
        ),
        left_next,
        ids_next,
        pos_rows,
        neg_rows,
        rel_rows,
        rel_grad,
        core=core,
        scratch=[pltpu.VMEM((HALF, RPAD), F32)],
        name="second",
    )
    theirs = swap_core(other)
    mine = call(
        own_half_kernel, half_array, ids_next, rel_grad, d_rel, core=core, name="own_half"
    )
    sent = call(send_kernel, parts, mine, theirs, name="send")
    got = lax.all_to_all(sent, CUBE, 0, 0, tiled=True)
    count = lax.axis_size("z_hi")
    codes = call(gather_kernel, kept((count, *part), jnp.int16), got, name="gather")
    codes = lax.all_to_all(codes, "z_hi", 0, 0, tiled=True)
    copies = call(gather_kernel, parts, codes, name="spread")
    ours = lax.all_to_all(copies, CUBE, 0, 0, tiled=True)
    theirs = swap_core(ours)
    grads, squares = call(
        ours_kernel, (half_array, kept((1, RPAD), F32)), ours, scratch=[last], name="ours"
    )
    slab_out, state_out, done = call(
        target_kernel,
        (struct(slab_array, F32), struct(state_array, F32), kept((1, 128), F32)),
        squares,
        slab,
        state,
        ids_next,
        prod,
        g_neg,
        d_pos,
        name="target",
    )
    relation_out, relation_state_out = call(
        update_kernel,
        (struct((D, NREL), F32), struct((NREL,), F32)),
        grads,
        squares,
        theirs,
        relation,
        relation_state,
        done,
        core=core,
        far_out=(0,),
        scratch=[
            pltpu.VMEM((HALF, RPAD), F32),
            last,
            pltpu.VMEM((D, NREL), F32),
            dma((8,)),
        ],
        name="update",
    )
    return (slab_out.T[None], state_out, relation_out.T, relation_state_out)


def solution(mesh):
    split = jax.sharding.Mesh(mesh.devices.reshape(4, 4, 2, 2, 2, 2), AXES)
    in_specs = (
        P(REPLICA, BUCKET, None),
        P(REPLICA, BUCKET, None),
        P(REPLICA, BUCKET),
        P(),
        P(),
        P(REPLICA, BUCKET, None, None),
        P(REPLICA, BUCKET, None, None),
        P(REPLICA, BUCKET, None, None),
        P(REPLICA, BUCKET, None, None),
    )
    out_specs = (P(REPLICA, BUCKET, None), P(REPLICA, BUCKET), P(), P())
    return jax.shard_map(
        per_device, mesh=split, in_specs=in_specs, out_specs=out_specs, check_vma=False
    )
```

```python
import jax
import jax.numpy as jnp
from jax import lax
from jax.experimental import pallas as pl
from jax.experimental.pallas import tpu as pltpu
from jax.sharding import PartitionSpec as P

AXES = ("x", "z_hi", "z_lo", "y_lo", "y_hi", "core")
BUCKET = ("x", "z_hi", "z_lo", "y_lo")
REPLICA = ("y_hi", "core")
CUBE = ("x", "z_lo", "y_lo", "y_hi")
OWNERS = 32
D = 400
HALF = 200
EPAD = 1024
NEG = 500
NPAD = 512
ROWS = 512
NREL = 2066
RMAIN = 2048
RPAD = 2176
CUT = 100
PART = 104
EXTRA = NREL - RMAIN
LEVELS = 32000.0
F32 = jnp.float32
BF16 = jnp.bfloat16


def struct(shape, dtype):
    return jax.ShapeDtypeStruct(shape, dtype)


def kept(shape, dtype):
    return pltpu.VMEM(shape, dtype)


def near(array):
    return pltpu.with_memory_space_constraint(array, pltpu.VMEM)


def away(array):
    return pltpu.with_memory_space_constraint(array, pltpu.HBM)


def call(kernel, out_shape, *args, core=None, scratch=(), far_in=(), far_out=(), name, flops=None):
    vmem = pl.BlockSpec(memory_space=pltpu.VMEM)
    far = pl.BlockSpec(memory_space=pltpu.HBM)
    several = isinstance(out_shape, tuple)
    outs = out_shape if several else (out_shape,)
    specs = tuple(far if i in far_out else vmem for i in range(len(outs)))
    in_specs = [far if i in far_in else vmem for i in range(len(args))]
    args = [away(arg) if i in far_in else near(arg) for i, arg in enumerate(args)]
    if core is not None:
        in_specs, args = [pl.BlockSpec(memory_space=pltpu.SMEM)] + in_specs, [core] + args
    return pl.pallas_call(
        kernel,
        out_shape=out_shape,
        in_specs=in_specs,
        out_specs=specs if several else specs[0],
        scratch_shapes=scratch,
        compiler_params=pltpu.CompilerParams(vmem_limit_bytes=32 * 1024 * 1024),
        cost_estimate=flops and pl.CostEstimate(flops=flops, bytes_accessed=0, transcendentals=0),
        name=name,
    )(*args)


def from_next(block):
    count = lax.axis_size(BUCKET)
    return lax.ppermute(block, BUCKET, [((i + 1) % count, i) for i in range(count)])


def swap_core(block):
    return lax.ppermute(block, "core", [(0, 1), (1, 0)])


def dot(a, b, dims=((1,), (0,))):
    return lax.dot_general(a, b, (dims, ((), ())), preferred_element_type=F32)


def places(row, count):
    at = lax.broadcasted_iota(jnp.int32, (count, row.shape[1]), 0).astype(jnp.int16)
    return jnp.where(at == row.astype(jnp.int16), BF16(1), BF16(0))


def target_rows_of(slab_low, ids):
    pos_rows = dot(slab_low, places(ids[1:2], ROWS))
    return pos_rows, dot(slab_low, places(ids[3:4, :NPAD], ROWS)).astype(BF16)


def relation_rows_of(table, ids):
    return dot(table, places(ids[2:3], RPAD))


def edge_terms(heads, pos_rows, neg_rows, rel_rows):
    h_re, h_im = heads[:HALF], heads[HALF:]
    r_re, r_im = rel_rows[:HALF], rel_rows[HALF:]
    prod = jnp.concatenate([h_re * r_re - h_im * r_im, h_re * r_im + h_im * r_re], 0).astype(BF16)
    prod_wide = prod.astype(F32)
    pos = jnp.sum(prod_wide * pos_rows, 0, keepdims=True)
    g_pos = -jax.nn.sigmoid(-pos)
    g_neg = (jax.nn.sigmoid(dot(neg_rows, prod, ((0,), (0,)))) * (1.0 / NEG)).astype(BF16)
    d_prod = g_pos * pos_rows + dot(neg_rows, g_neg)
    p_re, p_im = d_prod[:HALF], d_prod[HALF:]
    d_rel = (p_re * h_re + p_im * h_im, p_im * h_re - p_re * h_im)
    return prod, g_neg, g_pos, d_rel


def row_terms(prod, g_neg, g_pos):
    d_pos = (g_pos * prod.astype(F32)).astype(BF16)
    return d_pos, dot(prod, g_neg, ((1,), (1,))).astype(BF16)


def trained(slab, state, ids, d_pos, d_neg):
    along = ((1,), (1,))
    grad = dot(d_pos, places(ids[1:2], ROWS), along)
    grad = grad + dot(d_neg, places(ids[3:4, :NPAD], ROWS), along)
    state = state + jnp.sum(grad * grad, 0, keepdims=True) * (1.0 / D)
    return slab - grad * (0.1 * lax.rsqrt(state)), state


def prepare_kernel(left, src, dst, rel, neg, ids, next_ids, left_low, wide, places_in, sems):
    sources = (src, dst, rel, neg)
    copies = [pltpu.make_async_copy(left, wide, sems.at[4])]
    copies += [pltpu.make_async_copy(r, places_in[i], sems.at[i]) for i, r in enumerate(sources)]
    for copy in copies:
        copy.start()
    for step_ids in (ids, next_ids):
        step_ids[...] = jnp.full(step_ids.shape, -1, jnp.int32)
    for copy in copies[1:]:
        copy.wait()
    for place, source in enumerate(places_in):
        for step, step_ids in enumerate((ids, next_ids)):
            step_ids[place : place + 1, : source.shape[1]] = source[step : step + 1, :]
    copies[0].wait()
    left_low[...] = wide[...].astype(BF16)


CHUNKS = ((0, 104), (104, 200), (200, 304), (304, 400))


def first_kernel(
    left, ids, slab_far, state_far, relation_far, slab_out, state_out, rel_grad, table, slab, state, relation, sems
):
    copies = [
        pltpu.make_async_copy(slab_far, slab, sems.at[0]),
        pltpu.make_async_copy(state_far, state, sems.at[1]),
    ]
    for i, (start, stop) in enumerate(CHUNKS):
        rows = slice(start, stop)
        copies.append(pltpu.make_async_copy(relation_far.at[rows], relation.at[rows], sems.at[2 + i]))
    for copy in copies:
        copy.start()
    heads = dot(left[...], places(ids[0:1], ROWS))
    for copy in copies[:2]:
        copy.wait()
    pos_rows, neg_rows = target_rows_of(slab[...].astype(BF16), ids)
    for copy in copies[2:]:
        copy.wait()
    table[:, :RMAIN] = relation[:, :RMAIN].astype(BF16)
    table[:, RMAIN:] = jnp.zeros((D, RPAD - RMAIN), BF16)
    table[:, RMAIN:NREL] = relation[:, RMAIN:].astype(BF16)
    rel_rows = relation_rows_of(table[...], ids)
    prod, g_neg, g_pos, d_rel = edge_terms(heads, pos_rows, neg_rows, rel_rows)
    slab_out[...], state_out[...] = trained(
        slab[...], state[...], ids[...], *row_terms(prod, g_neg, g_pos)
    )
    whole = dot(jnp.concatenate(d_rel, 0).astype(BF16), places(ids[2:3], RPAD), ((1,), (1,)))
    for half in range(2):
        rel_grad[half] = whole[half * HALF : half * HALF + HALF]


def between_kernel(slab, table, ids, pos_rows, neg_rows, rel_rows):
    pos_rows[...], neg_rows[...] = target_rows_of(slab[...].astype(BF16), ids)
    rel_rows[...] = relation_rows_of(table[...], ids)


def rel_half(half, ids, d_rel, rel_grad):
    return rel_grad[half] + dot(d_rel[half], places(ids[2:3], RPAD), ((1,), (1,)))


def second_kernel(
    core, left, ids, pos_rows, neg_rows, rel_rows, rel_grad, prod, g_neg, g_pos, d_rel, other, grads
):
    heads = dot(left[...], places(ids[0:1], ROWS))
    prod[...], g_neg[...], g_pos[...], parts = edge_terms(
        heads, pos_rows[...], neg_rows[...], rel_rows[...]
    )
    for half in range(2):
        d_rel[half] = parts[half].astype(BF16)
    grads[...] = rel_half(1 - core[0], ids, d_rel, rel_grad)
    firsts, seconds = last_relations(grads)
    for part in range(OWNERS):
        other[part] = encode(block_of(grads, part), *picked(firsts, seconds, part))


def own_half_kernel(core, ids, rel_grad, d_rel, prod, g_neg, g_pos, mine, d_pos, d_neg):
    mine[...] = rel_half(core[0], ids, d_rel, rel_grad)
    d_pos[...], d_neg[...] = row_terms(prod[...], g_neg[...], g_pos[...])


def target_kernel(after, slab, state, ids, d_pos, d_neg, slab_out, state_out, done):
    slab_out[...], state_out[...] = trained(
        slab[...], state[...], ids[...], d_pos[...], d_neg[...]
    )
    done[...] = after[:, :128]


def power_of(top):
    return jnp.ceil(jnp.log2(jnp.maximum(top, 1e-30)))


def iota(shape, axis):
    return lax.broadcasted_iota(jnp.int32, shape, axis)


def encode(main, first, second):
    row = iota(main.shape, 0)
    main = jnp.where(row < CUT, main, 0.0)
    power = power_of(jnp.max(jnp.abs(main), axis=0, keepdims=True))
    top = jnp.maximum(jnp.abs(first), jnp.abs(second))
    last_power = power_of(jnp.max(top, axis=1, keepdims=True))
    scale = LEVELS * jnp.exp2(-last_power)
    second = jnp.where(iota(second.shape, 1) == 127, last_power, jnp.round(second * scale))
    codes = jnp.round(main * (LEVELS * jnp.exp2(-power)))
    codes = jnp.where(row == CUT, jnp.round(first * scale), codes)
    codes = jnp.where(row == CUT + 1, second, codes)
    codes = jnp.where(row == CUT + 2, power, codes)
    return codes.astype(jnp.int32).astype(jnp.int16)


def decode(codes):
    wide = codes.astype(jnp.int32).astype(F32)
    first, second, power = (wide[CUT + i : CUT + i + 1] for i in range(3))
    step = jnp.exp2(second[:, 127:]) * (1.0 / LEVELS)
    second = jnp.where(iota(second.shape, 1) < HALF - 128, second * step, 0.0)
    main = jnp.where(iota(wide.shape, 0) < CUT, wide, 0.0)
    return main * (jnp.exp2(power) * (1.0 / LEVELS)), first * step, second


def block_of(grads, part):
    tile, low = divmod(part, 2)
    lanes = slice(128 * tile, 128 * tile + 128)
    return pltpu.roll(grads[HALF - PART :, lanes], CUT, 0) if low else grads[:PART, lanes]


def last_relations(grads):
    gap = jnp.zeros((256 - HALF, 128), F32)
    rows = jnp.transpose(jnp.concatenate([grads[:, RMAIN:], gap], 0))
    return rows[:, :128], rows[:, 128:]


def picked(firsts, seconds, part):
    if part >= EXTRA:
        return jnp.zeros((1, 128), F32), jnp.zeros((1, 128), F32)
    return firsts[part : part + 1], seconds[part : part + 1]


def send_kernel(mine, theirs, codes):
    firsts, seconds = last_relations(mine)
    for part in range(OWNERS):
        main, first, second = decode(theirs[part])
        own_first, own_second = picked(firsts, seconds, part)
        codes[part] = encode(block_of(mine, part) + main, own_first + first, own_second + second)


def summed(parts):
    total = decode(parts[0])
    for part in range(1, parts.shape[0]):
        total = tuple(old + new for old, new in zip(total, decode(parts[part])))
    return total


def gather_kernel(parts, codes):
    code = encode(*summed(parts))
    for copy in range(codes.shape[0]):
        codes[copy] = code


def decoded_into(codes, grads, last):
    last[...] = jnp.zeros(last.shape, F32)
    for tile in range(OWNERS // 2):
        lanes = slice(128 * tile, 128 * tile + 128)
        blocks = []
        for part in (2 * tile, 2 * tile + 1):
            block, first, second = decode(codes[part])
            blocks.append(block)
            if part < EXTRA:
                last[part : part + 1, :128] = first
                last[part : part + 1, 128:] = second
        upper, lower = blocks[0], pltpu.roll(blocks[1], PART - CUT, 0)
        grads[: HALF - PART, lanes] = upper[: HALF - PART]
        grads[HALF - PART : PART, lanes] = upper[HALF - PART :] + lower[: 2 * PART - HALF]
        grads[PART:, lanes] = lower[2 * PART - HALF :]
    grads[:, RMAIN:] = jnp.transpose(last[...])[:HALF]
    return jnp.sum(grads[...] * grads[...], 0, keepdims=True)


def ours_kernel(codes, grads, squares, last):
    squares[...] = decoded_into(codes, grads, last)


def update_kernel(
    core, ours, squares, codes, relation, state, done, relation_out, state_out, theirs, last, wide, sems
):
    total = squares[...] + decoded_into(codes, theirs, last)
    new_state = state[...].reshape(1, NREL) + total[:, :NREL] * (1.0 / D)
    rate = 0.2 * lax.rsqrt(new_state)
    state_out[...] = new_state.reshape(NREL)
    copies = []
    for grad, half in ((ours, core[0]), (theirs, 1 - core[0])):
        for start, stop in ((0, 56), (56, 104), (104, 152), (152, 200)):
            rows = pl.ds(pl.multiple_of(half * HALF + start, 8), stop - start)
            wide[rows] = relation[rows] - grad[start:stop, :NREL] * rate
            copies.append(
                pltpu.make_async_copy(wide.at[rows], relation_out.at[rows], sems.at[len(copies)])
            )
            copies[-1].start()
    for copy in copies:
        copy.wait()


def per_device(
    left_embed,
    right_embed,
    right_state,
    relation_embed,
    relation_state,
    source_rows,
    target_rows,
    relation_ids,
    negative_rows,
):
    core = lax.axis_index("core").astype(jnp.int32)[None]
    id_array = kept((8, EPAD), jnp.int32)
    index_arrays = [
        array[0, 0] for array in (source_rows, target_rows, relation_ids, negative_rows)
    ]
    dma = pltpu.SemaphoreType.DMA
    ids, ids_next, left_low = call(
        prepare_kernel,
        (id_array, id_array, kept((D, ROWS), BF16)),
        left_embed[0].T,
        *index_arrays,
        far_in=range(5),
        scratch=[
            pltpu.VMEM((D, ROWS), F32),
            [pltpu.VMEM(array.shape, jnp.int32) for array in index_arrays],
            dma((5,)),
        ],
        name="prepare",
    )
    ids_next = from_next(ids_next)
    left_next = from_next(left_low)
    relation = relation_embed.T
    slab_array, state_array = (D, ROWS), (1, ROWS)
    edge_array = kept((D, EPAD), BF16)
    half_array = kept((HALF, RPAD), F32)
    slab, state, rel_grad, table = call(
        first_kernel,
        (
            kept(slab_array, F32),
            kept(state_array, F32),
            kept((2, HALF, RPAD), F32),
            kept((D, RPAD), BF16),
        ),
        left_low,
        ids,
        right_embed[0].T,
        right_state,
        relation,
        far_in=(2, 3, 4),
        scratch=[
            pltpu.VMEM(slab_array, F32),
            pltpu.VMEM(state_array, F32),
            pltpu.VMEM((D, NREL), F32),
            dma((6,)),
        ],

        name="first",
    )
    wide_array = kept((D, EPAD), F32)
    part = (PART, 128)
    last = pltpu.VMEM((128, 256), F32)
    parts = kept((OWNERS, *part), jnp.int16)
    pos_rows, neg_rows, rel_rows = call(
        between_kernel,
        (wide_array, kept((D, NPAD), BF16), wide_array),
        slab,
        table,
        ids_next,
        flops=2 * 10**10,
        name="between",
    )
    prod, g_neg, g_pos, d_rel, other = call(
        second_kernel,
        (
            edge_array,
            kept((NPAD, EPAD), BF16),
            kept((1, EPAD), F32),
            kept((2, HALF, EPAD), BF16),
            parts,
        ),
        left_next,
        ids_next,
        pos_rows,
        neg_rows,
        rel_rows,
        rel_grad,
        core=core,
        scratch=[pltpu.VMEM((HALF, RPAD), F32)],
        name="second",
    )
    theirs = swap_core(other)
    mine, d_pos, d_neg = call(
        own_half_kernel,
        (half_array, edge_array, kept((D, NPAD), BF16)),
        ids_next,
        rel_grad,
        d_rel,
        prod,
        g_neg,
        g_pos,
        core=core,
        name="own_half",
    )
    sent = call(send_kernel, parts, mine, theirs, name="send")
    got = lax.all_to_all(sent, CUBE, 0, 0, tiled=True)
    count = lax.axis_size("z_hi")
    codes = call(gather_kernel, kept((count, *part), jnp.int16), got, name="gather")
    codes = lax.all_to_all(codes, "z_hi", 0, 0, tiled=True)
    copies = call(gather_kernel, parts, codes, name="spread")
    ours = lax.all_to_all(copies, CUBE, 0, 0, tiled=True)
    theirs = swap_core(ours)
    grads, squares = call(
        ours_kernel, (half_array, kept((1, RPAD), F32)), ours, scratch=[last], name="ours"
    )
    slab_out, state_out, done = call(
        target_kernel,
        (struct(slab_array, F32), struct(state_array, F32), kept((1, 128), F32)),
        squares,
        slab,
        state,
        ids_next,
        d_pos,
        d_neg,
        name="target",
    )
    relation_out, relation_state_out = call(
        update_kernel,
        (struct((D, NREL), F32), struct((NREL,), F32)),
        grads,
        squares,
        theirs,
        relation,
        relation_state,
        done,
        core=core,
        far_out=(0,),
        scratch=[
            pltpu.VMEM((HALF, RPAD), F32),
            last,
            pltpu.VMEM((D, NREL), F32),
            dma((8,)),
        ],
        name="update",
    )
    return (slab_out.T[None], state_out, relation_out.T, relation_state_out)


def solution(mesh):
    split = jax.sharding.Mesh(mesh.devices.reshape(4, 4, 2, 2, 2, 2), AXES)
    in_specs = (
        P(REPLICA, BUCKET, None),
        P(REPLICA, BUCKET, None),
        P(REPLICA, BUCKET),
        P(),
        P(),
        P(REPLICA, BUCKET, None, None),
        P(REPLICA, BUCKET, None, None),
        P(REPLICA, BUCKET, None, None),
        P(REPLICA, BUCKET, None, None),
    )
    out_specs = (P(REPLICA, BUCKET, None), P(REPLICA, BUCKET), P(), P())
    return jax.shard_map(
        per_device, mesh=split, in_specs=in_specs, out_specs=out_specs, check_vma=False
    )
```

```python
import jax
import jax.numpy as jnp
from jax import lax
from jax.experimental import pallas as pl
from jax.experimental.pallas import tpu as pltpu
from jax.sharding import PartitionSpec as P

AXES = ("x", "z_hi", "z_lo", "y_lo", "y_hi", "core")
BUCKET = ("x", "z_hi", "z_lo", "y_lo")
REPLICA = ("y_hi", "core")
CUBE = ("x", "z_lo", "y_lo", "y_hi")
OWNERS = 32
D = 400
HALF = 200
EPAD = 1024
NEG = 500
NPAD = 512
ROWS = 512
NREL = 2066
RMAIN = 2048
RPAD = 2176
CUT = 100
PART = 104
EXTRA = NREL - RMAIN
LEVELS = 32000.0
F32 = jnp.float32
BF16 = jnp.bfloat16


def struct(shape, dtype):
    return jax.ShapeDtypeStruct(shape, dtype)


def kept(shape, dtype):
    return pltpu.VMEM(shape, dtype)


def near(array):
    return pltpu.with_memory_space_constraint(array, pltpu.VMEM)


def away(array):
    return pltpu.with_memory_space_constraint(array, pltpu.HBM)


def call(kernel, out_shape, *args, core=None, scratch=(), far_in=(), far_out=(), name, flops=None):
    vmem = pl.BlockSpec(memory_space=pltpu.VMEM)
    far = pl.BlockSpec(memory_space=pltpu.HBM)
    several = isinstance(out_shape, tuple)
    outs = out_shape if several else (out_shape,)
    specs = tuple(far if i in far_out else vmem for i in range(len(outs)))
    in_specs = [far if i in far_in else vmem for i in range(len(args))]
    args = [away(arg) if i in far_in else near(arg) for i, arg in enumerate(args)]
    if core is not None:
        in_specs, args = [pl.BlockSpec(memory_space=pltpu.SMEM)] + in_specs, [core] + args
    return pl.pallas_call(
        kernel,
        out_shape=out_shape,
        in_specs=in_specs,
        out_specs=specs if several else specs[0],
        scratch_shapes=scratch,
        compiler_params=pltpu.CompilerParams(vmem_limit_bytes=32 * 1024 * 1024),
        cost_estimate=flops and pl.CostEstimate(flops=flops, bytes_accessed=0, transcendentals=0),
        name=name,
    )(*args)


def from_next(block):
    count = lax.axis_size(BUCKET)
    return lax.ppermute(block, BUCKET, [((i + 1) % count, i) for i in range(count)])


def swap_core(block):
    return lax.ppermute(block, "core", [(0, 1), (1, 0)])


def dot(a, b, dims=((1,), (0,))):
    return lax.dot_general(a, b, (dims, ((), ())), preferred_element_type=F32)


def places(row, count):
    at = lax.broadcasted_iota(jnp.int32, (count, row.shape[1]), 0).astype(jnp.int16)
    return jnp.where(at == row.astype(jnp.int16), BF16(1), BF16(0))


def target_rows_of(slab_low, ids):
    pos_rows = dot(slab_low, places(ids[1:2], ROWS))
    return pos_rows, dot(slab_low, places(ids[3:4, :NPAD], ROWS)).astype(BF16)


def relation_rows_of(table, ids):
    return dot(table, places(ids[2:3], RPAD))


def edge_terms(heads, pos_rows, neg_rows, rel_rows):
    h_re, h_im = heads[:HALF], heads[HALF:]
    r_re, r_im = rel_rows[:HALF], rel_rows[HALF:]
    prod = jnp.concatenate([h_re * r_re - h_im * r_im, h_re * r_im + h_im * r_re], 0).astype(BF16)
    prod_wide = prod.astype(F32)
    pos = jnp.sum(prod_wide * pos_rows, 0, keepdims=True)
    g_pos = -jax.nn.sigmoid(-pos)
    g_neg = (jax.nn.sigmoid(dot(neg_rows, prod, ((0,), (0,)))) * (1.0 / NEG)).astype(BF16)
    d_prod = g_pos * pos_rows + dot(neg_rows, g_neg)
    p_re, p_im = d_prod[:HALF], d_prod[HALF:]
    d_rel = (p_re * h_re + p_im * h_im, p_im * h_re - p_re * h_im)
    return prod, g_neg, g_pos, d_rel


def row_terms(prod, g_neg, g_pos):
    d_pos = (g_pos * prod.astype(F32)).astype(BF16)
    return d_pos, dot(prod, g_neg, ((1,), (1,))).astype(BF16)


def trained(slab, state, ids, d_pos, d_neg):
    along = ((1,), (1,))
    grad = dot(d_pos, places(ids[1:2], ROWS), along)
    grad = grad + dot(d_neg, places(ids[3:4, :NPAD], ROWS), along)
    state = state + jnp.sum(grad * grad, 0, keepdims=True) * (1.0 / D)
    return slab - grad * (0.1 * lax.rsqrt(state)), state


def prepare_kernel(left, src, dst, rel, neg, ids, next_ids, left_low, wide, places_in, sems):
    sources = (src, dst, rel, neg)
    copies = [pltpu.make_async_copy(left, wide, sems.at[4])]
    copies += [pltpu.make_async_copy(r, places_in[i], sems.at[i]) for i, r in enumerate(sources)]
    for copy in copies:
        copy.start()
    for step_ids in (ids, next_ids):
        step_ids[...] = jnp.full(step_ids.shape, -1, jnp.int32)
    for copy in copies[1:]:
        copy.wait()
    for place, source in enumerate(places_in):
        for step, step_ids in enumerate((ids, next_ids)):
            step_ids[place : place + 1, : source.shape[1]] = source[step : step + 1, :]
    copies[0].wait()
    left_low[...] = wide[...].astype(BF16)


CHUNKS = ((0, 104), (104, 200), (200, 304), (304, 400))


def first_kernel(
    left, ids, slab_far, state_far, relation_far, slab_out, state_out, rel_grad, table, slab, state, relation, sems
):
    copies = [
        pltpu.make_async_copy(slab_far, slab, sems.at[0]),
        pltpu.make_async_copy(state_far, state, sems.at[1]),
    ]
    for i, (start, stop) in enumerate(CHUNKS):
        rows = slice(start, stop)
        copies.append(pltpu.make_async_copy(relation_far.at[rows], relation.at[rows], sems.at[2 + i]))
    for copy in copies:
        copy.start()
    heads = dot(left[...], places(ids[0:1], ROWS))
    for copy in copies[:2]:
        copy.wait()
    pos_rows, neg_rows = target_rows_of(slab[...].astype(BF16), ids)
    for copy in copies[2:]:
        copy.wait()
    table[:, :RMAIN] = relation[:, :RMAIN].astype(BF16)
    table[:, RMAIN:] = jnp.zeros((D, RPAD - RMAIN), BF16)
    table[:, RMAIN:NREL] = relation[:, RMAIN:].astype(BF16)
    rel_rows = relation_rows_of(table[...], ids)
    prod, g_neg, g_pos, d_rel = edge_terms(heads, pos_rows, neg_rows, rel_rows)
    slab_out[...], state_out[...] = trained(
        slab[...], state[...], ids[...], *row_terms(prod, g_neg, g_pos)
    )
    whole = dot(jnp.concatenate(d_rel, 0).astype(BF16), places(ids[2:3], RPAD), ((1,), (1,)))
    for half in range(2):
        rel_grad[half] = whole[half * HALF : half * HALF + HALF]


def between_kernel(slab, table, ids, pos_rows, neg_rows, rel_rows):
    pos_rows[...], neg_rows[...] = target_rows_of(slab[...].astype(BF16), ids)
    rel_rows[...] = relation_rows_of(table[...], ids)


def rel_half(half, ids, d_rel, rel_grad):
    return rel_grad[half] + dot(d_rel[half], places(ids[2:3], RPAD), ((1,), (1,)))


def second_kernel(
    core, left, ids, pos_rows, neg_rows, rel_rows, rel_grad, prod, g_neg, g_pos, d_rel, other, grads
):
    heads = dot(left[...], places(ids[0:1], ROWS))
    prod[...], g_neg[...], g_pos[...], parts = edge_terms(
        heads, pos_rows[...], neg_rows[...], rel_rows[...]
    )
    for half in range(2):
        d_rel[half] = parts[half].astype(BF16)
    grads[...] = rel_half(1 - core[0], ids, d_rel, rel_grad)
    firsts, seconds = last_relations(grads)
    for part in range(OWNERS):
        other[part] = encode(block_of(grads, part), *picked(firsts, seconds, part))


def own_half_kernel(core, ids, rel_grad, d_rel, prod, g_neg, g_pos, mine, d_pos, d_neg):
    mine[...] = rel_half(core[0], ids, d_rel, rel_grad)
    d_pos[...], d_neg[...] = row_terms(prod[...], g_neg[...], g_pos[...])


def target_kernel(after, slab, state, ids, d_pos, d_neg, slab_out, state_out):
    slab_out[...], state_out[...] = trained(
        slab[...], state[...], ids[...], d_pos[...], d_neg[...]
    )


def power_of(top):
    return jnp.ceil(jnp.log2(jnp.maximum(top, 1e-30)))


def iota(shape, axis):
    return lax.broadcasted_iota(jnp.int32, shape, axis)


def encode(main, first, second):
    row = iota(main.shape, 0)
    main = jnp.where(row < CUT, main, 0.0)
    power = power_of(jnp.max(jnp.abs(main), axis=0, keepdims=True))
    top = jnp.maximum(jnp.abs(first), jnp.abs(second))
    last_power = power_of(jnp.max(top, axis=1, keepdims=True))
    scale = LEVELS * jnp.exp2(-last_power)
    second = jnp.where(iota(second.shape, 1) == 127, last_power, jnp.round(second * scale))
    codes = jnp.round(main * (LEVELS * jnp.exp2(-power)))
    codes = jnp.where(row == CUT, jnp.round(first * scale), codes)
    codes = jnp.where(row == CUT + 1, second, codes)
    codes = jnp.where(row == CUT + 2, power, codes)
    return codes.astype(jnp.int32).astype(jnp.int16)


def decode(codes):
    wide = codes.astype(jnp.int32).astype(F32)
    first, second, power = (wide[CUT + i : CUT + i + 1] for i in range(3))
    step = jnp.exp2(second[:, 127:]) * (1.0 / LEVELS)
    second = jnp.where(iota(second.shape, 1) < HALF - 128, second * step, 0.0)
    main = jnp.where(iota(wide.shape, 0) < CUT, wide, 0.0)
    return main * (jnp.exp2(power) * (1.0 / LEVELS)), first * step, second


def block_of(grads, part):
    tile, low = divmod(part, 2)
    lanes = slice(128 * tile, 128 * tile + 128)
    return pltpu.roll(grads[HALF - PART :, lanes], CUT, 0) if low else grads[:PART, lanes]


def last_relations(grads):
    gap = jnp.zeros((256 - HALF, 128), F32)
    rows = jnp.transpose(jnp.concatenate([grads[:, RMAIN:], gap], 0))
    return rows[:, :128], rows[:, 128:]


def picked(firsts, seconds, part):
    if part >= EXTRA:
        return jnp.zeros((1, 128), F32), jnp.zeros((1, 128), F32)
    return firsts[part : part + 1], seconds[part : part + 1]


def send_kernel(mine, theirs, codes):
    firsts, seconds = last_relations(mine)
    for part in range(OWNERS):
        main, first, second = decode(theirs[part])
        own_first, own_second = picked(firsts, seconds, part)
        codes[part] = encode(block_of(mine, part) + main, own_first + first, own_second + second)


def summed(parts):
    total = decode(parts[0])
    for part in range(1, parts.shape[0]):
        total = tuple(old + new for old, new in zip(total, decode(parts[part])))
    return total


def gather_kernel(parts, codes):
    code = encode(*summed(parts))
    for copy in range(codes.shape[0]):
        codes[copy] = code


def decode_tile(codes, tile, grads, last):
    lanes = slice(128 * tile, 128 * tile + 128)
    blocks = []
    for part in (2 * tile, 2 * tile + 1):
        block, first, second = decode(codes[part])
        blocks.append(block)
        if part < EXTRA:
            last[part : part + 1, :128] = first
            last[part : part + 1, 128:] = second
    upper, lower = blocks[0], pltpu.roll(blocks[1], PART - CUT, 0)
    grads[: HALF - PART, lanes] = upper[: HALF - PART]
    grads[HALF - PART : PART, lanes] = upper[HALF - PART :] + lower[: 2 * PART - HALF]
    grads[PART:, lanes] = lower[2 * PART - HALF :]


def squares_of(grads):
    return jnp.sum(grads * grads, 0, keepdims=True)


def ours_kernel(codes, grads, squares, last):
    last[...] = jnp.zeros(last.shape, F32)
    for tile in range(OWNERS // 2):
        decode_tile(codes, tile, grads, last)
    grads[:, RMAIN:] = jnp.transpose(last[...])[:HALF]
    squares[...] = squares_of(grads[...])


GROUPS = ((0, 512), (512, 1024), (1024, 1536), (1536, RPAD))


def update_kernel(
    core,
    ours,
    squares,
    codes,
    relation,
    state,
    slab,
    relation_out,
    slab_out,
    state_out,
    theirs,
    last,
    wide,
    sems,
):
    copies = [pltpu.make_async_copy(slab, slab_out, sems.at[len(GROUPS)])]
    copies[0].start()
    last[...] = jnp.zeros(last.shape, F32)
    old_state = state[...].reshape(1, NREL)
    halves = [pl.ds(pl.multiple_of(half * HALF, 8), HALF) for half in (core[0], 1 - core[0])]
    states = []
    for place, (start, stop) in enumerate(GROUPS):
        for tile in range(start // 128, min(stop, RMAIN) // 128):
            decode_tile(codes, tile, theirs, last)
        if stop == RPAD:
            theirs[:, RMAIN:] = jnp.transpose(last[...])[:HALF]
        total = squares[:, start:stop] + squares_of(theirs[:, start:stop])
        end = min(stop, NREL)
        lanes = slice(start, end)
        states.append(old_state[:, lanes] + total[:, : end - start] * (1.0 / D))
        rate = 0.2 * lax.rsqrt(states[-1])
        for rows, grad in zip(halves, (ours, theirs)):
            wide[rows, lanes] = relation[rows, lanes] - grad[:, lanes] * rate
        copies.append(
            pltpu.make_async_copy(wide.at[:, lanes], relation_out.at[:, lanes], sems.at[place])
        )
        copies[-1].start()
    state_out[...] = jnp.concatenate(states, 1).reshape(NREL)
    for copy in copies:
        copy.wait()


def per_device(
    left_embed,
    right_embed,
    right_state,
    relation_embed,
    relation_state,
    source_rows,
    target_rows,
    relation_ids,
    negative_rows,
):
    core = lax.axis_index("core").astype(jnp.int32)[None]
    id_array = kept((8, EPAD), jnp.int32)
    index_arrays = [
        array[0, 0] for array in (source_rows, target_rows, relation_ids, negative_rows)
    ]
    dma = pltpu.SemaphoreType.DMA
    ids, ids_next, left_low = call(
        prepare_kernel,
        (id_array, id_array, kept((D, ROWS), BF16)),
        left_embed[0].T,
        *index_arrays,
        far_in=range(5),
        scratch=[
            pltpu.VMEM((D, ROWS), F32),
            [pltpu.VMEM(array.shape, jnp.int32) for array in index_arrays],
            dma((5,)),
        ],
        name="prepare",
    )
    ids_next = from_next(ids_next)
    left_next = from_next(left_low)
    relation = relation_embed.T
    slab_array, state_array = (D, ROWS), (1, ROWS)
    edge_array = kept((D, EPAD), BF16)
    half_array = kept((HALF, RPAD), F32)
    slab, state, rel_grad, table = call(
        first_kernel,
        (
            kept(slab_array, F32),
            kept(state_array, F32),
            kept((2, HALF, RPAD), F32),
            kept((D, RPAD), BF16),
        ),
        left_low,
        ids,
        right_embed[0].T,
        right_state,
        relation,
        far_in=(2, 3, 4),
        scratch=[
            pltpu.VMEM(slab_array, F32),
            pltpu.VMEM(state_array, F32),
            pltpu.VMEM((D, NREL), F32),
            dma((6,)),
        ],

        name="first",
    )
    wide_array = kept((D, EPAD), F32)
    part = (PART, 128)
    last = pltpu.VMEM((128, 256), F32)
    parts = kept((OWNERS, *part), jnp.int16)
    pos_rows, neg_rows, rel_rows = call(
        between_kernel,
        (wide_array, kept((D, NPAD), BF16), wide_array),
        slab,
        table,
        ids_next,
        flops=2 * 10**10,
        name="between",
    )
    prod, g_neg, g_pos, d_rel, other = call(
        second_kernel,
        (
            edge_array,
            kept((NPAD, EPAD), BF16),
            kept((1, EPAD), F32),
            kept((2, HALF, EPAD), BF16),
            parts,
        ),
        left_next,
        ids_next,
        pos_rows,
        neg_rows,
        rel_rows,
        rel_grad,
        core=core,
        scratch=[pltpu.VMEM((HALF, RPAD), F32)],
        name="second",
    )
    theirs = swap_core(other)
    mine, d_pos, d_neg = call(
        own_half_kernel,
        (half_array, edge_array, kept((D, NPAD), BF16)),
        ids_next,
        rel_grad,
        d_rel,
        prod,
        g_neg,
        g_pos,
        core=core,
        name="own_half",
    )
    sent = call(send_kernel, parts, mine, theirs, name="send")
    got = lax.all_to_all(sent, CUBE, 0, 0, tiled=True)
    count = lax.axis_size("z_hi")
    codes = call(gather_kernel, kept((count, *part), jnp.int16), got, name="gather")
    codes = lax.all_to_all(codes, "z_hi", 0, 0, tiled=True)
    copies = call(gather_kernel, parts, codes, name="spread")
    ours = lax.all_to_all(copies, CUBE, 0, 0, tiled=True)
    theirs = swap_core(ours)
    grads, squares = call(
        ours_kernel, (half_array, kept((1, RPAD), F32)), ours, scratch=[last], name="ours"
    )
    slab, state_out = call(
        target_kernel,
        (kept(slab_array, F32), struct(state_array, F32)),
        squares,
        slab,
        state,
        ids_next,
        d_pos,
        d_neg,
        name="target",
    )
    relation_out, slab_out, relation_state_out = call(
        update_kernel,
        (struct((D, NREL), F32), struct(slab_array, F32), struct((NREL,), F32)),
        grads,
        squares,
        theirs,
        relation,
        relation_state,
        slab,
        core=core,
        far_out=(0, 1),
        scratch=[
            pltpu.VMEM((HALF, RPAD), F32),
            last,
            pltpu.VMEM((D, NREL), F32),
            dma((len(GROUPS) + 1,)),
        ],
        name="update",
    )
    return (slab_out.T[None], state_out, relation_out.T, relation_state_out)


def solution(mesh):
    split = jax.sharding.Mesh(mesh.devices.reshape(4, 4, 2, 2, 2, 2), AXES)
    in_specs = (
        P(REPLICA, BUCKET, None),
        P(REPLICA, BUCKET, None),
        P(REPLICA, BUCKET),
        P(),
        P(),
        P(REPLICA, BUCKET, None, None),
        P(REPLICA, BUCKET, None, None),
        P(REPLICA, BUCKET, None, None),
        P(REPLICA, BUCKET, None, None),
    )
    out_specs = (P(REPLICA, BUCKET, None), P(REPLICA, BUCKET), P(), P())
    return jax.shard_map(
        per_device, mesh=split, in_specs=in_specs, out_specs=out_specs, check_vma=False
    )
```

```python
import jax
import jax.numpy as jnp
from jax import lax
from jax.experimental import pallas as pl
from jax.experimental.pallas import tpu as pltpu
from jax.sharding import PartitionSpec as P

AXES = ("x", "z_hi", "z_lo", "y_lo", "y_hi", "core")
BUCKET = ("x", "z_hi", "z_lo", "y_lo")
REPLICA = ("y_hi", "core")
CUBE = ("x", "z_lo", "y_lo", "y_hi")
OWNERS = 32
D = 400
HALF = 200
EPAD = 1024
NEG = 500
NPAD = 512
ROWS = 512
NREL = 2066
RMAIN = 2048
RPAD = 2176
CUT = 100
PART = 104
EXTRA = NREL - RMAIN
LEVELS = 32000.0
F32 = jnp.float32
BF16 = jnp.bfloat16


def struct(shape, dtype):
    return jax.ShapeDtypeStruct(shape, dtype)


def kept(shape, dtype):
    return pltpu.VMEM(shape, dtype)


def near(array):
    return pltpu.with_memory_space_constraint(array, pltpu.VMEM)


def away(array):
    return pltpu.with_memory_space_constraint(array, pltpu.HBM)


def call(kernel, out_shape, *args, core=None, scratch=(), far_in=(), far_out=(), name, flops=None):
    vmem = pl.BlockSpec(memory_space=pltpu.VMEM)
    far = pl.BlockSpec(memory_space=pltpu.HBM)
    several = isinstance(out_shape, tuple)
    outs = out_shape if several else (out_shape,)
    specs = tuple(far if i in far_out else vmem for i in range(len(outs)))
    in_specs = [far if i in far_in else vmem for i in range(len(args))]
    args = [away(arg) if i in far_in else near(arg) for i, arg in enumerate(args)]
    if core is not None:
        in_specs, args = [pl.BlockSpec(memory_space=pltpu.SMEM)] + in_specs, [core] + args
    return pl.pallas_call(
        kernel,
        out_shape=out_shape,
        in_specs=in_specs,
        out_specs=specs if several else specs[0],
        scratch_shapes=scratch,
        compiler_params=pltpu.CompilerParams(vmem_limit_bytes=32 * 1024 * 1024),
        cost_estimate=flops and pl.CostEstimate(flops=flops, bytes_accessed=0, transcendentals=0),
        name=name,
    )(*args)


def from_next(block):
    count = lax.axis_size(BUCKET)
    return lax.ppermute(block, BUCKET, [((i + 1) % count, i) for i in range(count)])


def swap_core(block):
    return lax.ppermute(block, "core", [(0, 1), (1, 0)])


def dot(a, b, dims=((1,), (0,))):
    return lax.dot_general(a, b, (dims, ((), ())), preferred_element_type=F32)


def places(row, count):
    at = lax.broadcasted_iota(jnp.int32, (count, row.shape[1]), 0).astype(jnp.int16)
    return jnp.where(at == row.astype(jnp.int16), BF16(1), BF16(0))


def target_rows_of(slab_low, ids):
    pos_rows = dot(slab_low, places(ids[1:2], ROWS))
    return pos_rows, dot(slab_low, places(ids[3:4, :NPAD], ROWS)).astype(BF16)


def relation_rows_of(table, ids):
    return dot(table, places(ids[2:3], RPAD))


def edge_terms(heads, pos_rows, neg_rows, rel_rows):
    h_re, h_im = heads[:HALF], heads[HALF:]
    r_re, r_im = rel_rows[:HALF], rel_rows[HALF:]
    prod = jnp.concatenate([h_re * r_re - h_im * r_im, h_re * r_im + h_im * r_re], 0).astype(BF16)
    prod_wide = prod.astype(F32)
    pos = jnp.sum(prod_wide * pos_rows, 0, keepdims=True)
    g_pos = -jax.nn.sigmoid(-pos)
    g_neg = (jax.nn.sigmoid(dot(neg_rows, prod, ((0,), (0,)))) * (1.0 / NEG)).astype(BF16)
    d_prod = g_pos * pos_rows + dot(neg_rows, g_neg)
    p_re, p_im = d_prod[:HALF], d_prod[HALF:]
    d_rel = (p_re * h_re + p_im * h_im, p_im * h_re - p_re * h_im)
    return prod, g_neg, g_pos, d_rel


def row_terms(prod, g_neg, g_pos):
    d_pos = (g_pos * prod.astype(F32)).astype(BF16)
    return d_pos, dot(prod, g_neg, ((1,), (1,))).astype(BF16)


def trained(slab, state, ids, d_pos, d_neg):
    along = ((1,), (1,))
    grad = dot(d_pos, places(ids[1:2], ROWS), along)
    grad = grad + dot(d_neg, places(ids[3:4, :NPAD], ROWS), along)
    state = state + jnp.sum(grad * grad, 0, keepdims=True) * (1.0 / D)
    return slab - grad * (0.1 * lax.rsqrt(state)), state


def prepare_kernel(left, src, dst, rel, neg, ids, next_ids, left_low, wide, places_in, sems):
    sources = (src, dst, rel, neg)
    copies = [pltpu.make_async_copy(left, wide, sems.at[4])]
    copies += [pltpu.make_async_copy(r, places_in[i], sems.at[i]) for i, r in enumerate(sources)]
    for copy in copies:
        copy.start()
    for step_ids in (ids, next_ids):
        step_ids[...] = jnp.full(step_ids.shape, -1, jnp.int32)
    for copy in copies[1:]:
        copy.wait()
    for place, source in enumerate(places_in):
        for step, step_ids in enumerate((ids, next_ids)):
            step_ids[place : place + 1, : source.shape[1]] = source[step : step + 1, :]
    copies[0].wait()
    left_low[...] = wide[...].astype(BF16)


GROUPS = ((0, 512), (512, 1024), (1024, 1536), (1536, RPAD))


def first_kernel(
    left, ids, slab_far, state_far, relation_far, slab_out, state_out, rel_grad, table, slab, state, relation, sems
):
    copies = [
        pltpu.make_async_copy(slab_far, slab, sems.at[0]),
        pltpu.make_async_copy(state_far, state, sems.at[1]),
    ]
    for i, (start, stop) in enumerate(GROUPS):
        at = (slice(None), slice(start, min(stop, NREL)))
        copies.append(pltpu.make_async_copy(relation_far.at[at], relation.at[at], sems.at[2 + i]))
    for copy in copies:
        copy.start()
    heads = dot(left[...], places(ids[0:1], ROWS))
    for copy in copies[:2]:
        copy.wait()
    pos_rows, neg_rows = target_rows_of(slab[...].astype(BF16), ids)
    table[:, RMAIN:] = jnp.zeros((D, RPAD - RMAIN), BF16)
    rel_rows = 0.0
    for copy, (start, stop) in zip(copies[2:], GROUPS):
        copy.wait()
        end = min(stop, NREL)
        table[:, start:end] = relation[:, start:end].astype(BF16)
        found = places(ids[2:3] - start, stop - start)
        rel_rows = rel_rows + dot(table[:, start:stop], found)
    prod, g_neg, g_pos, d_rel = edge_terms(heads, pos_rows, neg_rows, rel_rows)
    slab_out[...], state_out[...] = trained(
        slab[...], state[...], ids[...], *row_terms(prod, g_neg, g_pos)
    )
    whole = dot(jnp.concatenate(d_rel, 0).astype(BF16), places(ids[2:3], RPAD), ((1,), (1,)))
    for half in range(2):
        rel_grad[half] = whole[half * HALF : half * HALF + HALF]


def between_kernel(slab, table, ids, pos_rows, neg_rows, rel_rows):
    pos_rows[...], neg_rows[...] = target_rows_of(slab[...].astype(BF16), ids)
    rel_rows[...] = relation_rows_of(table[...], ids)


def rel_half(half, ids, d_rel, rel_grad):
    return rel_grad[half] + dot(d_rel[half], places(ids[2:3], RPAD), ((1,), (1,)))


def second_kernel(
    core, left, ids, pos_rows, neg_rows, rel_rows, rel_grad, prod, g_neg, g_pos, d_rel, other, grads
):
    heads = dot(left[...], places(ids[0:1], ROWS))
    prod[...], g_neg[...], g_pos[...], parts = edge_terms(
        heads, pos_rows[...], neg_rows[...], rel_rows[...]
    )
    for half in range(2):
        d_rel[half] = parts[half].astype(BF16)
    grads[...] = rel_half(1 - core[0], ids, d_rel, rel_grad)
    firsts, seconds = last_relations(grads)
    for part in range(OWNERS):
        other[part] = encode(block_of(grads, part), *picked(firsts, seconds, part))


def own_half_kernel(core, ids, rel_grad, d_rel, prod, g_neg, g_pos, mine, d_pos, d_neg):
    mine[...] = rel_half(core[0], ids, d_rel, rel_grad)
    d_pos[...], d_neg[...] = row_terms(prod[...], g_neg[...], g_pos[...])


def target_kernel(after, slab, state, ids, d_pos, d_neg, slab_out, state_out):
    slab_out[...], state_out[...] = trained(
        slab[...], state[...], ids[...], d_pos[...], d_neg[...]
    )


def power_of(top):
    return jnp.ceil(jnp.log2(jnp.maximum(top, 1e-30)))


def iota(shape, axis):
    return lax.broadcasted_iota(jnp.int32, shape, axis)


def encode(main, first, second):
    row = iota(main.shape, 0)
    main = jnp.where(row < CUT, main, 0.0)
    power = power_of(jnp.max(jnp.abs(main), axis=0, keepdims=True))
    top = jnp.maximum(jnp.abs(first), jnp.abs(second))
    last_power = power_of(jnp.max(top, axis=1, keepdims=True))
    scale = LEVELS * jnp.exp2(-last_power)
    second = jnp.where(iota(second.shape, 1) == 127, last_power, jnp.round(second * scale))
    codes = jnp.round(main * (LEVELS * jnp.exp2(-power)))
    codes = jnp.where(row == CUT, jnp.round(first * scale), codes)
    codes = jnp.where(row == CUT + 1, second, codes)
    codes = jnp.where(row == CUT + 2, power, codes)
    return codes.astype(jnp.int32).astype(jnp.int16)


def decode(codes):
    wide = codes.astype(jnp.int32).astype(F32)
    first, second, power = (wide[CUT + i : CUT + i + 1] for i in range(3))
    step = jnp.exp2(second[:, 127:]) * (1.0 / LEVELS)
    second = jnp.where(iota(second.shape, 1) < HALF - 128, second * step, 0.0)
    main = jnp.where(iota(wide.shape, 0) < CUT, wide, 0.0)
    return main * (jnp.exp2(power) * (1.0 / LEVELS)), first * step, second


def block_of(grads, part):
    tile, low = divmod(part, 2)
    lanes = slice(128 * tile, 128 * tile + 128)
    return pltpu.roll(grads[HALF - PART :, lanes], CUT, 0) if low else grads[:PART, lanes]


def last_relations(grads):
    gap = jnp.zeros((256 - HALF, 128), F32)
    rows = jnp.transpose(jnp.concatenate([grads[:, RMAIN:], gap], 0))
    return rows[:, :128], rows[:, 128:]


def picked(firsts, seconds, part):
    if part >= EXTRA:
        return jnp.zeros((1, 128), F32), jnp.zeros((1, 128), F32)
    return firsts[part : part + 1], seconds[part : part + 1]


def send_kernel(mine, theirs, codes):
    firsts, seconds = last_relations(mine)
    for part in range(OWNERS):
        main, first, second = decode(theirs[part])
        own_first, own_second = picked(firsts, seconds, part)
        codes[part] = encode(block_of(mine, part) + main, own_first + first, own_second + second)


def summed(parts):
    total = decode(parts[0])
    for part in range(1, parts.shape[0]):
        total = tuple(old + new for old, new in zip(total, decode(parts[part])))
    return total


def gather_kernel(parts, codes):
    code = encode(*summed(parts))
    for copy in range(codes.shape[0]):
        codes[copy] = code


def decode_tile(codes, tile, grads, last):
    lanes = slice(128 * tile, 128 * tile + 128)
    blocks = []
    for part in (2 * tile, 2 * tile + 1):
        block, first, second = decode(codes[part])
        blocks.append(block)
        if part < EXTRA:
            last[part : part + 1, :128] = first
            last[part : part + 1, 128:] = second
    upper, lower = blocks[0], pltpu.roll(blocks[1], PART - CUT, 0)
    grads[: HALF - PART, lanes] = upper[: HALF - PART]
    grads[HALF - PART : PART, lanes] = upper[HALF - PART :] + lower[: 2 * PART - HALF]
    grads[PART:, lanes] = lower[2 * PART - HALF :]


def squares_of(grads):
    return jnp.sum(grads * grads, 0, keepdims=True)


def ours_kernel(codes, grads, squares, last):
    last[...] = jnp.zeros(last.shape, F32)
    for tile in range(OWNERS // 2):
        decode_tile(codes, tile, grads, last)
    grads[:, RMAIN:] = jnp.transpose(last[...])[:HALF]
    squares[...] = squares_of(grads[...])


def update_kernel(
    core,
    ours,
    squares,
    codes,
    relation,
    state,
    slab,
    relation_out,
    slab_out,
    state_out,
    theirs,
    last,
    wide,
    sems,
):
    copies = [pltpu.make_async_copy(slab, slab_out, sems.at[len(GROUPS)])]
    copies[0].start()
    last[...] = jnp.zeros(last.shape, F32)
    old_state = state[...].reshape(1, NREL)
    halves = [pl.ds(pl.multiple_of(half * HALF, 8), HALF) for half in (core[0], 1 - core[0])]
    states = []
    for place, (start, stop) in enumerate(GROUPS):
        for tile in range(start // 128, min(stop, RMAIN) // 128):
            decode_tile(codes, tile, theirs, last)
        if stop == RPAD:
            theirs[:, RMAIN:] = jnp.transpose(last[...])[:HALF]
        total = squares[:, start:stop] + squares_of(theirs[:, start:stop])
        end = min(stop, NREL)
        lanes = slice(start, end)
        states.append(old_state[:, lanes] + total[:, : end - start] * (1.0 / D))
        rate = 0.2 * lax.rsqrt(states[-1])
        for rows, grad in zip(halves, (ours, theirs)):
            wide[rows, lanes] = relation[rows, lanes] - grad[:, lanes] * rate
        copies.append(
            pltpu.make_async_copy(wide.at[:, lanes], relation_out.at[:, lanes], sems.at[place])
        )
        copies[-1].start()
    state_out[...] = jnp.concatenate(states, 1).reshape(NREL)
    for copy in copies:
        copy.wait()


def per_device(
    left_embed,
    right_embed,
    right_state,
    relation_embed,
    relation_state,
    source_rows,
    target_rows,
    relation_ids,
    negative_rows,
):
    core = lax.axis_index("core").astype(jnp.int32)[None]
    id_array = kept((4, EPAD), jnp.int32)
    index_arrays = [
        array[0, 0] for array in (source_rows, target_rows, relation_ids, negative_rows)
    ]
    dma = pltpu.SemaphoreType.DMA
    ids, ids_next, left_low = call(
        prepare_kernel,
        (id_array, id_array, kept((D, ROWS), BF16)),
        left_embed[0].T,
        *index_arrays,
        far_in=range(5),
        scratch=[
            pltpu.VMEM((D, ROWS), F32),
            [pltpu.VMEM(array.shape, jnp.int32) for array in index_arrays],
            dma((5,)),
        ],
        name="prepare",
    )
    ids_next = from_next(ids_next)
    left_next = from_next(left_low)
    relation = relation_embed.T
    slab_array, state_array = (D, ROWS), (1, ROWS)
    edge_array = kept((D, EPAD), BF16)
    half_array = kept((HALF, RPAD), F32)
    slab, state, rel_grad, table = call(
        first_kernel,
        (
            kept(slab_array, F32),
            kept(state_array, F32),
            kept((2, HALF, RPAD), F32),
            kept((D, RPAD), BF16),
        ),
        left_low,
        ids,
        right_embed[0].T,
        right_state,
        relation,
        far_in=(2, 3, 4),
        scratch=[
            pltpu.VMEM(slab_array, F32),
            pltpu.VMEM(state_array, F32),
            pltpu.VMEM((D, NREL), F32),
            dma((6,)),
        ],

        name="first",
    )
    wide_array = kept((D, EPAD), F32)
    part = (PART, 128)
    last = pltpu.VMEM((128, 256), F32)
    parts = kept((OWNERS, *part), jnp.int16)
    pos_rows, neg_rows, rel_rows = call(
        between_kernel,
        (wide_array, kept((D, NPAD), BF16), wide_array),
        slab,
        table,
        ids_next,
        flops=2 * 10**10,
        name="between",
    )
    prod, g_neg, g_pos, d_rel, other = call(
        second_kernel,
        (
            edge_array,
            kept((NPAD, EPAD), BF16),
            kept((1, EPAD), F32),
            kept((2, HALF, EPAD), BF16),
            parts,
        ),
        left_next,
        ids_next,
        pos_rows,
        neg_rows,
        rel_rows,
        rel_grad,
        core=core,
        scratch=[pltpu.VMEM((HALF, RPAD), F32)],
        name="second",
    )
    theirs = swap_core(other)
    mine, d_pos, d_neg = call(
        own_half_kernel,
        (half_array, edge_array, kept((D, NPAD), BF16)),
        ids_next,
        rel_grad,
        d_rel,
        prod,
        g_neg,
        g_pos,
        core=core,
        name="own_half",
    )
    sent = call(send_kernel, parts, mine, theirs, name="send")
    got = lax.all_to_all(sent, CUBE, 0, 0, tiled=True)
    count = lax.axis_size("z_hi")
    codes = call(gather_kernel, kept((count, *part), jnp.int16), got, name="gather")
    codes = lax.all_to_all(codes, "z_hi", 0, 0, tiled=True)
    copies = call(gather_kernel, parts, codes, name="spread")
    ours = lax.all_to_all(copies, CUBE, 0, 0, tiled=True)
    theirs = swap_core(ours)
    grads, squares = call(
        ours_kernel, (half_array, kept((1, RPAD), F32)), ours, scratch=[last], name="ours"
    )
    slab, state_out = call(
        target_kernel,
        (kept(slab_array, F32), struct(state_array, F32)),
        squares,
        slab,
        state,
        ids_next,
        d_pos,
        d_neg,
        name="target",
    )
    relation_out, slab_out, relation_state_out = call(
        update_kernel,
        (struct((D, NREL), F32), struct(slab_array, F32), struct((NREL,), F32)),
        grads,
        squares,
        theirs,
        relation,
        relation_state,
        slab,
        core=core,
        far_out=(0, 1),
        scratch=[
            pltpu.VMEM((HALF, RPAD), F32),
            last,
            pltpu.VMEM((D, NREL), F32),
            dma((len(GROUPS) + 1,)),
        ],
        name="update",
    )
    return (slab_out.T[None], state_out, relation_out.T, relation_state_out)


def solution(mesh):
    split = jax.sharding.Mesh(mesh.devices.reshape(4, 4, 2, 2, 2, 2), AXES)
    in_specs = (
        P(REPLICA, BUCKET, None),
        P(REPLICA, BUCKET, None),
        P(REPLICA, BUCKET),
        P(),
        P(),
        P(REPLICA, BUCKET, None, None),
        P(REPLICA, BUCKET, None, None),
        P(REPLICA, BUCKET, None, None),
        P(REPLICA, BUCKET, None, None),
    )
    out_specs = (P(REPLICA, BUCKET, None), P(REPLICA, BUCKET), P(), P())
    return jax.shard_map(
        per_device, mesh=split, in_specs=in_specs, out_specs=out_specs, check_vma=False
    )
```

```python
import jax
import jax.numpy as jnp
from jax import lax
from jax.experimental import pallas as pl
from jax.experimental.pallas import tpu as pltpu
from jax.sharding import PartitionSpec as P

AXES = ("x", "z_hi", "z_lo", "y_lo", "y_hi", "core")
BUCKET = ("x", "z_hi", "z_lo", "y_lo")
REPLICA = ("y_hi", "core")
CUBE = ("x", "z_lo", "y_lo", "y_hi")
OWNERS = 32
D = 400
HALF = 200
EPAD = 1024
NEG = 500
NPAD = 512
ROWS = 512
NREL = 2066
RMAIN = 2048
RPAD = 2176
CUT = 100
PART = 104
EXTRA = NREL - RMAIN
LEVELS = 32000.0
F32 = jnp.float32
BF16 = jnp.bfloat16


def struct(shape, dtype):
    return jax.ShapeDtypeStruct(shape, dtype)


def kept(shape, dtype):
    return pltpu.VMEM(shape, dtype)


def near(array):
    return pltpu.with_memory_space_constraint(array, pltpu.VMEM)


def away(array):
    return pltpu.with_memory_space_constraint(array, pltpu.HBM)


def call(kernel, out_shape, *args, core=None, scratch=(), far_in=(), far_out=(), name, flops=None):
    vmem = pl.BlockSpec(memory_space=pltpu.VMEM)
    far = pl.BlockSpec(memory_space=pltpu.HBM)
    several = isinstance(out_shape, tuple)
    outs = out_shape if several else (out_shape,)
    specs = tuple(far if i in far_out else vmem for i in range(len(outs)))
    in_specs = [far if i in far_in else vmem for i in range(len(args))]
    args = [away(arg) if i in far_in else near(arg) for i, arg in enumerate(args)]
    if core is not None:
        in_specs, args = [pl.BlockSpec(memory_space=pltpu.SMEM)] + in_specs, [core] + args
    return pl.pallas_call(
        kernel,
        out_shape=out_shape,
        in_specs=in_specs,
        out_specs=specs if several else specs[0],
        scratch_shapes=scratch,
        compiler_params=pltpu.CompilerParams(vmem_limit_bytes=32 * 1024 * 1024),
        cost_estimate=flops and pl.CostEstimate(flops=flops, bytes_accessed=0, transcendentals=0),
        name=name,
    )(*args)


def from_next(block):
    count = lax.axis_size(BUCKET)
    return lax.ppermute(block, BUCKET, [((i + 1) % count, i) for i in range(count)])


def swap_core(block):
    return lax.ppermute(block, "core", [(0, 1), (1, 0)])


def dot(a, b, dims=((1,), (0,))):
    return lax.dot_general(a, b, (dims, ((), ())), preferred_element_type=F32)


def places(row, count):
    at = lax.broadcasted_iota(jnp.int32, (count, row.shape[1]), 0).astype(jnp.int16)
    return jnp.where(at == row.astype(jnp.int16), BF16(1), BF16(0))


def target_rows_of(slab_low, ids):
    pos_rows = dot(slab_low, places(ids[1:2], ROWS))
    return pos_rows, dot(slab_low, places(ids[3:4, :NPAD], ROWS)).astype(BF16)


def relation_rows_of(table, ids):
    return dot(table, places(ids[2:3], RPAD))


def edge_terms(heads, pos_rows, neg_rows, rel_rows):
    h_re, h_im = heads[:HALF], heads[HALF:]
    r_re, r_im = rel_rows[:HALF], rel_rows[HALF:]
    prod = jnp.concatenate([h_re * r_re - h_im * r_im, h_re * r_im + h_im * r_re], 0).astype(BF16)
    prod_wide = prod.astype(F32)
    pos = jnp.sum(prod_wide * pos_rows, 0, keepdims=True)
    g_pos = -jax.nn.sigmoid(-pos)
    g_neg = (jax.nn.sigmoid(dot(neg_rows, prod, ((0,), (0,)))) * (1.0 / NEG)).astype(BF16)
    d_prod = g_pos * pos_rows + dot(neg_rows, g_neg)
    p_re, p_im = d_prod[:HALF], d_prod[HALF:]
    d_rel = (p_re * h_re + p_im * h_im, p_im * h_re - p_re * h_im)
    return prod, g_neg, g_pos, d_rel


def row_terms(prod, g_neg, g_pos):
    d_pos = (g_pos * prod.astype(F32)).astype(BF16)
    return d_pos, dot(prod, g_neg, ((1,), (1,))).astype(BF16)


def trained(slab, state, ids, d_pos, d_neg):
    along = ((1,), (1,))
    grad = dot(d_pos, places(ids[1:2], ROWS), along)
    grad = grad + dot(d_neg, places(ids[3:4, :NPAD], ROWS), along)
    state = state + jnp.sum(grad * grad, 0, keepdims=True) * (1.0 / D)
    return slab - grad * (0.1 * lax.rsqrt(state)), state


def prepare_kernel(left, src, dst, rel, neg, ids, next_ids, left_low, wide, places_in, sems):
    sources = (src, dst, rel, neg)
    copies = [pltpu.make_async_copy(left, wide, sems.at[4])]
    copies += [pltpu.make_async_copy(r, places_in[i], sems.at[i]) for i, r in enumerate(sources)]
    for copy in copies:
        copy.start()
    for step_ids in (ids, next_ids):
        step_ids[...] = jnp.full(step_ids.shape, -1, jnp.int32)
    for copy in copies[1:]:
        copy.wait()
    for place, source in enumerate(places_in):
        for step, step_ids in enumerate((ids, next_ids)):
            step_ids[place : place + 1, : source.shape[1]] = source[step : step + 1, :]
    copies[0].wait()
    left_low[...] = wide[...].astype(BF16)


CHUNKS = ((0, 104), (104, 200), (200, 304), (304, 400))


def first_kernel(
    left, ids, slab_far, state_far, relation_far, slab_out, state_out, rel_grad, table, slab, state, relation, sems
):
    copies = [
        pltpu.make_async_copy(slab_far, slab, sems.at[0]),
        pltpu.make_async_copy(state_far, state, sems.at[1]),
    ]
    for i, (start, stop) in enumerate(CHUNKS):
        rows = slice(start, stop)
        copies.append(pltpu.make_async_copy(relation_far.at[rows], relation.at[rows], sems.at[2 + i]))
    for copy in copies:
        copy.start()
    heads = dot(left[...], places(ids[0:1], ROWS))
    for copy in copies[:2]:
        copy.wait()
    pos_rows, neg_rows = target_rows_of(slab[...].astype(BF16), ids)
    for copy in copies[2:]:
        copy.wait()
    table[:, :RMAIN] = relation[:, :RMAIN].astype(BF16)
    table[:, RMAIN:] = jnp.zeros((D, RPAD - RMAIN), BF16)
    table[:, RMAIN:NREL] = relation[:, RMAIN:].astype(BF16)
    rel_rows = relation_rows_of(table[...], ids)
    prod, g_neg, g_pos, d_rel = edge_terms(heads, pos_rows, neg_rows, rel_rows)
    slab_out[...], state_out[...] = trained(
        slab[...], state[...], ids[...], *row_terms(prod, g_neg, g_pos)
    )
    whole = dot(jnp.concatenate(d_rel, 0).astype(BF16), places(ids[2:3], RPAD), ((1,), (1,)))
    for half in range(2):
        rel_grad[half] = whole[half * HALF : half * HALF + HALF]


def between_kernel(slab, table, ids, pos_rows, neg_rows, rel_rows):
    pos_rows[...], neg_rows[...] = target_rows_of(slab[...].astype(BF16), ids)
    rel_rows[...] = relation_rows_of(table[...], ids)


def rel_half(half, ids, d_rel, rel_grad):
    return rel_grad[half] + dot(d_rel[half], places(ids[2:3], RPAD), ((1,), (1,)))


def second_kernel(
    core, left, ids, pos_rows, neg_rows, rel_rows, rel_grad, prod, g_neg, g_pos, d_rel, other, grads
):
    heads = dot(left[...], places(ids[0:1], ROWS))
    prod[...], g_neg[...], g_pos[...], parts = edge_terms(
        heads, pos_rows[...], neg_rows[...], rel_rows[...]
    )
    for half in range(2):
        d_rel[half] = parts[half].astype(BF16)
    grads[...] = rel_half(1 - core[0], ids, d_rel, rel_grad)
    firsts, seconds = last_relations(grads)
    for part in range(OWNERS):
        other[part] = encode(block_of(grads, part), *picked(firsts, seconds, part))


def own_half_kernel(core, ids, rel_grad, d_rel, prod, g_neg, g_pos, mine, d_pos, d_neg):
    mine[...] = rel_half(core[0], ids, d_rel, rel_grad)
    d_pos[...], d_neg[...] = row_terms(prod[...], g_neg[...], g_pos[...])


def target_kernel(after, slab, state, ids, d_pos, d_neg, slab_out, state_out):
    slab_out[...], state_out[...] = trained(
        slab[...], state[...], ids[...], d_pos[...], d_neg[...]
    )


def power_of(top):
    return jnp.ceil(jnp.log2(jnp.maximum(top, 1e-30)))


def iota(shape, axis):
    return lax.broadcasted_iota(jnp.int32, shape, axis)


def encode(main, first, second):
    row = iota(main.shape, 0)
    main = jnp.where(row < CUT, main, 0.0)
    power = power_of(jnp.max(jnp.abs(main), axis=0, keepdims=True))
    top = jnp.maximum(jnp.abs(first), jnp.abs(second))
    last_power = power_of(jnp.max(top, axis=1, keepdims=True))
    scale = LEVELS * jnp.exp2(-last_power)
    second = jnp.where(iota(second.shape, 1) == 127, last_power, jnp.round(second * scale))
    codes = jnp.round(main * (LEVELS * jnp.exp2(-power)))
    codes = jnp.where(row == CUT, jnp.round(first * scale), codes)
    codes = jnp.where(row == CUT + 1, second, codes)
    codes = jnp.where(row == CUT + 2, power, codes)
    return codes.astype(jnp.int32).astype(jnp.int16)


def decode(codes):
    wide = codes.astype(jnp.int32).astype(F32)
    first, second, power = (wide[CUT + i : CUT + i + 1] for i in range(3))
    step = jnp.exp2(second[:, 127:]) * (1.0 / LEVELS)
    second = jnp.where(iota(second.shape, 1) < HALF - 128, second * step, 0.0)
    main = jnp.where(iota(wide.shape, 0) < CUT, wide, 0.0)
    return main * (jnp.exp2(power) * (1.0 / LEVELS)), first * step, second


def block_of(grads, part):
    tile, low = divmod(part, 2)
    lanes = slice(128 * tile, 128 * tile + 128)
    return pltpu.roll(grads[HALF - PART :, lanes], CUT, 0) if low else grads[:PART, lanes]


def last_relations(grads):
    gap = jnp.zeros((256 - HALF, 128), F32)
    rows = jnp.transpose(jnp.concatenate([grads[:, RMAIN:], gap], 0))
    return rows[:, :128], rows[:, 128:]


def picked(firsts, seconds, part):
    if part >= EXTRA:
        return jnp.zeros((1, 128), F32), jnp.zeros((1, 128), F32)
    return firsts[part : part + 1], seconds[part : part + 1]


def send_kernel(mine, theirs, codes):
    firsts, seconds = last_relations(mine)
    for part in range(OWNERS):
        main, first, second = decode(theirs[part])
        own_first, own_second = picked(firsts, seconds, part)
        codes[part] = encode(block_of(mine, part) + main, own_first + first, own_second + second)


def summed(parts):
    total = decode(parts[0])
    for part in range(1, parts.shape[0]):
        total = tuple(old + new for old, new in zip(total, decode(parts[part])))
    return total


def gather_kernel(parts, code):
    code[...] = encode(*summed(parts))


def spread_kernel(a, b, c, d, copies):
    rows = zip(*(decode(part[...]) for part in (a, b, c, d)))
    code = encode(*((w + y) + (x + z) for w, x, y, z in rows))
    for copy in range(OWNERS):
        copies[copy] = code


def decode_tile(codes, tile, grads, last):
    lanes = slice(128 * tile, 128 * tile + 128)
    blocks = []
    for part in (2 * tile, 2 * tile + 1):
        block, first, second = decode(codes[part])
        blocks.append(block)
        if part < EXTRA:
            last[part : part + 1, :128] = first
            last[part : part + 1, 128:] = second
    upper, lower = blocks[0], pltpu.roll(blocks[1], PART - CUT, 0)
    grads[: HALF - PART, lanes] = upper[: HALF - PART]
    grads[HALF - PART : PART, lanes] = upper[HALF - PART :] + lower[: 2 * PART - HALF]
    grads[PART:, lanes] = lower[2 * PART - HALF :]


def squares_of(grads):
    return jnp.sum(grads * grads, 0, keepdims=True)


def ours_kernel(codes, grads, squares, last):
    last[...] = jnp.zeros(last.shape, F32)
    for tile in range(OWNERS // 2):
        decode_tile(codes, tile, grads, last)
    grads[:, RMAIN:] = jnp.transpose(last[...])[:HALF]
    squares[...] = squares_of(grads[...])


GROUPS = ((0, 512), (512, 1024), (1024, 1536), (1536, RPAD))


def update_kernel(
    core,
    ours,
    squares,
    codes,
    relation,
    state,
    slab,
    relation_out,
    slab_out,
    state_out,
    theirs,
    last,
    wide,
    sems,
):
    copies = [pltpu.make_async_copy(slab, slab_out, sems.at[len(GROUPS)])]
    copies[0].start()
    last[...] = jnp.zeros(last.shape, F32)
    old_state = state[...].reshape(1, NREL)
    halves = [pl.ds(pl.multiple_of(half * HALF, 8), HALF) for half in (core[0], 1 - core[0])]
    states = []
    for place, (start, stop) in enumerate(GROUPS):
        for tile in range(start // 128, min(stop, RMAIN) // 128):
            decode_tile(codes, tile, theirs, last)
        if stop == RPAD:
            theirs[:, RMAIN:] = jnp.transpose(last[...])[:HALF]
        total = squares[:, start:stop] + squares_of(theirs[:, start:stop])
        end = min(stop, NREL)
        lanes = slice(start, end)
        states.append(old_state[:, lanes] + total[:, : end - start] * (1.0 / D))
        rate = 0.2 * lax.rsqrt(states[-1])
        for rows, grad in zip(halves, (ours, theirs)):
            wide[rows, lanes] = relation[rows, lanes] - grad[:, lanes] * rate
        copies.append(
            pltpu.make_async_copy(wide.at[:, lanes], relation_out.at[:, lanes], sems.at[place])
        )
        copies[-1].start()
    state_out[...] = jnp.concatenate(states, 1).reshape(NREL)
    for copy in copies:
        copy.wait()


def per_device(
    left_embed,
    right_embed,
    right_state,
    relation_embed,
    relation_state,
    source_rows,
    target_rows,
    relation_ids,
    negative_rows,
):
    core = lax.axis_index("core").astype(jnp.int32)[None]
    id_array = kept((8, EPAD), jnp.int32)
    index_arrays = [
        array[0, 0] for array in (source_rows, target_rows, relation_ids, negative_rows)
    ]
    dma = pltpu.SemaphoreType.DMA
    ids, ids_next, left_low = call(
        prepare_kernel,
        (id_array, id_array, kept((D, ROWS), BF16)),
        left_embed[0].T,
        *index_arrays,
        far_in=range(5),
        scratch=[
            pltpu.VMEM((D, ROWS), F32),
            [pltpu.VMEM(array.shape, jnp.int32) for array in index_arrays],
            dma((5,)),
        ],
        name="prepare",
    )
    ids_next = from_next(ids_next)
    left_next = from_next(left_low)
    relation = relation_embed.T
    slab_array, state_array = (D, ROWS), (1, ROWS)
    edge_array = kept((D, EPAD), BF16)
    half_array = kept((HALF, RPAD), F32)
    slab, state, rel_grad, table = call(
        first_kernel,
        (
            kept(slab_array, F32),
            kept(state_array, F32),
            kept((2, HALF, RPAD), F32),
            kept((D, RPAD), BF16),
        ),
        left_low,
        ids,
        right_embed[0].T,
        right_state,
        relation,
        far_in=(2, 3, 4),
        scratch=[
            pltpu.VMEM(slab_array, F32),
            pltpu.VMEM(state_array, F32),
            pltpu.VMEM((D, NREL), F32),
            dma((6,)),
        ],

        name="first",
    )
    wide_array = kept((D, EPAD), F32)
    part = (PART, 128)
    last = pltpu.VMEM((128, 256), F32)
    parts = kept((OWNERS, *part), jnp.int16)
    pos_rows, neg_rows, rel_rows = call(
        between_kernel,
        (wide_array, kept((D, NPAD), BF16), wide_array),
        slab,
        table,
        ids_next,
        flops=2 * 10**10,
        name="between",
    )
    prod, g_neg, g_pos, d_rel, other = call(
        second_kernel,
        (
            edge_array,
            kept((NPAD, EPAD), BF16),
            kept((1, EPAD), F32),
            kept((2, HALF, EPAD), BF16),
            parts,
        ),
        left_next,
        ids_next,
        pos_rows,
        neg_rows,
        rel_rows,
        rel_grad,
        core=core,
        scratch=[pltpu.VMEM((HALF, RPAD), F32)],
        name="second",
    )
    theirs = swap_core(other)
    mine, d_pos, d_neg = call(
        own_half_kernel,
        (half_array, edge_array, kept((D, NPAD), BF16)),
        ids_next,
        rel_grad,
        d_rel,
        prod,
        g_neg,
        g_pos,
        core=core,
        name="own_half",
    )
    sent = call(send_kernel, parts, mine, theirs, name="send")
    got = lax.all_to_all(sent, CUBE, 0, 0, tiled=True)
    count = lax.axis_size("z_hi")
    codes = call(gather_kernel, kept(part, jnp.int16), got, name="gather")
    ring = [
        lax.ppermute(codes, "z_hi", [((i + k) % count, i) for i in range(count)])
        for k in range(1, count)
    ]
    copies = call(spread_kernel, parts, codes, *ring, name="spread")
    ours = lax.all_to_all(copies, CUBE, 0, 0, tiled=True)
    theirs = swap_core(ours)
    grads, squares = call(
        ours_kernel, (half_array, kept((1, RPAD), F32)), ours, scratch=[last], name="ours"
    )
    slab, state_out = call(
        target_kernel,
        (kept(slab_array, F32), struct(state_array, F32)),
        squares,
        slab,
        state,
        ids_next,
        d_pos,
        d_neg,
        name="target",
    )
    relation_out, slab_out, relation_state_out = call(
        update_kernel,
        (struct((D, NREL), F32), struct(slab_array, F32), struct((NREL,), F32)),
        grads,
        squares,
        theirs,
        relation,
        relation_state,
        slab,
        core=core,
        far_out=(0, 1),
        scratch=[
            pltpu.VMEM((HALF, RPAD), F32),
            last,
            pltpu.VMEM((D, NREL), F32),
            dma((len(GROUPS) + 1,)),
        ],
        name="update",
    )
    return (slab_out.T[None], state_out, relation_out.T, relation_state_out)


def solution(mesh):
    split = jax.sharding.Mesh(mesh.devices.reshape(4, 4, 2, 2, 2, 2), AXES)
    in_specs = (
        P(REPLICA, BUCKET, None),
        P(REPLICA, BUCKET, None),
        P(REPLICA, BUCKET),
        P(),
        P(),
        P(REPLICA, BUCKET, None, None),
        P(REPLICA, BUCKET, None, None),
        P(REPLICA, BUCKET, None, None),
        P(REPLICA, BUCKET, None, None),
    )
    out_specs = (P(REPLICA, BUCKET, None), P(REPLICA, BUCKET), P(), P())
    return jax.shard_map(
        per_device, mesh=split, in_specs=in_specs, out_specs=out_specs, check_vma=False
    )
```
